32 devices in a mesh: lat: 4 (over x, core), lon: 8 (over z, y).
Axes of the slice: x: 2, y: 2, z: 4, core: 2. Of those that a mesh axis runs over, the one named last changes fastest.
Arguments:
- spectra: bfloat16 [16384, 616], P(('lat', 'lon')), may hold values from -6 to 6
- owner: int32 [16384, 1], P(('lat', 'lon')), may hold values from 0 to 31; in each aligned block of 512 rows (0 to 511, 512 to 1023, ...) at most 32 rows name the same one
- cell: int32 [16384], P(('lat', 'lon')), may hold values from 0 to 2047
- w_in: bfloat16 [616, 512], replicated, may hold values from -0.25 to 0.25
- w_out: bfloat16 [512, 512], replicated, may hold values from -0.25 to 0.25
- w_point: bfloat16 [512, 512], replicated, may hold values from -0.25 to 0.25
- w_depth: float32 [9, 512], replicated, may hold values from -2 to 2
- cotangent: bfloat16 [64, 1024, 512], P('lat', 'lon'), may hold values from -6 to 6
Outputs:
- latent: bfloat16 [64, 1024, 512], P('lat', 'lon')
- grad_in: float32 [616, 512], replicated
- grad_out: float32 [512, 512], replicated
- grad_point: float32 [512, 512], replicated
- grad_depth: float32 [9, 512], replicated
The draws below stay inside these ranges and needn't reach their ends.
Inputs may be any that keep to these rules, and one draw needn't show every extreme that they name: `owner`: among the 512 rows of one device at most 32 name the same tile, a bound that some block reaches.
All inputs are finite; a program needn't handle non-finite values.
Results may differ from the reference program's by a relative error of at most 0.007.
Values may be sent and summed in bfloat16 or wider, within the bound.
No kernel may reach another device: no remote copies, remote signals or barrier semaphores. Data moves between devices by JAX's collectives and lax.ppermute only.
A program may use at most 64 MiB of HBM per device.

```python
import math
import jax
import jax.numpy as jnp
import numpy as np
from jax import lax

SPEC = 616
HID = 512
C = 512
OBS_DEV = 512
CAP = 32
CLAT = 16
CLON = 128
TILES = 32
CELLS = 2048
OBS = 16384
LAT = 64
LON = 1024
N_LON = 8


def touch_ends(array, own_key, low, top_value):
    longest = array.shape.index(max(array.shape))
    spots = []
    for shift in (0, 1):
        where = [jax.random.randint(jax.random.fold_in(own_key, axis), (), 0, length) for axis, length in enumerate(array.shape)]
        where[longest] = (where[longest] + shift) % array.shape[longest]
        spots.append(tuple(where))
    return array.at[spots[0]].set(low).at[spots[1]].set(top_value)


def levels(key, dims, split, least, top_value):
    loudness, own = 1.0, jax.random.fold_in(key, 6)
    for position, shards_of in split:
        draws = jnp.exp(jax.random.uniform(jax.random.fold_in(own, position), (shards_of,), jnp.float32, least / len(split), top_value / len(split)))
        loudness = loudness * jnp.repeat(draws, dims[position] // shards_of).reshape([-1 if axis == position else 1 for axis in range(len(dims))])
    return loudness


def routed_block(stream_key, own, number, rows, number_of, top, reach, lean):
    order = jax.random.permutation(stream_key, number_of)
    heavy_load, common = load_shares(number_of, rows * top, reach, lean, True), load_shares(number_of, rows * top, reach, lean, False)
    places = jnp.arange(number_of)

    def named(sizes, rotation):
        used = int((sizes > 0).sum())
        fixed = max(1, used // 4)
        shifted = fixed + (places - fixed + rotation * (used - fixed)) % max(1, number_of - fixed)
        return jnp.zeros((number_of,), jnp.int32).at[order[jnp.where(places < fixed, places, shifted)]].set(jnp.asarray(sizes, jnp.int32))

    sizes = jnp.where(number % 4 == 0, named(heavy_load, number // 4), named(common, number - number // 4 - 1))
    mixed = jax.random.permutation(jax.random.fold_in(own, 3), number_of)
    giver, sink = mixed[0:number_of // 2 * 2:2], mixed[1:number_of // 2 * 2:2]
    slack = jnp.minimum(sizes[giver] - 1, reach - sizes[sink]) // 2
    slack = jnp.where((giver == order[0]) | (sink == order[0]) | (sizes[sink] == 0), 0, jnp.maximum(slack, 0))
    shifted = jax.random.randint(jax.random.fold_in(own, 4), (number_of // 2,), 0, 1 << 20) % (slack + 1)
    sizes = sizes.at[giver].add(-shifted).at[sink].add(shifted)
    labels = jnp.searchsorted(jnp.cumsum(sizes), jnp.arange(rows * top), side="right").astype(jnp.int32)
    table = labels.reshape(top, rows).T
    table = table[jax.random.permutation(jax.random.fold_in(own, 1), rows)]
    rotation = jax.random.randint(jax.random.fold_in(own, 2), (rows, 1), 0, top)
    return jnp.take_along_axis(table, (jnp.arange(top)[None, :] + rotation) % top, axis=1)


def load_shares(number_of, total, most, slope, full):
    weights = [(1 << 20) // math.isqrt(rank ** slope) + 1 for rank in range(1, number_of + 1)]
    largest = most if full else min(most, max(-(-total // number_of), total * weights[0] // sum(weights)))
    least = 1 if total - largest >= number_of - 1 else 0
    given, spare = [largest] + [least] * (number_of - 1), total - largest - least * (number_of - 1)
    while spare > 0:
        movable = [i for i in range(1, number_of) if given[i] < largest] or [i for i in range(1, number_of) if given[i] < most]
        pool, budget = sum([weights[i] for i in movable]), spare
        for i in movable:
            more = min(most - given[i], max(1, budget * weights[i] // pool), spare)
            given[i] = given[i] + more
            spare = spare - more
    return np.array(given)


def scatter_about(own_key, extent, deviation, most, split=(), kind=jnp.bfloat16):
    values = deviation * jax.random.normal(own_key, extent, jnp.float32)
    if split:
        values = values * levels(own_key, extent, split, -0.22, 0.18)
    return jnp.clip(values, -most, most).astype(kind)


def setup_inputs(seed: int = 0) -> dict:
    keys = jax.random.split(jax.random.key(seed), 9)
    spectra = scatter_about(keys[0], (OBS, SPEC), 1.0, 6.0, ((0, 32),))
    owner_keys = jax.random.split(jax.random.fold_in(keys[1], 1), OBS // OBS_DEV)
    owner_turns = jax.random.permutation(jax.random.fold_in(keys[1], 3), OBS // OBS_DEV)
    owner = jax.vmap(lambda own, number: routed_block(jax.random.fold_in(keys[1], 2), own, number, OBS_DEV, TILES, 1, CAP, 2))(owner_keys, owner_turns).reshape((OBS, 1))
    cell = touch_ends(jax.random.randint(keys[2], (OBS,), 0, CELLS), jax.random.fold_in(keys[2], 1), 0, CELLS - 1).astype(jnp.int32)
    w_in = scatter_about(keys[3], (SPEC, HID), SPEC ** -0.5, 0.25)
    w_out = scatter_about(keys[4], (HID, C), HID ** -0.5, 0.25)
    w_point = scatter_about(keys[5], (C, C), C ** -0.5, 0.25)
    w_depth = scatter_about(keys[6], (9, C), 9 ** -0.5, 2.0, (), jnp.float32)
    cotangent = scatter_about(keys[7], (LAT, LON, C), 1.0, 6.0, ((0, 4), (1, 8)))
    return dict(spectra=spectra, owner=owner, cell=cell, w_in=w_in, w_out=w_out, w_point=w_point, w_depth=w_depth, cotangent=cotangent)


offsets = [(a, b) for a in (-1, 0, 1) for b in (-1, 0, 1)]

def extend(field):
    wide = field.astype(jnp.float32)
    wide = jnp.concatenate([wide[:, -1:], wide, wide[:, :1]], axis=1)
    return jnp.pad(wide, ((1, 1), (0, 0), (0, 0)))

def reference(spectra, owner, cell, w_in, w_out, w_point, w_depth, cotangent):
    tile = owner[:, 0].astype(jnp.int32)
    grid_row = tile // N_LON * CLAT + cell // CLON
    grid_col = tile % N_LON * CLON + cell % CLON
    place = (grid_row * LON + grid_col).astype(jnp.int32)
    preact = jnp.dot(spectra, w_in, preferred_element_type=jnp.float32)
    hidden = jax.nn.silu(preact).astype(jnp.bfloat16)
    embedded = jnp.dot(hidden, w_out, preferred_element_type=jnp.float32).astype(jnp.bfloat16)
    grid = jax.ops.segment_sum(embedded.astype(jnp.float32), place, num_segments=LAT * LON)
    grid = grid.astype(jnp.bfloat16).reshape(LAT, LON, C)
    padded = extend(grid)
    mixed = jnp.zeros((LAT, LON, C), jnp.float32)
    for k, (a, b) in enumerate(offsets):
        mixed = mixed + w_depth[k] * padded[1 + a:1 + a + LAT, 1 + b:1 + b + LON]
    mixed = mixed.astype(jnp.bfloat16)
    mixed_rows = mixed.reshape(-1, C)
    latent = grid.astype(jnp.float32) + jnp.dot(mixed_rows, w_point, preferred_element_type=jnp.float32).reshape(LAT, LON, C)
    latent = latent.astype(jnp.bfloat16)
    cot_rows = cotangent.reshape(-1, C)
    grad_point = jnp.dot(mixed_rows.T, cot_rows, preferred_element_type=jnp.float32)
    g_mixed = jnp.dot(cot_rows, w_point.T, preferred_element_type=jnp.float32).astype(jnp.bfloat16).reshape(LAT, LON, C)
    g_mixed_f = g_mixed.astype(jnp.float32)
    grad_depth = jnp.stack([lax.optimization_barrier(jnp.sum(g_mixed_f * padded[1 + a:1 + a + LAT, 1 + b:1 + b + LON], axis=(0, 1))) for a, b in offsets])
    padded_g = extend(g_mixed)
    g_grid = cotangent.astype(jnp.float32)
    for k, (a, b) in enumerate(offsets):
        g_grid = g_grid + w_depth[k] * padded_g[1 - a:1 - a + LAT, 1 - b:1 - b + LON]
    g_grid = g_grid.astype(jnp.bfloat16).reshape(-1, C)
    g_embedded = g_grid[place]
    grad_out = jnp.dot(hidden.T, g_embedded, preferred_element_type=jnp.float32)
    g_hidden = jnp.dot(g_embedded, w_out.T, preferred_element_type=jnp.float32)
    sigmoid_pre = jax.nn.sigmoid(preact)
    g_preact = (g_hidden * sigmoid_pre * (1.0 + preact * (1.0 - sigmoid_pre))).astype(jnp.bfloat16)
    grad_in = jnp.dot(spectra.T, g_preact, preferred_element_type=jnp.float32)
    obs_scale = 1.0 / jnp.sqrt(jnp.float32(OBS))
    cell_scale = 1.0 / jnp.sqrt(jnp.float32(LAT * LON))
    return (latent, grad_in * obs_scale, grad_out * obs_scale, grad_point * cell_scale, grad_depth * cell_scale)
```

```python
import functools

import jax
import jax.numpy as jnp
from jax import lax
from jax.experimental import pallas as pl
from jax.experimental.pallas import tpu as pltpu
from jax.sharding import Mesh
from jax.sharding import PartitionSpec as P

LANES = 128
bf16 = jnp.bfloat16
f32 = jnp.float32
i32 = jnp.int32


def params(mib):
    return pltpu.CompilerParams(vmem_limit_bytes=mib * 1024 * 1024)


def round_up(n, m):
    return -(-n // m) * m


def dot(a, b, dims=(1, 0)):
    return lax.dot_general(
        a, b, (((dims[0],), (dims[1],)), ((), ())), preferred_element_type=f32
    )


def cost(us):
    return pl.CostEstimate(flops=us * 1153500000, bytes_accessed=0, transcendentals=0)


def smem():
    return pl.BlockSpec(memory_space=pltpu.SMEM)


def anywhere():
    return pl.BlockSpec(memory_space=pl.ANY)


def vmem():
    return pl.BlockSpec(memory_space=pltpu.VMEM)


def route_kernel(tiles, cap, clon, places_ref, rows_ref, out_ref):
    spec, n = rows_ref.shape
    head = out_ref.shape[1] - LANES
    owner = places_ref[0:1, :]
    hits = owner == lax.broadcasted_iota(i32, (tiles, n), 0)
    above = lax.broadcasted_iota(i32, (n, n), 0) < lax.broadcasted_iota(i32, (n, n), 1)
    count = dot(hits.astype(f32).astype(bf16), above.astype(f32).astype(bf16))
    rank = jnp.sum(jnp.where(hits, count, 0.0), axis=0, keepdims=True)
    slot = owner * cap + rank.astype(i32)
    cell = places_ref[1:2, :]
    line = lax.broadcasted_iota(i32, (LANES - (spec - head), n), 0)
    high = cell // clon
    spots = jnp.where(line == 0, high, jnp.where(line == 1, cell - high * clon, 0)).astype(f32)
    last = jnp.concatenate([rows_ref[head:, :].astype(f32), spots], axis=0).astype(bf16)
    first = rows_ref[:head, :]
    step = min(256, tiles * cap)

    def body(t, carry):
        base = t * step
        place = lax.broadcasted_iota(i32, (step, n), 0) + base
        pick = (slot == place).astype(f32).astype(bf16)
        at = pl.ds(pl.multiple_of(base, step), step)
        out_ref[at, :head] = dot(pick, first, (1, 1)).astype(bf16)
        out_ref[at, head:] = dot(pick, last, (1, 1)).astype(bf16)
        return carry

    lax.fori_loop(0, tiles * cap // step, body, 0)


def route(places, rows, tiles, cap, clon, spec_wide):
    return pl.pallas_call(
        functools.partial(route_kernel, tiles, cap, clon),
        out_shape=jax.ShapeDtypeStruct((tiles * cap, spec_wide), bf16),
        in_specs=[vmem()] * 2,
        out_specs=vmem(),
        compiler_params=params(12),
        cost_estimate=cost(3),
        name="route",
    )(places, rows)


def grid_grad_kernel(
    clat, clon, wide, cot_ref, east_ref, west_ref, north_ref, south_ref, wp_ref, wd_ref,
    cot_ext, gm_ref, gg_ref, east, west,
):
    width = wp_ref.shape[0]
    w_point = wp_ref[...]
    east[...] = east_ref[...].astype(f32)
    west[...] = west_ref[...].astype(f32)
    line = lax.broadcasted_iota(i32, (wide - clon, width), 0)

    def matmul(i, carry):
        at = pl.multiple_of((i + 1) * wide, 16)
        cot_ext[pl.ds(at, clon), :] = cot_ref[pl.ds(pl.multiple_of(i * clon, 16), clon), :]
        tail = jnp.where(
            line == 0, east[pl.ds(i, 1), :], jnp.where(line == wide - clon - 1, west[pl.ds(i, 1), :], 0.0)
        )
        cot_ext[pl.ds(at + clon, wide - clon), :] = tail.astype(bf16)
        at = pl.ds(at, wide)
        gm_ref[at, :] = dot(cot_ext[at, :], w_point, (1, 1)).astype(bf16)
        return carry

    for ref, at in ((north_ref, 0), (south_ref, (clat + 1) * wide)):
        cot_ext[at : at + wide, :] = ref[...]
        gm_ref[at : at + wide, :] = dot(ref[...], w_point, (1, 1)).astype(bf16)
    lax.fori_loop(0, clat, matmul, 0)

    def conv(i, carry):
        out_at = pl.ds(pl.multiple_of(i * clon, 16), clon)
        mid = pl.ds(pl.multiple_of((i + 1) * wide, 16), wide)
        for lane in range(0, width, LANES):
            cols = slice(lane, lane + LANES)
            sums = []
            for b in range(3):
                total = None
                for a in range(3):
                    at = pl.ds(pl.multiple_of((i + 2 - a) * wide, 16), wide)
                    term = wd_ref[3 * a + b : 3 * a + b + 1, cols] * gm_ref[at, cols].astype(f32)
                    total = term if total is None else total + term
                sums.append(total)
            out = cot_ext[mid, cols].astype(f32) + sums[1]
            out = out + pltpu.roll(sums[2], 1, 0) + pltpu.roll(sums[0], wide - 1, 0)
            gg_ref[out_at, cols] = out[:clon].astype(bf16)
        return carry

    lax.fori_loop(0, clat, conv, 0)


def grid_grad(cot, sides, w_point, w_depth, clat, clon, wide):
    width = w_point.shape[0]
    ext = jax.ShapeDtypeStruct(((clat + 2) * wide, width), bf16)
    return pl.pallas_call(
        functools.partial(grid_grad_kernel, clat, clon, wide),
        out_shape=(ext, ext, jax.ShapeDtypeStruct((clat * clon, width), bf16)),
        in_specs=[vmem()] * 7,
        out_specs=(vmem(),) * 3,
        scratch_shapes=[pltpu.VMEM((clat, width), f32)] * 2,
        compiler_params=params(8),
        cost_estimate=cost(10),
        name="grid_grad",
    )(cot, *sides, w_point, w_depth)


def write_halves(core, total, start, mine_ref, other_ref, first=0, size=None):
    size = total.shape[0] if size is None else size
    half = total.shape[1] // 2
    for ref, base in ((mine_ref, core * half), (other_ref, (1 - core) * half)):
        for n in range(half // LANES):
            cols = pl.ds(pl.multiple_of(base + n * LANES, LANES), LANES)
            ref[n, start : start + size, :] = total[first : first + size, cols].astype(bf16)


def clear_tail(start, *refs):
    for ref in refs:
        unused = ref.shape[1] - start
        if unused:
            ref[:, start:, :] = jnp.zeros((ref.shape[0], unused, LANES), bf16)


def owner_kernel(
    spec, clat, clon, wide, core_ref, rows_hbm, wi_hbm, wo_hbm, gg_hbm, cot_hbm, gm_hbm, wd_hbm,
    grid_hbm, mix_hbm, east_hbm, west_hbm, mine_hbm, other_hbm,
    rows_ref, wi_ref, wo_ref, gg_ref, cot_ref, gm_ref, wd_ref,
    padded, mix_ref, east_ref, west_ref, mine_ref, other_ref,
    emb_ref, gi, go, gp, gd, sems,
):
    core = core_ref[0]
    slots, spec_wide = rows_ref.shape
    cells, width = gg_ref.shape
    sources = rows_hbm, wi_hbm, wo_hbm, gg_hbm, wd_hbm, cot_hbm, gm_hbm
    targets = rows_ref, wi_ref, wo_ref, gg_ref, wd_ref, cot_ref, gm_ref
    loads = [
        pltpu.make_async_copy(source, target, sems.at[i])
        for i, (source, target) in enumerate(zip(sources, targets))
    ]
    for load in loads:
        load.start()
    gi[...] = jnp.zeros_like(gi)
    go[...] = jnp.zeros_like(go)
    gd[...] = jnp.zeros_like(gd)
    gp[...] = jnp.zeros_like(gp)
    padded[pl.ds(0, 2 * clon), :] = jnp.zeros((2 * clon, width), bf16)
    padded[pl.ds((clat + 2) * clon, 2 * clon), :] = jnp.zeros((2 * clon, width), bf16)
    for load in loads[:4]:
        load.wait()

    step = min(256, slots)

    def encode(t, carry):
        at = pl.ds(pl.multiple_of(t * step, step), step)
        rows = rows_ref[at, :]
        preact = dot(rows, wi_ref[...])
        sig = 1.0 / (1.0 + jnp.exp(-preact))
        hidden = (preact * sig).astype(bf16)
        emb_ref[at, :] = dot(hidden, wo_ref[...]).astype(bf16)
        place = rows[:, spec : spec + 1].astype(f32) * clon + rows[:, spec + 1 : spec + 2].astype(f32)
        hits = place.astype(i32) == lax.broadcasted_iota(i32, (step, cells), 1)
        g_emb = dot(hits.astype(f32).astype(bf16), gg_ref[...]).astype(bf16)
        go[...] += dot(hidden, g_emb, (0, 0))
        g_hid = dot(g_emb, wo_ref[...], (1, 1))
        g_pre = (g_hid * (sig * (1.0 + preact * (1.0 - sig)))).astype(bf16)
        gi[...] += dot(rows, g_pre, (0, 0))
        return carry

    lax.fori_loop(0, slots // step, encode, 0)

    last = rows_ref[:, spec_wide - LANES :]
    col = spec - (spec_wide - LANES)
    lane = lax.broadcasted_iota(i32, (16, LANES), 1)
    pick = jnp.where(lane == col, float(clon), jnp.where(lane == col + 1, 1.0, 0.0)).astype(bf16)
    place = dot(pick, last, (1, 1))[0:1, :].astype(i32)
    block = 2 * clon

    def bins(t, carry):
        cell = lax.broadcasted_iota(i32, (block, slots), 0) + t * block
        hits = (place == cell).astype(f32).astype(bf16)
        grid = dot(hits, emb_ref[...]).astype(bf16)
        padded[pl.ds(pl.multiple_of((t + 1) * block, 16), block), :] = grid
        return carry

    lax.fori_loop(0, clat // 2, bins, 0)
    put_grid = pltpu.make_async_copy(padded.at[pl.ds(2 * clon, cells)], grid_hbm, sems.at[7])
    put_grid.start()
    for load in loads[4:]:
        load.wait()

    fill = jnp.zeros((wide - clon, LANES), f32)

    def conv(e, carry):
        out_at = pl.ds(pl.multiple_of(e * wide, 16), wide)
        for lane in range(0, width, LANES):
            cols = slice(lane, lane + LANES)
            near = [
                padded[pl.ds(pl.multiple_of((e + a) * clon, 16), clon), cols].astype(f32)
                for a in range(3)
            ]
            sums = []
            for b in range(3):
                total = None
                for a in range(3):
                    term = wd_ref[3 * a + b : 3 * a + b + 1, cols] * near[a]
                    total = term if total is None else total + term
                sums.append(jnp.concatenate([total, fill], axis=0))
            mixed = sums[1] + pltpu.roll(sums[2], wide - 1, 0) + pltpu.roll(sums[0], 1, 0)
            mix_ref[out_at, cols] = mixed.astype(bf16)
            east_ref[e, :, cols] = mixed[clon : clon + 8]
            west_ref[e, :, cols] = mixed[wide - 8 : wide]
            g_mid = gm_ref[out_at, cols].astype(f32)
            for b, g in ((0, pltpu.roll(g_mid, wide - 1, 0)), (1, g_mid), (2, pltpu.roll(g_mid, 1, 0))):
                g = g[:clon]
                for a in range(3):
                    part = jnp.sum((g * near[a]).reshape(clon // 8, 8, LANES), axis=0)
                    gd[8 * (3 * a + b) : 8 * (3 * a + b) + 8, cols] += part
        return carry

    lax.fori_loop(0, clat + 2, conv, 0)
    puts = [
        pltpu.make_async_copy(mix_ref, mix_hbm, sems.at[8]),
        pltpu.make_async_copy(east_ref, east_hbm, sems.at[9]),
        pltpu.make_async_copy(west_ref, west_hbm, sems.at[10]),
    ]
    for put in puts:
        put.start()

    def point(t, carry):
        at = pl.ds(pl.multiple_of(t * 3 * wide, 16), 3 * wide)
        gp[...] += dot(mix_ref[at, :], cot_ref[at, :], (0, 0))
        return carry

    lax.fori_loop(0, (clat + 2) // 3, point, 0)
    taps = [jnp.sum(gd[8 * k : 8 * k + 8, :], axis=0, keepdims=True) for k in range(9)]
    gd[0:16, :] = jnp.concatenate(taps + [jnp.zeros((7, width), f32)], axis=0)
    start = 0
    for total, size in ((go, width), (gi, round_up(spec, 16)), (gp, width), (gd, 16)):
        write_halves(core, total, start, mine_ref, other_ref, 0, size)
        start += size
    clear_tail(start, mine_ref, other_ref)
    puts += [put_grid] + [
        pltpu.make_async_copy(mine_ref, mine_hbm, sems.at[11]),
        pltpu.make_async_copy(other_ref, other_hbm, sems.at[12]),
    ]
    for put in puts[-2:]:
        put.start()
    for put in puts:
        put.wait()


def owner_part(core, rows, w_in, w_out, g_grid, cot_ext, gm_ext, w_depth, spec, clat, clon, wide, out_rows):
    slots, spec_wide = rows.shape
    width = w_out.shape[0]
    half = jax.ShapeDtypeStruct((width // LANES // 2, out_rows, LANES), bf16)
    column = jax.ShapeDtypeStruct((clat + 2, 8, width), f32)
    operands = rows, w_in, w_out, g_grid, cot_ext, gm_ext, w_depth
    padded = pltpu.VMEM(((clat + 4) * clon, width), bf16)
    outs = jax.ShapeDtypeStruct(cot_ext.shape, bf16), column, column, half, half
    return pl.pallas_call(
        functools.partial(owner_kernel, spec, clat, clon, wide),
        out_shape=(jax.ShapeDtypeStruct((clat * clon, width), bf16),) + outs,
        in_specs=[smem()] + [anywhere()] * 7,
        out_specs=(anywhere(),) * 6,
        scratch_shapes=[pltpu.VMEM(x.shape, x.dtype) for x in operands]
        + [padded]
        + [pltpu.VMEM(x.shape, x.dtype) for x in outs]
        + [
            pltpu.VMEM((slots, width), bf16),
            pltpu.VMEM((spec_wide, width), f32),
            pltpu.VMEM((width, width), f32),
            pltpu.VMEM((width, width), f32),
            pltpu.VMEM((72, width), f32),
            pltpu.SemaphoreType.DMA((13,)),
        ],
        compiler_params=params(56),
        cost_estimate=cost(22),
        name="owner",
    )(core, *operands)


def latent_kernel(
    clat, clon, wide, grid_ref, mix_ref, top_ref, bottom_ref, left_ref, right_ref, wp_ref, out_ref
):
    width = wp_ref.shape[0]
    w_point = wp_ref[...]
    line = lax.broadcasted_iota(i32, (clon, width), 0)

    def body(i, carry):
        at = pl.ds(pl.multiple_of(i * clon, 16), clon)
        mixed = mix_ref[pl.ds(pl.multiple_of((i + 1) * wide, 16), clon), :].astype(f32)
        mixed = mixed + (i == 0).astype(f32) * top_ref[:clon, :].astype(f32)
        mixed = mixed + (i == clat - 1).astype(f32) * bottom_ref[:clon, :].astype(f32)
        mixed = mixed + jnp.where(
            line == 0, left_ref[pl.ds(i, 1), :], jnp.where(line == clon - 1, right_ref[pl.ds(i, 1), :], 0.0)
        )
        out = grid_ref[at, :].astype(f32) + dot(mixed.astype(bf16), w_point)
        out_ref[at, :] = out.astype(bf16)
        return carry

    lax.fori_loop(0, clat, body, 0)


def finish_latent(grid, mix_ext, sides, w_point, clat, clon, wide):
    return pl.pallas_call(
        functools.partial(latent_kernel, clat, clon, wide),
        out_shape=jax.ShapeDtypeStruct(grid.shape, bf16),
        in_specs=[vmem()] * 7,
        out_specs=vmem(),
        compiler_params=params(6),
        cost_estimate=cost(5),
        name="latent",
    )(grid, mix_ext, *sides, w_point)


def totals_kernel(parts_ref, *refs):
    out_ref = refs[-1]
    total = jnp.sum(parts_ref[...].astype(f32), axis=0).astype(bf16)
    out_ref[...] = jnp.broadcast_to(total[None], parts_ref.shape)


def totals(parts, *after):
    return pl.pallas_call(
        totals_kernel,
        out_shape=jax.ShapeDtypeStruct(parts.shape, bf16),
        in_specs=[vmem()] + [anywhere()] * len(after),
        out_specs=vmem(),
        compiler_params=params(6),
        cost_estimate=cost(1),
        name="totals",
    )(parts, *after)


def unpack_kernel(
    obs_scale, cell_scale, core_ref, own_ref, sibling_ref, gi_ref, go_ref, gp_ref, gd_ref
):
    spec, width = gi_ref.shape
    chips = own_ref.shape[0]
    count = width // (2 * LANES)
    per = chips // count
    core = core_ref[0]
    for ref, half in ((own_ref, core), (sibling_ref, 1 - core)):
        for n in range(count):
            cols = pl.ds(pl.multiple_of((half * count + n) * LANES, LANES), LANES)
            block = ref[n * per : (n + 1) * per].astype(f32)
            block = block.reshape(per * block.shape[1], LANES)
            start = 0
            for out_ref, scale in (
                (go_ref, obs_scale), (gi_ref, obs_scale), (gp_ref, cell_scale), (gd_ref, cell_scale)
            ):
                size = out_ref.shape[0]
                out_ref[:, cols] = block[start : start + size] * scale
                start += round_up(size, 16)


def unpack(core, own, sibling, spec, width, obs_scale, cell_scale):
    return pl.pallas_call(
        functools.partial(unpack_kernel, obs_scale, cell_scale),
        out_shape=tuple(
            jax.ShapeDtypeStruct((rows, width), f32) for rows in (spec, width, width, 9)
        ),
        in_specs=[smem()] + [vmem()] * 2,
        out_specs=(vmem(),) * 4,
        compiler_params=params(8),
        cost_estimate=cost(3),
        name="unpack",
    )(core, own, sibling)


def neighbours(axes, periodic):
    count = lax.axis_size(axes)
    up = [(i, i + 1) for i in range(count - 1)]
    if periodic:
        up.append((count - 1, 0))
    return up, [(t, s) for s, t in up]


LAT = ("x", "core")
CHIPS = ("x", "lon")


SWAP = [(0, 1), (1, 0)]


def core_sum(mine, other):
    got = lax.ppermute(other, "core", SWAP)
    return (mine.astype(f32) + got.astype(f32)).astype(bf16)


def spread(values):
    chips = lax.axis_size(CHIPS)
    blocks, rows, _ = values.shape
    values = values.reshape(chips, blocks * rows // chips, LANES)
    return lax.all_to_all(values, CHIPS, split_axis=0, concat_axis=0, tiled=True)


def on_device(spectra, owner, cell, w_in, w_out, w_point, w_depth, cotangent):
    tiles = lax.axis_size(LAT) * lax.axis_size("lon")
    rows_here, spec = spectra.shape
    cap = max(2, 2 * rows_here // tiles)
    clat, clon, width = cotangent.shape
    cells = clat * clon
    wide = clon + 16
    spec_wide = round_up(spec + 2, LANES)
    core = lax.axis_index("core").reshape(1)
    east_way, west_way = neighbours("lon", True)
    south_way, north_way = neighbours(LAT, False)

    from_west = lax.ppermute(cotangent[:, -1], "lon", east_way)
    from_east = lax.ppermute(cotangent[:, 0], "lon", west_way)

    places = jnp.concatenate([owner.reshape(1, rows_here), cell.reshape(1, rows_here)], axis=0)
    outgoing = route(places, spectra.T, tiles, cap, clon, spec_wide)
    outgoing, from_west, from_east = lax.optimization_barrier((outgoing, from_west, from_east))
    arrived = lax.all_to_all(
        outgoing.reshape(tiles, cap, spec_wide), ("x", "core", "lon"), 0, 0, tiled=True
    ).reshape(tiles * cap, spec_wide)

    fill = jnp.zeros((wide - clon - 2, width), bf16)

    def edge_row(i):
        return jnp.concatenate([cotangent[i], from_east[i, None], fill, from_west[i, None]], axis=0)

    from_north = lax.ppermute(edge_row(clat - 1), LAT, south_way)
    from_south = lax.ppermute(edge_row(0), LAT, north_way)
    cot_ext, gm_ext, g_grid = grid_grad(
        cotangent.reshape(cells, width),
        (from_east, from_west, from_north, from_south),
        w_point, w_depth, clat, clon, wide,
    )
    w_in_wide = jnp.pad(w_in, ((0, spec_wide - spec), (0, 0)))

    out_rows = round_up(2 * width + round_up(spec, 16) + 16, 16 * tiles * LANES // width)
    grid, mix_ext, east, west, mine, other = owner_part(
        core, arrived, w_in_wide, w_out, g_grid, cot_ext, gm_ext, w_depth,
        spec, clat, clon, wide, out_rows,
    )
    summed = core_sum(mine, other)
    summed, grid, mix_ext, east, west = lax.optimization_barrier((summed, grid, mix_ext, east, west))
    parts = spread(summed)

    ext = mix_ext.reshape(clat + 2, wide, width)
    top = lax.ppermute(ext[clat + 1], LAT, south_way)
    bottom = lax.ppermute(ext[0], LAT, north_way)

    def edge_column(own, at):
        return own[1:-1].at[0].add(top[at].astype(f32)).at[-1].add(bottom[at].astype(f32))

    left = lax.ppermute(edge_column(east[:, 0], clon), "lon", east_way)
    right = lax.ppermute(edge_column(west[:, 7], wide - 1), "lon", west_way)
    sent = totals(parts, left, right)
    full = lax.all_to_all(sent, CHIPS, split_axis=0, concat_axis=0, tiled=True)
    latent = finish_latent(grid, mix_ext, (top, bottom, left, right), w_point, clat, clon, wide)

    obs_scale = float((rows_here * tiles) ** -0.5)
    cell_scale = float((cells * tiles) ** -0.5)
    full, latent = lax.optimization_barrier((full, latent))
    sibling = lax.ppermute(full, "core", SWAP)
    grad_in, grad_out, grad_point, grad_depth = unpack(
        core, full, sibling, spec, width, obs_scale, cell_scale
    )
    return latent.reshape(clat, clon, width), grad_in, grad_out, grad_point, grad_depth


def solution(mesh):
    lat, lon = mesh.devices.shape
    fine = Mesh(mesh.devices.reshape(lat // 2, 2, lon), ("x", "core", "lon"))
    everyone = P(("x", "core", "lon"))
    field = P(LAT, "lon", None)
    in_specs = (everyone, everyone, everyone, P(), P(), P(), P(), field)
    out_specs = (field, P(), P(), P(), P())
    return jax.shard_map(
        on_device, mesh=fine, in_specs=in_specs, out_specs=out_specs, check_vma=False
    )
```

```python
import functools

import jax
import jax.numpy as jnp
from jax import lax
from jax.experimental import pallas as pl
from jax.experimental.pallas import tpu as pltpu
from jax.sharding import Mesh
from jax.sharding import PartitionSpec as P

LANES = 128
bf16 = jnp.bfloat16
f32 = jnp.float32
i32 = jnp.int32


def params(mib):
    return pltpu.CompilerParams(vmem_limit_bytes=mib * 1024 * 1024)


def round_up(n, m):
    return -(-n // m) * m


def dot(a, b, dims=(1, 0)):
    return lax.dot_general(
        a, b, (((dims[0],), (dims[1],)), ((), ())), preferred_element_type=f32
    )


def cost(us):
    return pl.CostEstimate(flops=us * 1153500000, bytes_accessed=0, transcendentals=0)


def smem():
    return pl.BlockSpec(memory_space=pltpu.SMEM)


def anywhere():
    return pl.BlockSpec(memory_space=pl.ANY)


def vmem():
    return pl.BlockSpec(memory_space=pltpu.VMEM)


def route_kernel(tiles, cap, clon, places_ref, rows_ref, out_ref):
    spec, n = rows_ref.shape
    head = out_ref.shape[1] - LANES
    owner = places_ref[0:1, :]
    hits = owner == lax.broadcasted_iota(i32, (tiles, n), 0)
    above = lax.broadcasted_iota(i32, (n, n), 0) < lax.broadcasted_iota(i32, (n, n), 1)
    count = dot(hits.astype(f32).astype(bf16), above.astype(f32).astype(bf16))
    rank = jnp.sum(jnp.where(hits, count, 0.0), axis=0, keepdims=True)
    slot = owner * cap + rank.astype(i32)
    cell = places_ref[1:2, :]
    line = lax.broadcasted_iota(i32, (LANES - (spec - head), n), 0)
    high = cell // clon
    spots = jnp.where(line == 0, high, jnp.where(line == 1, cell - high * clon, 0)).astype(f32)
    last = jnp.concatenate([rows_ref[head:, :].astype(f32), spots], axis=0).astype(bf16)
    first = rows_ref[:head, :]
    step = min(256, tiles * cap)

    def body(t, carry):
        base = t * step
        place = lax.broadcasted_iota(i32, (step, n), 0) + base
        pick = (slot == place).astype(f32).astype(bf16)
        at = pl.ds(pl.multiple_of(base, step), step)
        out_ref[at, :head] = dot(pick, first, (1, 1)).astype(bf16)
        out_ref[at, head:] = dot(pick, last, (1, 1)).astype(bf16)
        return carry

    lax.fori_loop(0, tiles * cap // step, body, 0)


def route(places, rows, tiles, cap, clon, spec_wide):
    return pl.pallas_call(
        functools.partial(route_kernel, tiles, cap, clon),
        out_shape=jax.ShapeDtypeStruct((tiles * cap, spec_wide), bf16),
        in_specs=[vmem()] * 2,
        out_specs=vmem(),
        compiler_params=params(12),
        cost_estimate=cost(3),
        name="route",
    )(places, rows)


PAD = 16
CHUNK = 32


def shifted(ref, n, row, start, by, size):
    return ref[n, row, pl.ds(start + by, size), :]


def grid_grad_kernel(
    clat, clon, wide, one_ref, cot_ref, east_ref, west_ref, north_ref, south_ref, wp_ref, wd_ref,
    cott_hbm, gm_hbm, gg_hbm, cott_ref, gm_ref, gg_ref, cot_ext, east, west, sems,
):
    width = wp_ref.shape[0]
    w_point = wp_ref[...]
    one = one_ref[0]
    east[...] = east_ref[...].astype(f32)
    west[...] = west_ref[...].astype(f32)
    line = lax.broadcasted_iota(i32, (wide - clon, width), 0)
    puts = [
        pltpu.make_async_copy(source, target, sems.at[i])
        for i, (source, target) in enumerate(
            ((gg_ref, gg_hbm), (gm_ref, gm_hbm), (cott_ref, cott_hbm))
        )
    ]

    def mixed_grad(e, rows):
        g = dot(rows, w_point, (1, 1)).astype(bf16).astype(f32)
        for n in range(width // LANES):
            cols = slice(n * LANES, (n + 1) * LANES)
            gm_ref[n, e, 0:PAD, :] = g[clon:, cols]
            gm_ref[n, e, PAD : PAD + clon, :] = g[:clon, cols]
            gm_ref[n, e, PAD + clon :, :] = g[clon:, cols]

    def matmul(i, carry):
        at = pl.multiple_of((i + 1) * wide, 16)
        cot_ext[pl.ds(at, clon), :] = cot_ref[pl.ds(pl.multiple_of(i * clon, 16), clon), :]
        tail = jnp.where(
            line == 0, east[pl.ds(i, 1), :], jnp.where(line == wide - clon - 1, west[pl.ds(i, 1), :], 0.0)
        )
        cot_ext[pl.ds(at + clon, wide - clon), :] = tail.astype(bf16)
        mixed_grad(i + 1, cot_ext[pl.ds(at, wide), :])
        return carry

    for ref, e in ((north_ref, 0), (south_ref, clat + 1)):
        cot_ext[e * wide : (e + 1) * wide, :] = ref[...]
        mixed_grad(e, ref[...])
    used = (clat + 2) * wide
    cot_ext[used:, :] = jnp.zeros((cot_ext.shape[0] - used, width), bf16)
    lax.fori_loop(0, clat, matmul, 0)
    puts[1].start()

    def conv(i, carry):
        for n in range(width // LANES):
            cols = slice(n * LANES, (n + 1) * LANES)
            for j in range(0, clon, CHUNK):
                at = pl.ds(pl.multiple_of(i * clon + j, CHUNK), CHUNK)
                out = cot_ref[at, cols].astype(f32)
                for a in range(3):
                    for b in range(3):
                        k = 3 * a + b
                        g = shifted(gm_ref, n, i + 2 - a, PAD + j, (1 - b) * one, CHUNK)
                        out = out + wd_ref[k : k + 1, cols] * g
                gg_ref[at, cols] = out.astype(bf16)
        return carry

    lax.fori_loop(0, clat, conv, 0)
    puts[0].start()

    def transpose(k, carry):
        at = pl.ds(pl.multiple_of(k * LANES, LANES), LANES)
        cott_ref[:, at] = cot_ext[at, :].T
        return carry

    lax.fori_loop(0, cot_ext.shape[0] // LANES, transpose, 0)
    puts[2].start()
    for put in puts:
        put.wait()


def grid_grad(one, cot, sides, w_point, w_depth, clat, clon, wide):
    width = w_point.shape[0]
    ext_rows = round_up((clat + 2) * wide, LANES)
    outs = (
        jax.ShapeDtypeStruct((width, ext_rows), bf16),
        jax.ShapeDtypeStruct((width // LANES, clat + 2, clon + 2 * PAD, LANES), f32),
        jax.ShapeDtypeStruct((clat * clon, width), bf16),
    )
    return pl.pallas_call(
        functools.partial(grid_grad_kernel, clat, clon, wide),
        out_shape=outs,
        in_specs=[smem()] + [vmem()] * 7,
        out_specs=(anywhere(),) * 3,
        scratch_shapes=[pltpu.VMEM(x.shape, x.dtype) for x in outs]
        + [pltpu.VMEM((ext_rows, width), bf16)]
        + [pltpu.VMEM((clat, width), f32)] * 2
        + [pltpu.SemaphoreType.DMA((3,))],
        compiler_params=params(50),
        cost_estimate=cost(10),
        name="grid_grad",
    )(one, cot, *sides, w_point, w_depth)


def write_halves(core, total, start, mine_ref, other_ref, first=0, size=None):
    size = total.shape[0] if size is None else size
    half = total.shape[1] // 2
    for ref, base in ((mine_ref, core * half), (other_ref, (1 - core) * half)):
        for n in range(half // LANES):
            cols = pl.ds(pl.multiple_of(base + n * LANES, LANES), LANES)
            ref[n, start : start + size, :] = total[first : first + size, cols].astype(bf16)


def clear_tail(start, *refs):
    for ref in refs:
        unused = ref.shape[1] - start
        if unused:
            ref[:, start:, :] = jnp.zeros((ref.shape[0], unused, LANES), bf16)


def owner_kernel(
    spec, clat, clon, wide, core_ref, rows_hbm, wit_hbm, wot_hbm, wo_hbm, gg_hbm, wd_hbm, gm_hbm, cott_hbm,
    grid_hbm, mix_hbm, east_hbm, west_hbm, mine_hbm, other_hbm,
    rows_ref, wit_ref, wot_ref, wo_ref, gg_ref, wd_ref, gm_ref, cott_ref,
    grid_ref, mix_ref, east_ref, west_ref, mine_ref, other_ref,
    padded, emb_ref, gi, gi_out, go, gp, gd, sems,
):
    core, one = core_ref[0], core_ref[1]
    slots, spec_wide = rows_ref.shape
    cells, width = gg_ref.shape
    sources = rows_hbm, wit_hbm, wot_hbm, wo_hbm, gg_hbm, wd_hbm, gm_hbm, cott_hbm
    targets = rows_ref, wit_ref, wot_ref, wo_ref, gg_ref, wd_ref, gm_ref, cott_ref
    loads = [
        pltpu.make_async_copy(source, target, sems.at[i])
        for i, (source, target) in enumerate(zip(sources, targets))
    ]
    for load in loads:
        load.start()
    outs = (
        (grid_ref, grid_hbm), (mix_ref, mix_hbm), (east_ref, east_hbm), (west_ref, west_hbm),
        (mine_ref, mine_hbm), (other_ref, other_hbm),
    )
    puts = [
        pltpu.make_async_copy(source, target, sems.at[len(loads) + i])
        for i, (source, target) in enumerate(outs)
    ]
    gi[...] = jnp.zeros_like(gi)
    go[...] = jnp.zeros_like(go)
    gd[...] = jnp.zeros_like(gd)
    blocks = width // LANES
    side = jnp.zeros((blocks, clat + 4, PAD, LANES), f32)
    padded[:, :, :PAD, :] = side
    padded[:, :, PAD + clon :, :] = side
    for e in (0, 1, clat + 2, clat + 3):
        padded[:, e, PAD : PAD + clon, :] = jnp.zeros((blocks, clon, LANES), f32)
    used = (clat + 2) * wide
    mix_ref[used:, :] = jnp.zeros((mix_ref.shape[0] - used, width), bf16)
    for load in loads[:5]:
        load.wait()

    step = min(512, slots)

    def encode(t, carry):
        at = pl.ds(pl.multiple_of(t * step, step), step)
        rows = rows_ref[at, :]
        preact = dot(wit_ref[...], rows, (1, 1))
        sig = 1.0 / (1.0 + jnp.exp(-preact))
        hidden = (preact * sig).astype(bf16)
        emb_ref[:, at] = dot(wot_ref[...], hidden).astype(bf16)
        place = rows[:, spec : spec + 1].astype(f32) * clon + rows[:, spec + 1 : spec + 2].astype(f32)
        hits = place.astype(i32) == lax.broadcasted_iota(i32, (step, cells), 1)
        g_emb = dot(hits.astype(f32).astype(bf16), gg_ref[...]).astype(bf16)
        go[...] += dot(hidden, g_emb)
        g_hid = dot(wo_ref[...], g_emb, (1, 1))
        g_pre = (g_hid * (sig * (1.0 + preact * (1.0 - sig)))).astype(bf16)
        gi[...] += dot(g_pre, rows)
        return carry

    lax.fori_loop(0, slots // step, encode, 0)

    last = rows_ref[:, spec_wide - LANES :]
    col = spec - (spec_wide - LANES)
    lane = lax.broadcasted_iota(i32, (16, LANES), 1)
    pick = jnp.where(lane == col, float(clon), jnp.where(lane == col + 1, 1.0, 0.0)).astype(bf16)
    place = dot(pick, last, (1, 1))[0:1, :].astype(i32)
    block = 4 * clon

    def bins(t, carry):
        cell = lax.broadcasted_iota(i32, (block, slots), 0) + t * block
        hits = (place == cell).astype(f32).astype(bf16)
        grid = dot(hits, emb_ref[...], (1, 1)).astype(bf16)
        grid_ref[pl.ds(pl.multiple_of(t * block, 16), block), :] = grid
        for n in range(blocks):
            part = grid[:, n * LANES : (n + 1) * LANES].astype(f32)
            padded[n, pl.ds(4 * t + 2, 4), PAD : PAD + clon, :] = part.reshape(4, clon, LANES)
        return carry

    lax.fori_loop(0, cells // block, bins, 0)
    puts[0].start()
    for load in loads[5:]:
        load.wait()

    def conv(e, carry):
        for n in range(blocks):
            cols = slice(n * LANES, (n + 1) * LANES)
            weights = [wd_ref[k : k + 1, cols] for k in range(9)]
            taps = [gd[8 * k : 8 * k + 8, cols] for k in range(9)]
            for j in range(0, clon, CHUNK):
                at = PAD + j
                grads = [shifted(gm_ref, n, e, at, (1 - b) * one, CHUNK) for b in range(3)]
                mixed = None
                for a in range(3):
                    for b in range(3):
                        k = 3 * a + b
                        cell = shifted(padded, n, e + a, at, (b - 1) * one, CHUNK)
                        mixed = weights[k] * cell if mixed is None else mixed + weights[k] * cell
                    middle = padded[n, e + a, at : at + CHUNK, :]
                    for b in range(3):
                        k = 3 * a + b
                        part = (grads[b] * middle).reshape(CHUNK // 8, 8, LANES)
                        taps[k] = taps[k] + jnp.sum(part, axis=0)
                out_at = pl.ds(pl.multiple_of(e * wide + j, 16), CHUNK)
                mix_ref[out_at, cols] = mixed.astype(bf16)
            for k in range(9):
                gd[8 * k : 8 * k + 8, cols] = taps[k]
            ends = []
            for b, at in ((0, PAD + clon), (2, PAD - 8)):
                end = None
                for a in range(3):
                    term = weights[3 * a + b] * shifted(padded, n, e + a, at, (b - 1) * one, 8)
                    end = term if end is None else end + term
                ends.append(end)
            east_ref[e, :, cols] = ends[0]
            west_ref[e, :, cols] = ends[1]
            out_at = pl.ds(pl.multiple_of(e * wide + clon, 16), wide - clon)
            mix_ref[out_at, cols] = jnp.concatenate(ends, axis=0).astype(bf16)
        return carry

    lax.fori_loop(0, clat + 2, conv, 0)
    for put in puts[1:4]:
        put.start()
    gp[...] = dot(cott_ref[...], mix_ref[...]).T
    gi_out[...] = gi[...].T
    gi_rows = round_up(spec, 16)
    taps = [jnp.sum(gd[8 * k : 8 * k + 8, :], axis=0, keepdims=True) for k in range(9)]
    gd[0:16, :] = jnp.concatenate(taps + [jnp.zeros((7, width), f32)], axis=0)
    start = 0
    for total, size in ((go, width), (gi_out, gi_rows), (gp, width), (gd, 16)):
        write_halves(core, total, start, mine_ref, other_ref, 0, size)
        start += size
    clear_tail(start, mine_ref, other_ref)
    for put in puts[4:]:
        put.start()
    for put in puts:
        put.wait()


def owner_part(core, operands, spec, clat, clon, wide, out_rows):
    slots, spec_wide = operands[0].shape
    width = operands[2].shape[0]
    half = jax.ShapeDtypeStruct((width // LANES // 2, out_rows, LANES), bf16)
    column = jax.ShapeDtypeStruct((clat + 2, 8, width), f32)
    grid = jax.ShapeDtypeStruct((clat * clon, width), bf16)
    ext = jax.ShapeDtypeStruct(operands[-1].shape[::-1], bf16)
    outs = grid, ext, column, column, half, half
    return pl.pallas_call(
        functools.partial(owner_kernel, spec, clat, clon, wide),
        out_shape=outs,
        in_specs=[smem()] + [anywhere()] * len(operands),
        out_specs=(anywhere(),) * len(outs),
        scratch_shapes=[pltpu.VMEM(x.shape, x.dtype) for x in operands + outs]
        + [
            pltpu.VMEM((width // LANES, clat + 4, clon + 2 * PAD, LANES), f32),
            pltpu.VMEM((width, slots), bf16),
            pltpu.VMEM((width, spec_wide), f32),
            pltpu.VMEM((spec_wide, width), f32),
            pltpu.VMEM((width, width), f32),
            pltpu.VMEM((width, width), f32),
            pltpu.VMEM((72, width), f32),
            pltpu.SemaphoreType.DMA((len(operands) + len(outs),)),
        ],
        compiler_params=params(56),
        cost_estimate=cost(20),
        name="owner",
    )(core, *operands)


def latent_kernel(
    clat, clon, wide, grid_ref, mix_ref, top_ref, bottom_ref, left_ref, right_ref, wp_ref, out_ref
):
    width = wp_ref.shape[0]
    w_point = wp_ref[...]
    line = lax.broadcasted_iota(i32, (clon, width), 0)

    def body(i, carry):
        at = pl.ds(pl.multiple_of(i * clon, 16), clon)
        mixed = mix_ref[pl.ds(pl.multiple_of((i + 1) * wide, 16), clon), :].astype(f32)
        mixed = mixed + (i == 0).astype(f32) * top_ref[:clon, :].astype(f32)
        mixed = mixed + (i == clat - 1).astype(f32) * bottom_ref[:clon, :].astype(f32)
        mixed = mixed + jnp.where(
            line == 0, left_ref[pl.ds(i, 1), :], jnp.where(line == clon - 1, right_ref[pl.ds(i, 1), :], 0.0)
        )
        out = grid_ref[at, :].astype(f32) + dot(mixed.astype(bf16), w_point)
        out_ref[at, :] = out.astype(bf16)
        return carry

    lax.fori_loop(0, clat, body, 0)


def finish_latent(grid, mix_ext, sides, w_point, clat, clon, wide):
    return pl.pallas_call(
        functools.partial(latent_kernel, clat, clon, wide),
        out_shape=jax.ShapeDtypeStruct(grid.shape, bf16),
        in_specs=[vmem()] * 7,
        out_specs=vmem(),
        compiler_params=params(6),
        cost_estimate=cost(5),
        name="latent",
    )(grid, mix_ext, *sides, w_point)


def totals_kernel(parts_ref, *refs):
    out_ref = refs[-1]
    total = jnp.sum(parts_ref[...].astype(f32), axis=0).astype(bf16)
    out_ref[...] = jnp.broadcast_to(total[None], parts_ref.shape)


def totals(parts, *after):
    return pl.pallas_call(
        totals_kernel,
        out_shape=jax.ShapeDtypeStruct(parts.shape, bf16),
        in_specs=[vmem()] + [anywhere()] * len(after),
        out_specs=vmem(),
        compiler_params=params(6),
        cost_estimate=cost(1),
        name="totals",
    )(parts, *after)


def unpack_kernel(
    obs_scale, cell_scale, core_ref, own_ref, sibling_ref, gi_ref, go_ref, gp_ref, gd_ref
):
    spec, width = gi_ref.shape
    chips = own_ref.shape[0]
    count = width // (2 * LANES)
    per = chips // count
    core = core_ref[0]
    for ref, half in ((own_ref, core), (sibling_ref, 1 - core)):
        for n in range(count):
            cols = pl.ds(pl.multiple_of((half * count + n) * LANES, LANES), LANES)
            block = ref[n * per : (n + 1) * per].astype(f32)
            block = block.reshape(per * block.shape[1], LANES)
            start = 0
            for out_ref, scale in (
                (go_ref, obs_scale), (gi_ref, obs_scale), (gp_ref, cell_scale), (gd_ref, cell_scale)
            ):
                size = out_ref.shape[0]
                out_ref[:, cols] = block[start : start + size] * scale
                start += round_up(size, 16)


def unpack(core, own, sibling, spec, width, obs_scale, cell_scale):
    return pl.pallas_call(
        functools.partial(unpack_kernel, obs_scale, cell_scale),
        out_shape=tuple(
            jax.ShapeDtypeStruct((rows, width), f32) for rows in (spec, width, width, 9)
        ),
        in_specs=[smem()] + [vmem()] * 2,
        out_specs=(vmem(),) * 4,
        compiler_params=params(8),
        cost_estimate=cost(3),
        name="unpack",
    )(core, own, sibling)


def neighbours(axes, periodic):
    count = lax.axis_size(axes)
    up = [(i, i + 1) for i in range(count - 1)]
    if periodic:
        up.append((count - 1, 0))
    return up, [(t, s) for s, t in up]


LAT = ("x", "core")
CHIPS = ("x", "lon")


SWAP = [(0, 1), (1, 0)]


def core_sum(mine, other):
    got = lax.ppermute(other, "core", SWAP)
    return (mine.astype(f32) + got.astype(f32)).astype(bf16)


def spread(values):
    chips = lax.axis_size(CHIPS)
    blocks, rows, _ = values.shape
    values = values.reshape(chips, blocks * rows // chips, LANES)
    return lax.all_to_all(values, CHIPS, split_axis=0, concat_axis=0, tiled=True)


def on_device(spectra, owner, cell, w_in, w_out, w_point, w_depth, cotangent):
    tiles = lax.axis_size(LAT) * lax.axis_size("lon")
    rows_here, spec = spectra.shape
    cap = max(2, 2 * rows_here // tiles)
    clat, clon, width = cotangent.shape
    cells = clat * clon
    wide = clon + 16
    spec_wide = round_up(spec + 2, LANES)
    core = jnp.stack([lax.axis_index("core"), jnp.int32(1)])
    one = jnp.ones((1,), i32)
    east_way, west_way = neighbours("lon", True)
    south_way, north_way = neighbours(LAT, False)

    from_west = lax.ppermute(cotangent[:, -1], "lon", east_way)
    from_east = lax.ppermute(cotangent[:, 0], "lon", west_way)

    places = jnp.concatenate([owner.reshape(1, rows_here), cell.reshape(1, rows_here)], axis=0)
    outgoing = route(places, spectra.T, tiles, cap, clon, spec_wide)
    outgoing, from_west, from_east, w_in, w_out = lax.optimization_barrier(
        (outgoing, from_west, from_east, w_in, w_out)
    )
    arrived = lax.all_to_all(
        outgoing.reshape(tiles, cap, spec_wide), ("x", "core", "lon"), 0, 0, tiled=True
    ).reshape(tiles * cap, spec_wide)

    fill = jnp.zeros((wide - clon - 2, width), bf16)

    def edge_row(i):
        return jnp.concatenate([cotangent[i], from_east[i, None], fill, from_west[i, None]], axis=0)

    from_north = lax.ppermute(edge_row(clat - 1), LAT, south_way)
    from_south = lax.ppermute(edge_row(0), LAT, north_way)
    cot_t, g_mixed, g_grid = grid_grad(
        one,
        cotangent.reshape(cells, width),
        (from_east, from_west, from_north, from_south),
        w_point, w_depth, clat, clon, wide,
    )
    w_in_t = jnp.pad(w_in.T, ((0, 0), (0, spec_wide - spec)))

    out_rows = round_up(2 * width + round_up(spec, 16) + 16, 16 * tiles * LANES // width)
    operands = arrived, w_in_t, w_out.T, w_out, g_grid, w_depth, g_mixed, cot_t
    grid, mix_ext, east, west, mine, other = owner_part(
        core, operands, spec, clat, clon, wide, out_rows
    )
    summed = core_sum(mine, other)
    summed, grid, mix_ext, east, west = lax.optimization_barrier((summed, grid, mix_ext, east, west))
    parts = spread(summed)

    top = lax.ppermute(mix_ext[(clat + 1) * wide : (clat + 2) * wide], LAT, south_way)
    bottom = lax.ppermute(mix_ext[:wide], LAT, north_way)

    def edge_column(own, at):
        return own[1:-1].at[0].add(top[at].astype(f32)).at[-1].add(bottom[at].astype(f32))

    left = lax.ppermute(edge_column(east[:, 0], clon), "lon", east_way)
    right = lax.ppermute(edge_column(west[:, 7], wide - 1), "lon", west_way)
    sent = totals(parts, left, right)
    full = lax.all_to_all(sent, CHIPS, split_axis=0, concat_axis=0, tiled=True)
    latent = finish_latent(grid, mix_ext, (top, bottom, left, right), w_point, clat, clon, wide)

    obs_scale = float((rows_here * tiles) ** -0.5)
    cell_scale = float((cells * tiles) ** -0.5)
    full, latent = lax.optimization_barrier((full, latent))
    sibling = lax.ppermute(full, "core", SWAP)
    grad_in, grad_out, grad_point, grad_depth = unpack(
        core, full, sibling, spec, width, obs_scale, cell_scale
    )
    return latent.reshape(clat, clon, width), grad_in, grad_out, grad_point, grad_depth


def solution(mesh):
    lat, lon = mesh.devices.shape
    fine = Mesh(mesh.devices.reshape(lat // 2, 2, lon), ("x", "core", "lon"))
    everyone = P(("x", "core", "lon"))
    field = P(LAT, "lon", None)
    in_specs = (everyone, everyone, everyone, P(), P(), P(), P(), field)
    out_specs = (field, P(), P(), P(), P())
    return jax.shard_map(
        on_device, mesh=fine, in_specs=in_specs, out_specs=out_specs, check_vma=False
    )
```

```python
import functools

import jax
import jax.numpy as jnp
from jax import lax
from jax.experimental import pallas as pl
from jax.experimental.pallas import tpu as pltpu
from jax.sharding import Mesh
from jax.sharding import PartitionSpec as P

LANES = 128
bf16 = jnp.bfloat16
f32 = jnp.float32
i32 = jnp.int32


def params(mib):
    return pltpu.CompilerParams(vmem_limit_bytes=mib * 1024 * 1024)


def round_up(n, m):
    return -(-n // m) * m


def dot(a, b, dims=(1, 0)):
    return lax.dot_general(
        a, b, (((dims[0],), (dims[1],)), ((), ())), preferred_element_type=f32
    )


def cost(us):
    return pl.CostEstimate(flops=us * 1153500000, bytes_accessed=0, transcendentals=0)


def smem():
    return pl.BlockSpec(memory_space=pltpu.SMEM)


def anywhere():
    return pl.BlockSpec(memory_space=pl.ANY)


def vmem():
    return pl.BlockSpec(memory_space=pltpu.VMEM)


def route_kernel(tiles, cap, clon, places_ref, rows_ref, out_ref):
    spec, n = rows_ref.shape
    head = out_ref.shape[1] - LANES
    owner = places_ref[0:1, :]
    hits = owner == lax.broadcasted_iota(i32, (tiles, n), 0)
    above = lax.broadcasted_iota(i32, (n, n), 0) < lax.broadcasted_iota(i32, (n, n), 1)
    count = dot(hits.astype(f32).astype(bf16), above.astype(f32).astype(bf16))
    rank = jnp.sum(jnp.where(hits, count, 0.0), axis=0, keepdims=True)
    slot = owner * cap + rank.astype(i32)
    cell = places_ref[1:2, :]
    line = lax.broadcasted_iota(i32, (LANES - (spec - head), n), 0)
    high = cell // clon
    spots = jnp.where(line == 0, high, jnp.where(line == 1, cell - high * clon, 0)).astype(f32)
    last = jnp.concatenate([rows_ref[head:, :].astype(f32), spots], axis=0).astype(bf16)
    first = rows_ref[:head, :]
    step = min(256, tiles * cap)

    def body(t, carry):
        base = t * step
        place = lax.broadcasted_iota(i32, (step, n), 0) + base
        pick = (slot == place).astype(f32).astype(bf16)
        at = pl.ds(pl.multiple_of(base, step), step)
        out_ref[at, :head] = dot(pick, first, (1, 1)).astype(bf16)
        out_ref[at, head:] = dot(pick, last, (1, 1)).astype(bf16)
        return carry

    lax.fori_loop(0, tiles * cap // step, body, 0)


def route(places, rows, tiles, cap, clon, spec_wide):
    return pl.pallas_call(
        functools.partial(route_kernel, tiles, cap, clon),
        out_shape=jax.ShapeDtypeStruct((tiles * cap, spec_wide), bf16),
        in_specs=[vmem()] * 2,
        out_specs=vmem(),
        compiler_params=params(12),
        cost_estimate=cost(3),
        name="route",
    )(places, rows)


PAD = 16
CHUNK = 32


def shifted(ref, n, row, start, by, size):
    return ref[n, row, pl.ds(start + by, size), :]


def grid_grad_kernel(
    clat, clon, wide, one_ref, cot_ref, east_ref, west_ref, north_ref, south_ref, wp_ref, wd_ref,
    cott_hbm, gm_hbm, gg_hbm, cott_ref, gm_ref, gg_ref, cot_ext, east, west, sems,
):
    width = wp_ref.shape[0]
    w_point = wp_ref[...]
    one = one_ref[0]
    east[...] = east_ref[...].astype(f32)
    west[...] = west_ref[...].astype(f32)
    line = lax.broadcasted_iota(i32, (wide - clon, width), 0)
    puts = [
        pltpu.make_async_copy(source, target, sems.at[i])
        for i, (source, target) in enumerate(
            ((gg_ref, gg_hbm), (gm_ref, gm_hbm), (cott_ref, cott_hbm))
        )
    ]

    def mixed_grad(e, rows):
        g = dot(rows, w_point, (1, 1)).astype(bf16).astype(f32)
        for n in range(width // LANES):
            cols = slice(n * LANES, (n + 1) * LANES)
            gm_ref[n, e, 0:PAD, :] = g[clon:, cols]
            gm_ref[n, e, PAD : PAD + clon, :] = g[:clon, cols]
            gm_ref[n, e, PAD + clon :, :] = g[clon:, cols]

    def matmul(i, carry):
        at = pl.multiple_of((i + 1) * wide, 16)
        cot_ext[pl.ds(at, clon), :] = cot_ref[pl.ds(pl.multiple_of(i * clon, 16), clon), :]
        tail = jnp.where(
            line == 0, east[pl.ds(i, 1), :], jnp.where(line == wide - clon - 1, west[pl.ds(i, 1), :], 0.0)
        )
        cot_ext[pl.ds(at + clon, wide - clon), :] = tail.astype(bf16)
        mixed_grad(i + 1, cot_ext[pl.ds(at, wide), :])
        return carry

    for ref, e in ((north_ref, 0), (south_ref, clat + 1)):
        cot_ext[e * wide : (e + 1) * wide, :] = ref[...]
        mixed_grad(e, ref[...])
    used = (clat + 2) * wide
    cot_ext[used:, :] = jnp.zeros((cot_ext.shape[0] - used, width), bf16)
    lax.fori_loop(0, clat, matmul, 0)
    puts[1].start()

    def conv(i, carry):
        for n in range(width // LANES):
            cols = slice(n * LANES, (n + 1) * LANES)
            for j in range(0, clon, CHUNK):
                at = pl.ds(pl.multiple_of(i * clon + j, CHUNK), CHUNK)
                out = cot_ref[at, cols].astype(f32)
                for a in range(3):
                    for b in range(3):
                        k = 3 * a + b
                        g = shifted(gm_ref, n, i + 2 - a, PAD + j, (1 - b) * one, CHUNK)
                        out = out + wd_ref[k : k + 1, cols] * g
                gg_ref[at, cols] = out.astype(bf16)
        return carry

    lax.fori_loop(0, clat, conv, 0)
    puts[0].start()

    def transpose(k, carry):
        at = pl.ds(pl.multiple_of(k * LANES, LANES), LANES)
        cott_ref[:, at] = cot_ext[at, :].T
        return carry

    lax.fori_loop(0, cot_ext.shape[0] // LANES, transpose, 0)
    puts[2].start()
    for put in puts:
        put.wait()


def grid_grad(one, cot, sides, w_point, w_depth, clat, clon, wide):
    width = w_point.shape[0]
    ext_rows = round_up((clat + 2) * wide, LANES)
    outs = (
        jax.ShapeDtypeStruct((width, ext_rows), bf16),
        jax.ShapeDtypeStruct((width // LANES, clat + 2, clon + 2 * PAD, LANES), f32),
        jax.ShapeDtypeStruct((clat * clon, width), bf16),
    )
    return pl.pallas_call(
        functools.partial(grid_grad_kernel, clat, clon, wide),
        out_shape=outs,
        in_specs=[smem()] + [vmem()] * 7,
        out_specs=(anywhere(),) * 3,
        scratch_shapes=[pltpu.VMEM(x.shape, x.dtype) for x in outs]
        + [pltpu.VMEM((ext_rows, width), bf16)]
        + [pltpu.VMEM((clat, width), f32)] * 2
        + [pltpu.SemaphoreType.DMA((3,))],
        compiler_params=params(50),
        cost_estimate=cost(10),
        name="grid_grad",
    )(one, cot, *sides, w_point, w_depth)


def write_halves(core, total, start, mine_ref, other_ref, first=0, size=None):
    size = total.shape[0] if size is None else size
    half = total.shape[1] // 2
    for ref, base in ((mine_ref, core * half), (other_ref, (1 - core) * half)):
        for n in range(half // LANES):
            cols = pl.ds(pl.multiple_of(base + n * LANES, LANES), LANES)
            ref[n, start : start + size, :] = total[first : first + size, cols].astype(bf16)


def clear_tail(start, *refs):
    for ref in refs:
        unused = ref.shape[1] - start
        if unused:
            ref[:, start:, :] = jnp.zeros((ref.shape[0], unused, LANES), bf16)


def start_loads(sources, targets, sems):
    loads = [
        pltpu.make_async_copy(source, target, sems.at[i])
        for i, (source, target) in enumerate(zip(sources, targets))
    ]
    for load in loads:
        load.start()
    return loads


def encode_kernel(
    spec, clon, ids_ref, rows_ref, wit_hbm, wot_hbm, gg_hbm, wo_hbm,
    emb_ref, mine_ref, other_ref, mine_rest, other_rest,
    wit_ref, wot_ref, gg_ref, wo_ref, gi, gi_out, go, sems,
):
    loads = start_loads((wit_hbm, wot_hbm, gg_hbm, wo_hbm), (wit_ref, wot_ref, gg_ref, wo_ref), sems)
    core = ids_ref[0]
    slots, spec_wide = rows_ref.shape
    cells, width = gg_ref.shape
    step = min(512, slots)

    for t in range(slots // step):
        at = slice(t * step, (t + 1) * step)
        rows = rows_ref[at, :]
        place = rows[:, spec : spec + 1].astype(f32) * clon + rows[:, spec + 1 : spec + 2].astype(f32)
        hits = place.astype(i32) == lax.broadcasted_iota(i32, (step, cells), 1)
        hits = hits.astype(f32).astype(bf16)
        if t == 0:
            loads[0].wait()
        preact = dot(wit_ref[...], rows, (1, 1))
        sig = 1.0 / (1.0 + jnp.exp(-preact))
        hidden = (preact * sig).astype(bf16)
        if t == 0:
            loads[1].wait()
        emb_ref[:, at] = dot(wot_ref[...], hidden).astype(bf16)
        if t == 0:
            loads[2].wait()
        g_emb = dot(hits, gg_ref[...]).astype(bf16)
        g_out = dot(hidden, g_emb)
        if t == 0:
            loads[3].wait()
        g_hid = dot(wo_ref[...], g_emb, (1, 1))
        g_pre = (g_hid * (sig * (1.0 + preact * (1.0 - sig)))).astype(bf16)
        g_in = dot(g_pre, rows)
        if t == 0:
            go[...] = g_out
            gi[...] = g_in
        else:
            go[...] += g_out
            gi[...] += g_in

    gi_out[...] = gi[...].T
    head = spec_wide - LANES
    write_halves(core, go, 0, mine_ref, other_ref)
    write_halves(core, gi_out, width, mine_ref, other_ref, 0, head)
    write_halves(core, gi_out, 0, mine_rest, other_rest, head, mine_rest.shape[1])
    clear_tail(width + head, mine_ref, other_ref)


def encode(ids, rows, weights, spec, clon, out_rows, rest_rows):
    slots, spec_wide = rows.shape
    width = weights[-1].shape[0]
    half = jax.ShapeDtypeStruct((width // LANES // 2, out_rows, LANES), bf16)
    rest = jax.ShapeDtypeStruct((width // LANES // 2, rest_rows, LANES), bf16)
    return pl.pallas_call(
        functools.partial(encode_kernel, spec, clon),
        out_shape=(jax.ShapeDtypeStruct((width, slots), bf16), half, half, rest, rest),
        in_specs=[smem(), vmem()] + [anywhere()] * len(weights),
        out_specs=(vmem(),) * 5,
        scratch_shapes=[pltpu.VMEM(x.shape, x.dtype) for x in weights]
        + [
            pltpu.VMEM((width, spec_wide), f32),
            pltpu.VMEM((spec_wide, width), f32),
            pltpu.VMEM((width, width), f32),
            pltpu.SemaphoreType.DMA((len(weights),)),
        ],
        compiler_params=params(24),
        cost_estimate=cost(10),
        name="encode",
    )(ids, rows, *weights)


def bins_kernel(spec, clon, rows_ref, emb_ref, grid_ref, grid_hbm, sem):
    slots, spec_wide = rows_ref.shape
    cells = grid_ref.shape[0]
    last = rows_ref[:, spec_wide - LANES :]
    col = spec - (spec_wide - LANES)
    lane = lax.broadcasted_iota(i32, (16, LANES), 1)
    pick = jnp.where(lane == col, float(clon), jnp.where(lane == col + 1, 1.0, 0.0)).astype(bf16)
    place = dot(pick, last, (1, 1))[0:1, :].astype(i32)
    block = 4 * clon

    def body(t, carry):
        cell = lax.broadcasted_iota(i32, (block, slots), 0) + t * block
        hits = (place == cell).astype(f32).astype(bf16)
        grid = dot(hits, emb_ref[...], (1, 1)).astype(bf16)
        grid_ref[pl.ds(pl.multiple_of(t * block, 16), block), :] = grid
        return carry

    lax.fori_loop(0, cells // block, body, 0)
    put = pltpu.make_async_copy(grid_ref, grid_hbm, sem)
    put.start()
    put.wait()


def bins(rows, emb, spec, cells, clon):
    grid = jax.ShapeDtypeStruct((cells, emb.shape[0]), bf16)
    return pl.pallas_call(
        functools.partial(bins_kernel, spec, clon),
        out_shape=(grid, grid),
        in_specs=[vmem()] * 2,
        out_specs=(vmem(), anywhere()),
        scratch_shapes=[pltpu.SemaphoreType.DMA],
        compiler_params=params(12),
        cost_estimate=cost(4),
        name="bins",
    )(rows, emb)


def mix_kernel(
    clat, clon, wide, ids_ref, grid_ref, wd_ref, gm_ref, after_ref,
    mix_ref, gd_ref, mix_hbm, east_hbm, west_hbm, east_ref, west_ref, padded, gd, sems,
):
    one = ids_ref[1]
    width = grid_ref.shape[1]
    blocks = width // LANES
    puts = [
        pltpu.make_async_copy(source, target, sems.at[i])
        for i, (source, target) in enumerate(
            ((mix_ref, mix_hbm), (east_ref, east_hbm), (west_ref, west_hbm))
        )
    ]
    gd[...] = jnp.zeros_like(gd)
    side = jnp.zeros((blocks, clat + 4, PAD, LANES), f32)
    padded[:, :, :PAD, :] = side
    padded[:, :, PAD + clon :, :] = side
    for e in (0, 1, clat + 2, clat + 3):
        padded[:, e, PAD : PAD + clon, :] = jnp.zeros((blocks, clon, LANES), f32)
    used = (clat + 2) * wide
    mix_ref[used:, :] = jnp.zeros((mix_ref.shape[0] - used, width), bf16)

    def widen(i, carry):
        at = pl.ds(pl.multiple_of(i * clon, 16), clon)
        for n in range(blocks):
            part = grid_ref[at, n * LANES : (n + 1) * LANES].astype(f32)
            padded[n, i + 2, PAD : PAD + clon, :] = part
        return carry

    lax.fori_loop(0, clat, widen, 0)

    def conv(e, carry):
        for n in range(blocks):
            cols = slice(n * LANES, (n + 1) * LANES)
            weights = [wd_ref[k : k + 1, cols] for k in range(9)]
            taps = [gd[8 * k : 8 * k + 8, cols] for k in range(9)]
            for j in range(0, clon, CHUNK):
                at = PAD + j
                grads = [shifted(gm_ref, n, e, at, (1 - b) * one, CHUNK) for b in range(3)]
                mixed = None
                for a in range(3):
                    for b in range(3):
                        k = 3 * a + b
                        cell = shifted(padded, n, e + a, at, (b - 1) * one, CHUNK)
                        mixed = weights[k] * cell if mixed is None else mixed + weights[k] * cell
                    middle = padded[n, e + a, at : at + CHUNK, :]
                    for b in range(3):
                        k = 3 * a + b
                        part = (grads[b] * middle).reshape(CHUNK // 8, 8, LANES)
                        taps[k] = taps[k] + jnp.sum(part, axis=0)
                out_at = pl.ds(pl.multiple_of(e * wide + j, 16), CHUNK)
                mix_ref[out_at, cols] = mixed.astype(bf16)
            for k in range(9):
                gd[8 * k : 8 * k + 8, cols] = taps[k]
            ends = []
            for b, at in ((0, PAD + clon), (2, PAD - 8)):
                end = None
                for a in range(3):
                    term = weights[3 * a + b] * shifted(padded, n, e + a, at, (b - 1) * one, 8)
                    end = term if end is None else end + term
                ends.append(end)
            east_ref[e, :, cols] = ends[0]
            west_ref[e, :, cols] = ends[1]
            out_at = pl.ds(pl.multiple_of(e * wide + clon, 16), wide - clon)
            mix_ref[out_at, cols] = jnp.concatenate(ends, axis=0).astype(bf16)
        return carry

    lax.fori_loop(0, clat + 2, conv, 0)
    for put in puts:
        put.start()
    taps = [jnp.sum(gd[8 * k : 8 * k + 8, :], axis=0, keepdims=True) for k in range(9)]
    gd_ref[...] = jnp.concatenate(taps + [jnp.zeros((7, width), f32)], axis=0)
    for put in puts:
        put.wait()


def mix(ids, grid, w_depth, g_mixed, after, clat, clon, wide):
    width = grid.shape[1]
    column = jax.ShapeDtypeStruct((clat + 2, 8, width), f32)
    ext = jax.ShapeDtypeStruct((round_up((clat + 2) * wide, LANES), width), bf16)
    return pl.pallas_call(
        functools.partial(mix_kernel, clat, clon, wide),
        out_shape=(ext, jax.ShapeDtypeStruct((16, width), f32), ext, column, column),
        in_specs=[smem()] + [vmem()] * 3 + [anywhere()],
        out_specs=(vmem(),) * 2 + (anywhere(),) * 3,
        scratch_shapes=[pltpu.VMEM(column.shape, column.dtype)] * 2
        + [
            pltpu.VMEM((width // LANES, clat + 4, clon + 2 * PAD, LANES), f32),
            pltpu.VMEM((72, width), f32),
            pltpu.SemaphoreType.DMA((3,)),
        ],
        compiler_params=params(16),
        cost_estimate=cost(10),
        name="mix",
    )(ids, grid, w_depth, g_mixed, after)


def point_kernel(
    ids_ref, cott_ref, mix_ref, gd_ref, mine_rest, other_rest, after_ref, mine_ref, other_ref, gp
):
    core = ids_ref[0]
    width = mix_ref.shape[1]
    rest = mine_rest.shape[1]
    gp[...] = dot(cott_ref[...], mix_ref[...]).T
    write_halves(core, gp, 0, mine_ref, other_ref)
    mine_ref[:, width : width + rest, :] = mine_rest[...]
    other_ref[:, width : width + rest, :] = other_rest[...]
    write_halves(core, gd_ref, width + rest, mine_ref, other_ref, 0, 16)
    clear_tail(width + rest + 16, mine_ref, other_ref)


def point(ids, cot_t, mix_ext, grad_depth, rest, after, out_rows):
    width = mix_ext.shape[1]
    half = jax.ShapeDtypeStruct((width // LANES // 2, out_rows, LANES), bf16)
    return pl.pallas_call(
        point_kernel,
        out_shape=(half, half),
        in_specs=[smem()] + [vmem()] * 5 + [anywhere()],
        out_specs=(vmem(),) * 2,
        scratch_shapes=[pltpu.VMEM((width, width), f32)],
        compiler_params=params(12),
        cost_estimate=cost(3),
        name="point",
    )(ids, cot_t, mix_ext, grad_depth, *rest, after)


def latent_kernel(
    clat, clon, wide, grid_ref, mix_ref, top_ref, bottom_ref, left_ref, right_ref, wp_ref, out_ref
):
    width = wp_ref.shape[0]
    w_point = wp_ref[...]
    line = lax.broadcasted_iota(i32, (clon, width), 0)

    def body(i, carry):
        at = pl.ds(pl.multiple_of(i * clon, 16), clon)
        mixed = mix_ref[pl.ds(pl.multiple_of((i + 1) * wide, 16), clon), :].astype(f32)
        mixed = mixed + (i == 0).astype(f32) * top_ref[:clon, :].astype(f32)
        mixed = mixed + (i == clat - 1).astype(f32) * bottom_ref[:clon, :].astype(f32)
        mixed = mixed + jnp.where(
            line == 0, left_ref[pl.ds(i, 1), :], jnp.where(line == clon - 1, right_ref[pl.ds(i, 1), :], 0.0)
        )
        out = grid_ref[at, :].astype(f32) + dot(mixed.astype(bf16), w_point)
        out_ref[at, :] = out.astype(bf16)
        return carry

    lax.fori_loop(0, clat, body, 0)


def finish_latent(grid, mix_ext, sides, w_point, clat, clon, wide):
    return pl.pallas_call(
        functools.partial(latent_kernel, clat, clon, wide),
        out_shape=jax.ShapeDtypeStruct(grid.shape, bf16),
        in_specs=[vmem()] * 7,
        out_specs=vmem(),
        compiler_params=params(6),
        cost_estimate=cost(5),
        name="latent",
    )(grid, mix_ext, *sides, w_point)


def split_kernel(ids_ref, mine_ref, got_ref, keep_ref, send_ref):
    x = ids_ref[2]
    for ref, i in ((keep_ref, x), (send_ref, 1 - x)):
        at = pl.ds(i, 1)
        ref[...] = (mine_ref[at].astype(f32) + got_ref[at].astype(f32))[0].astype(bf16)


def split(ids, mine, got):
    half = jax.ShapeDtypeStruct(mine.shape[1:], bf16)
    return pl.pallas_call(
        split_kernel,
        out_shape=(half, half),
        in_specs=[smem()] + [vmem()] * 2,
        out_specs=(vmem(),) * 2,
        compiler_params=params(8),
        cost_estimate=cost(1),
        name="split",
    )(ids, mine, got)


def merge_kernel(a_keep, a_got, b_keep, b_got, out_ref):
    count = out_ref.shape[0]
    start = 0
    for keep, got in ((a_keep, a_got), (b_keep, b_got)):
        total = (keep[...].astype(f32) + got[...].astype(f32)).astype(bf16)
        size = total.shape[0] // count
        out_ref[:, start : start + size, :] = total.reshape(count, size, LANES)
        start += size


def merge(a_keep, a_got, b_keep, b_got, count):
    rows = (a_keep.shape[0] + b_keep.shape[0]) // count
    return pl.pallas_call(
        merge_kernel,
        out_shape=jax.ShapeDtypeStruct((count, rows, LANES), bf16),
        in_specs=[vmem()] * 4,
        out_specs=vmem(),
        compiler_params=params(8),
        cost_estimate=cost(1),
        name="merge",
    )(a_keep, a_got, b_keep, b_got)


def totals_kernel(parts_ref, *refs):
    out_ref = refs[-1]
    total = jnp.sum(parts_ref[...].astype(f32), axis=0).astype(bf16)
    out_ref[...] = jnp.broadcast_to(total[None], out_ref.shape)


def totals(parts, chips, *after):
    return pl.pallas_call(
        totals_kernel,
        out_shape=jax.ShapeDtypeStruct((chips,) + parts.shape[1:], bf16),
        in_specs=[vmem()] + [anywhere()] * len(after),
        out_specs=vmem(),
        compiler_params=params(8),
        cost_estimate=cost(1),
        name="totals",
    )(parts, *after)


def unpack_kernel(
    rows_a, rest, obs_scale, cell_scale, ids_ref, own_ref, sibling_ref, gi_ref, go_ref, gp_ref, gd_ref
):
    spec, width = gi_ref.shape
    chips = own_ref.shape[0]
    count = width // (2 * LANES)
    per = chips // count
    core = ids_ref[0]
    cut = rows_a // per
    head = spec - spec % LANES
    for ref, half in ((own_ref, core), (sibling_ref, 1 - core)):
        for n in range(count):
            cols = pl.ds(pl.multiple_of((half * count + n) * LANES, LANES), LANES)
            block = ref[n * per : (n + 1) * per].astype(f32)
            a = block[:, :cut].reshape(rows_a, LANES)
            b = block[:, cut:].reshape(per * (block.shape[1] - cut), LANES)
            go_ref[:, cols] = a[:width] * obs_scale
            gi_ref[:head, cols] = a[width : width + head] * obs_scale
            gp_ref[:, cols] = b[:width] * cell_scale
            gi_ref[head:, cols] = b[width : width + spec - head] * obs_scale
            gd_ref[:, cols] = b[width + rest : width + rest + gd_ref.shape[0]] * cell_scale


def unpack(ids, own, sibling, spec, width, rows_a, rest, obs_scale, cell_scale):
    return pl.pallas_call(
        functools.partial(unpack_kernel, rows_a, rest, obs_scale, cell_scale),
        out_shape=tuple(
            jax.ShapeDtypeStruct((rows, width), f32) for rows in (spec, width, width, 9)
        ),
        in_specs=[smem()] + [vmem()] * 2,
        out_specs=(vmem(),) * 4,
        compiler_params=params(8),
        cost_estimate=cost(3),
        name="unpack",
    )(ids, own, sibling)


def neighbours(axes, periodic):
    count = lax.axis_size(axes)
    up = [(i, i + 1) for i in range(count - 1)]
    if periodic:
        up.append((count - 1, 0))
    return up, [(t, s) for s, t in up]


LAT = ("x", "core")
CHIPS = ("x", "lon")


SWAP = [(0, 1), (1, 0)]


def spread(values, axes):
    return lax.all_to_all(values, axes, split_axis=0, concat_axis=0, tiled=True)


def on_device(spectra, owner, cell, w_in, w_out, w_point, w_depth, cotangent):
    tiles = lax.axis_size(LAT) * lax.axis_size("lon")
    rows_here, spec = spectra.shape
    cap = max(2, 2 * rows_here // tiles)
    clat, clon, width = cotangent.shape
    cells = clat * clon
    wide = clon + 16
    spec_wide = round_up(spec + 2, LANES)
    ids = jnp.stack([lax.axis_index("core"), jnp.int32(1), lax.axis_index("x")])
    one = jnp.ones((1,), i32)
    east_way, west_way = neighbours("lon", True)
    south_way, north_way = neighbours(LAT, False)

    from_west = lax.ppermute(cotangent[:, -1], "lon", east_way)
    from_east = lax.ppermute(cotangent[:, 0], "lon", west_way)

    places = jnp.concatenate([owner.reshape(1, rows_here), cell.reshape(1, rows_here)], axis=0)
    outgoing = route(places, spectra.T, tiles, cap, clon, spec_wide)
    outgoing, from_west, from_east, w_in, w_out = lax.optimization_barrier(
        (outgoing, from_west, from_east, w_in, w_out)
    )
    arrived = lax.all_to_all(
        outgoing.reshape(tiles, cap, spec_wide), ("x", "core", "lon"), 0, 0, tiled=True
    ).reshape(tiles * cap, spec_wide)

    fill = jnp.zeros((wide - clon - 2, width), bf16)

    def edge_row(i):
        return jnp.concatenate([cotangent[i], from_east[i, None], fill, from_west[i, None]], axis=0)

    from_north = lax.ppermute(edge_row(clat - 1), LAT, south_way)
    from_south = lax.ppermute(edge_row(0), LAT, north_way)
    cot_t, g_mixed, g_grid = grid_grad(
        one,
        cotangent.reshape(cells, width),
        (from_east, from_west, from_north, from_south),
        w_point, w_depth, clat, clon, wide,
    )
    w_in_t = jnp.pad(w_in.T, ((0, 0), (0, spec_wide - spec)))

    chips, pairs = lax.axis_size(CHIPS), lax.axis_size("x") == 2
    align = 16 * tiles * LANES // width
    head = spec - spec % LANES
    rest = round_up(spec - head, 16)
    rows_a = round_up(width + head, align)
    rows_b = round_up(width + rest + 16, align)
    emb, mine_a, other_a, *rest_halves = encode(
        ids, arrived, (w_in_t, w_out.T, g_grid, w_out), spec, clon, rows_a, rest
    )
    got_a = lax.ppermute(other_a, "core", SWAP)
    grid_here, grid = bins(arrived, emb, spec, cells, clon)
    keep_a, send_a = split(ids, mine_a, got_a) if pairs else (mine_a, got_a)

    mix_here, grad_depth, mix_ext, east, west = mix(
        ids, grid_here, w_depth, g_mixed, keep_a, clat, clon, wide
    )
    got_a = lax.ppermute(send_a, "x", SWAP) if pairs else send_a
    mine_b, other_b = point(ids, cot_t, mix_here, grad_depth, rest_halves, got_a, rows_b)
    got_b = lax.ppermute(other_b, "core", SWAP)
    if pairs:
        keep_b, send_b = split(ids, mine_b, got_b)
        got_b = lax.ppermute(send_b, "x", SWAP)
        summed = merge(keep_a, got_a, keep_b, got_b, lax.axis_size("lon"))
    else:
        sums = [
            (mine.astype(f32) + got.astype(f32)).astype(bf16).reshape(chips, -1, LANES)
            for mine, got in ((keep_a, send_a), (mine_b, got_b))
        ]
        summed = jnp.concatenate(sums, axis=1)
    summed, mix_ext, east, west = lax.optimization_barrier((summed, mix_ext, east, west))
    parts = spread(summed, "lon" if pairs else CHIPS)

    top = lax.ppermute(mix_ext[(clat + 1) * wide : (clat + 2) * wide], LAT, south_way)
    bottom = lax.ppermute(mix_ext[:wide], LAT, north_way)

    def edge_column(own, at):
        return own[1:-1].at[0].add(top[at].astype(f32)).at[-1].add(bottom[at].astype(f32))

    left = lax.ppermute(edge_column(east[:, 0], clon), "lon", east_way)
    right = lax.ppermute(edge_column(west[:, 7], wide - 1), "lon", west_way)
    full = spread(totals(parts, chips, left, right), CHIPS)
    latent = finish_latent(grid, mix_ext, (top, bottom, left, right), w_point, clat, clon, wide)

    obs_scale = float((rows_here * tiles) ** -0.5)
    cell_scale = float((cells * tiles) ** -0.5)
    full, latent = lax.optimization_barrier((full, latent))
    sibling = lax.ppermute(full, "core", SWAP)
    grad_in, grad_out, grad_point, grad_depth = unpack(
        ids, full, sibling, spec, width, rows_a, rest, obs_scale, cell_scale
    )
    return latent.reshape(clat, clon, width), grad_in, grad_out, grad_point, grad_depth


def solution(mesh):
    lat, lon = mesh.devices.shape
    fine = Mesh(mesh.devices.reshape(lat // 2, 2, lon), ("x", "core", "lon"))
    everyone = P(("x", "core", "lon"))
    field = P(LAT, "lon", None)
    in_specs = (everyone, everyone, everyone, P(), P(), P(), P(), field)
    out_specs = (field, P(), P(), P(), P())
    return jax.shard_map(
        on_device, mesh=fine, in_specs=in_specs, out_specs=out_specs, check_vma=False
    )
```

```python
import functools

import jax
import jax.numpy as jnp
from jax import lax
from jax.experimental import pallas as pl
from jax.experimental.pallas import tpu as pltpu
from jax.sharding import Mesh
from jax.sharding import PartitionSpec as P

LANES = 128
bf16 = jnp.bfloat16
f32 = jnp.float32
i32 = jnp.int32


def params(mib):
    return pltpu.CompilerParams(vmem_limit_bytes=mib * 1024 * 1024)


def round_up(n, m):
    return -(-n // m) * m


def dot(a, b, dims=(1, 0)):
    return lax.dot_general(
        a, b, (((dims[0],), (dims[1],)), ((), ())), preferred_element_type=f32
    )


def cost(us):
    return pl.CostEstimate(flops=us * 1153500000, bytes_accessed=0, transcendentals=0)


def smem():
    return pl.BlockSpec(memory_space=pltpu.SMEM)


def anywhere():
    return pl.BlockSpec(memory_space=pl.ANY)


def vmem():
    return pl.BlockSpec(memory_space=pltpu.VMEM)


def route_kernel(tiles, cap, clon, places_ref, rows_ref, out_ref):
    spec, n = rows_ref.shape
    head = out_ref.shape[1] - LANES
    owner = places_ref[0:1, :]
    hits = owner == lax.broadcasted_iota(i32, (tiles, n), 0)
    above = lax.broadcasted_iota(i32, (n, n), 0) < lax.broadcasted_iota(i32, (n, n), 1)
    count = dot(hits.astype(f32).astype(bf16), above.astype(f32).astype(bf16))
    rank = jnp.sum(jnp.where(hits, count, 0.0), axis=0, keepdims=True)
    slot = owner * cap + rank.astype(i32)
    cell = places_ref[1:2, :]
    line = lax.broadcasted_iota(i32, (LANES - (spec - head), n), 0)
    high = cell // clon
    spots = jnp.where(line == 0, high, jnp.where(line == 1, cell - high * clon, 0)).astype(f32)
    last = jnp.concatenate([rows_ref[head:, :].astype(f32), spots], axis=0).astype(bf16)
    first = rows_ref[:head, :]
    step = min(256, tiles * cap)

    def body(t, carry):
        base = t * step
        place = lax.broadcasted_iota(i32, (step, n), 0) + base
        pick = (slot == place).astype(f32).astype(bf16)
        at = pl.ds(pl.multiple_of(base, step), step)
        out_ref[at, :head] = dot(pick, first, (1, 1)).astype(bf16)
        out_ref[at, head:] = dot(pick, last, (1, 1)).astype(bf16)
        return carry

    lax.fori_loop(0, tiles * cap // step, body, 0)


def route(places, rows, tiles, cap, clon, spec_wide):
    return pl.pallas_call(
        functools.partial(route_kernel, tiles, cap, clon),
        out_shape=jax.ShapeDtypeStruct((tiles * cap, spec_wide), bf16),
        in_specs=[vmem()] * 2,
        out_specs=vmem(),
        compiler_params=params(12),
        cost_estimate=cost(3),
        name="route",
    )(places, rows)


GROUPS = 8
CHUNK = 8 * GROUPS


def column_of(place, per):
    return per * (place % GROUPS) + place // GROUPS


def place_of(column, per):
    return GROUPS * (column % per) + column // per


def one_hot(wanted, count):
    hit = wanted == lax.broadcasted_iota(i32, (wanted.shape[0], count), 1)
    return hit.astype(f32).astype(bf16)


def grid_grad_kernel(
    clat, clon, wide, cot_ref, east_ref, west_ref, north_ref, south_ref, wp_ref, wd_ref,
    cott_hbm, gm_hbm, gg_hbm, cott_ref, gm_ref, gg_ref, cot_ext, cot_own, east, west, sems,
):
    width = wp_ref.shape[0]
    per = clon // GROUPS
    w_point = wp_ref[...]
    east[...] = east_ref[...].astype(f32)
    west[...] = west_ref[...].astype(f32)
    line = lax.broadcasted_iota(i32, (wide - clon, width), 0)
    place = lax.broadcasted_iota(i32, (wide, 1), 0)
    column = column_of(place, per) - 1
    spread_order = one_hot(jnp.where(column < 0, wide - 1, column), wide)
    ends = jnp.where(place == clon + GROUPS - 1, clon, jnp.where(place == clon + GROUPS, wide - 1, -1))
    point_order = one_hot(jnp.where(place < clon, column_of(place, per), ends), wide)
    puts = [
        pltpu.make_async_copy(source, target, sems.at[i])
        for i, (source, target) in enumerate(
            ((gg_ref, gg_hbm), (gm_ref, gm_hbm), (cott_ref, cott_hbm))
        )
    ]

    def reorder(e, rows):
        ordered = dot(spread_order, rows)
        g = dot(ordered.astype(bf16), w_point, (1, 1)).astype(bf16).astype(f32)
        for n in range(width // LANES):
            gm_ref[n, e] = g[:, n * LANES : (n + 1) * LANES]
        cot_ext[pl.ds(pl.multiple_of(e * wide, 16), wide), :] = dot(point_order, rows).astype(bf16)
        return ordered

    def matmul(i, carry):
        at = pl.ds(pl.multiple_of(i * clon, 16), clon)
        tail = jnp.where(
            line == 0, east[pl.ds(i, 1), :], jnp.where(line == wide - clon - 1, west[pl.ds(i, 1), :], 0.0)
        )
        ordered = reorder(i + 1, jnp.concatenate([cot_ref[at, :], tail.astype(bf16)], axis=0))
        cot_own[at, :] = ordered[GROUPS : GROUPS + clon].astype(bf16)
        return carry

    reorder(0, north_ref[...])
    reorder(clat + 1, south_ref[...])
    used = (clat + 2) * wide
    cot_ext[used:, :] = jnp.zeros((cot_ext.shape[0] - used, width), bf16)
    lax.fori_loop(0, clat, matmul, 0)
    puts[1].start()

    def conv(i, carry):
        for n in range(width // LANES):
            cols = slice(n * LANES, (n + 1) * LANES)
            for c in range(0, clon, CHUNK):
                at = pl.ds(pl.multiple_of(i * clon + c, 16), CHUNK)
                out = cot_own[at, cols].astype(f32)
                for a in range(3):
                    g = gm_ref[n, i + 2 - a, c : c + CHUNK + 2 * GROUPS, :]
                    for b in range(3):
                        k = 3 * a + b
                        first = GROUPS * (2 - b)
                        out = out + wd_ref[k : k + 1, cols] * g[first : first + CHUNK]
                gg_ref[at, cols] = out.astype(bf16)
        return carry

    lax.fori_loop(0, clat, conv, 0)
    puts[0].start()

    def transpose(k, carry):
        at = pl.ds(pl.multiple_of(k * LANES, LANES), LANES)
        cott_ref[:, at] = cot_ext[at, :].T
        return carry

    lax.fori_loop(0, cot_ext.shape[0] // LANES, transpose, 0)
    puts[2].start()
    for put in puts:
        put.wait()


def grid_grad(cot, sides, w_point, w_depth, clat, clon, wide):
    width = w_point.shape[0]
    ext_rows = round_up((clat + 2) * wide, LANES)
    outs = (
        jax.ShapeDtypeStruct((width, ext_rows), bf16),
        jax.ShapeDtypeStruct((width // LANES, clat + 2, wide, LANES), f32),
        jax.ShapeDtypeStruct((clat * clon, width), bf16),
    )
    return pl.pallas_call(
        functools.partial(grid_grad_kernel, clat, clon, wide),
        out_shape=outs,
        in_specs=[vmem()] * 7,
        out_specs=(anywhere(),) * 3,
        scratch_shapes=[pltpu.VMEM(x.shape, x.dtype) for x in outs]
        + [pltpu.VMEM((ext_rows, width), bf16), pltpu.VMEM((clat * clon, width), bf16)]
        + [pltpu.VMEM((clat, width), f32)] * 2
        + [pltpu.SemaphoreType.DMA((3,))],
        compiler_params=params(58),
        cost_estimate=cost(10),
        name="grid_grad",
    )(cot, *sides, w_point, w_depth)


def write_halves(core, total, start, mine_ref, other_ref, first=0, size=None):
    size = total.shape[0] if size is None else size
    half = total.shape[1] // 2
    for ref, base in ((mine_ref, core * half), (other_ref, (1 - core) * half)):
        for n in range(half // LANES):
            cols = pl.ds(pl.multiple_of(base + n * LANES, LANES), LANES)
            ref[n, start : start + size, :] = total[first : first + size, cols].astype(bf16)


def clear_tail(start, *refs):
    for ref in refs:
        unused = ref.shape[1] - start
        if unused:
            ref[:, start:, :] = jnp.zeros((ref.shape[0], unused, LANES), bf16)


def start_loads(sources, targets, sems):
    loads = [
        pltpu.make_async_copy(source, target, sems.at[i])
        for i, (source, target) in enumerate(zip(sources, targets))
    ]
    for load in loads:
        load.start()
    return loads


def encode_kernel(
    spec, clon, ids_ref, rows_ref, wit_hbm, wot_hbm, gg_hbm, wo_hbm,
    emb_ref, mine_ref, other_ref, mine_rest, other_rest,
    wit_ref, wot_ref, gg_ref, wo_ref, gi, gi_out, go, sems,
):
    loads = start_loads((wit_hbm, wot_hbm, gg_hbm, wo_hbm), (wit_ref, wot_ref, gg_ref, wo_ref), sems)
    core = ids_ref[0]
    slots, spec_wide = rows_ref.shape
    cells, width = gg_ref.shape
    step = min(512, slots)

    for t in range(slots // step):
        at = slice(t * step, (t + 1) * step)
        rows = rows_ref[at, :]
        line = rows[:, spec : spec + 1].astype(f32).astype(i32)
        column = rows[:, spec + 1 : spec + 2].astype(f32).astype(i32)
        hits = one_hot(line * clon + place_of(column, clon // GROUPS), cells)
        if t == 0:
            loads[0].wait()
        preact = dot(wit_ref[...], rows, (1, 1))
        sig = 1.0 / (1.0 + jnp.exp(-preact))
        hidden = (preact * sig).astype(bf16)
        if t == 0:
            loads[1].wait()
        emb_ref[:, at] = dot(wot_ref[...], hidden).astype(bf16)
        if t == 0:
            loads[2].wait()
        g_emb = dot(hits, gg_ref[...]).astype(bf16)
        g_out = dot(hidden, g_emb)
        if t == 0:
            loads[3].wait()
        g_hid = dot(wo_ref[...], g_emb, (1, 1))
        g_pre = (g_hid * (sig * (1.0 + preact * (1.0 - sig)))).astype(bf16)
        g_in = dot(g_pre, rows)
        if t == 0:
            go[...] = g_out
            gi[...] = g_in
        else:
            go[...] += g_out
            gi[...] += g_in

    gi_out[...] = gi[...].T
    head = spec_wide - LANES
    write_halves(core, go, 0, mine_ref, other_ref)
    write_halves(core, gi_out, width, mine_ref, other_ref, 0, head)
    write_halves(core, gi_out, 0, mine_rest, other_rest, head, mine_rest.shape[1])
    clear_tail(width + head, mine_ref, other_ref)


def encode(ids, rows, weights, spec, clon, out_rows, rest_rows):
    slots, spec_wide = rows.shape
    width = weights[-1].shape[0]
    half = jax.ShapeDtypeStruct((width // LANES // 2, out_rows, LANES), bf16)
    rest = jax.ShapeDtypeStruct((width // LANES // 2, rest_rows, LANES), bf16)
    return pl.pallas_call(
        functools.partial(encode_kernel, spec, clon),
        out_shape=(jax.ShapeDtypeStruct((width, slots), bf16), half, half, rest, rest),
        in_specs=[smem(), vmem()] + [anywhere()] * len(weights),
        out_specs=(vmem(),) * 5,
        scratch_shapes=[pltpu.VMEM(x.shape, x.dtype) for x in weights]
        + [
            pltpu.VMEM((width, spec_wide), f32),
            pltpu.VMEM((spec_wide, width), f32),
            pltpu.VMEM((width, width), f32),
            pltpu.SemaphoreType.DMA((len(weights),)),
        ],
        compiler_params=params(59),
        cost_estimate=cost(10),
        name="encode",
    )(ids, rows, *weights)


def bins_kernel(spec, clat, clon, wide, rows_ref, emb_ref, wide_ref, grid_hbm, grid_ref, sem):
    slots, spec_wide = rows_ref.shape
    width = emb_ref.shape[0]
    blocks = width // LANES
    last = rows_ref[:, spec_wide - LANES :]
    col = spec - (spec_wide - LANES)
    lane = lax.broadcasted_iota(i32, (16, LANES), 1)
    pick = jnp.where(lane == col, float(clon), jnp.where(lane == col + 1, 1.0, 0.0)).astype(bf16)
    cell = dot(pick, last, (1, 1))[0:1, :].astype(i32)
    lines = 4
    place = lax.broadcasted_iota(i32, (wide, 1), 0)
    column = column_of(place, clon // GROUPS) - 1
    inside = (column >= 0) & (column < clon)
    wanted = [jnp.where(inside, column + k * clon, -clat * clon) for k in range(lines)]
    wanted = jnp.concatenate(wanted, axis=0)
    empty = jnp.zeros((blocks, 2, wide, LANES), f32)
    wide_ref[:, 0:2] = empty
    wide_ref[:, clat + 2 :] = empty

    def body(t, carry):
        hits = (cell == wanted + t * (lines * clon)).astype(f32).astype(bf16)
        grid = dot(hits, emb_ref[...], (1, 1)).astype(bf16).astype(f32)
        for k in range(lines):
            line = grid[k * wide : (k + 1) * wide]
            for n in range(blocks):
                wide_ref[n, t * lines + k + 2] = line[:, n * LANES : (n + 1) * LANES]
            at = pl.ds(pl.multiple_of((t * lines + k) * clon, 16), clon)
            grid_ref[at, :] = line[GROUPS : GROUPS + clon].astype(bf16)
        return carry

    lax.fori_loop(0, clat // lines, body, 0)
    put = pltpu.make_async_copy(grid_ref, grid_hbm, sem)
    put.start()
    put.wait()


def bins(rows, emb, spec, clat, clon, wide):
    width = emb.shape[0]
    grid = jax.ShapeDtypeStruct((clat * clon, width), bf16)
    wide_grid = jax.ShapeDtypeStruct((width // LANES, clat + 4, wide, LANES), f32)
    return pl.pallas_call(
        functools.partial(bins_kernel, spec, clat, clon, wide),
        out_shape=(wide_grid, grid),
        in_specs=[vmem()] * 2,
        out_specs=(vmem(), anywhere()),
        scratch_shapes=[pltpu.VMEM(grid.shape, bf16), pltpu.SemaphoreType.DMA],
        compiler_params=params(12),
        cost_estimate=cost(4),
        name="bins",
    )(rows, emb)


def mix_kernel(
    clat, clon, wide, grid_ref, wd_ref, gm_ref, after_ref,
    mix_ref, gd_ref, mix_hbm, east_hbm, west_hbm, east_ref, west_ref, gd, sems,
):
    width = wd_ref.shape[1]
    blocks = width // LANES
    puts = [
        pltpu.make_async_copy(source, target, sems.at[i])
        for i, (source, target) in enumerate(
            ((mix_ref, mix_hbm), (east_ref, east_hbm), (west_ref, west_hbm))
        )
    ]
    gd[...] = jnp.zeros_like(gd)
    used = (clat + 2) * wide
    mix_ref[used:, :] = jnp.zeros((mix_ref.shape[0] - used, width), bf16)
    group = lax.broadcasted_iota(i32, (GROUPS, LANES), 0)

    def conv(e, carry):
        for n in range(blocks):
            cols = slice(n * LANES, (n + 1) * LANES)
            weights = [wd_ref[k : k + 1, cols] for k in range(9)]
            taps = [gd[8 * k : 8 * k + 8, cols] for k in range(9)]
            for c in range(0, clon, CHUNK):
                grads = gm_ref[n, e, c : c + CHUNK + 2 * GROUPS, :]
                mixed = None
                for a in range(3):
                    cells = grid_ref[n, e + a, c : c + CHUNK + 2 * GROUPS, :]
                    middle = cells[GROUPS : GROUPS + CHUNK]
                    for b in range(3):
                        k = 3 * a + b
                        term = weights[k] * cells[GROUPS * b : GROUPS * b + CHUNK]
                        mixed = term if mixed is None else mixed + term
                        first = GROUPS * (2 - b)
                        part = (grads[first : first + CHUNK] * middle).reshape(CHUNK // 8, 8, LANES)
                        taps[k] = taps[k] + jnp.sum(part, axis=0)
                out_at = pl.ds(pl.multiple_of(e * wide + c, 16), CHUNK)
                mix_ref[out_at, cols] = mixed.astype(bf16)
            for k in range(9):
                gd[8 * k : 8 * k + 8, cols] = taps[k]
            ends = []
            for b, at, valid in ((0, clon, GROUPS - 1), (2, GROUPS, 0)):
                end = None
                for a in range(3):
                    term = weights[3 * a + b] * grid_ref[n, e + a, at : at + GROUPS, :]
                    end = term if end is None else end + term
                ends.append(jnp.where(group == valid, end, 0.0))
            east_ref[e, :, cols] = ends[0]
            west_ref[e, :, cols] = ends[1]
            out_at = pl.ds(pl.multiple_of(e * wide + clon, 16), wide - clon)
            mix_ref[out_at, cols] = jnp.concatenate(ends, axis=0).astype(bf16)
        return carry

    lax.fori_loop(0, clat + 2, conv, 0)
    for put in puts:
        put.start()
    taps = [jnp.sum(gd[8 * k : 8 * k + 8, :], axis=0, keepdims=True) for k in range(9)]
    gd_ref[...] = jnp.concatenate(taps + [jnp.zeros((7, width), f32)], axis=0)
    for put in puts:
        put.wait()


def mix(grid, w_depth, g_mixed, after, clat, clon, wide):
    width = w_depth.shape[1]
    column = jax.ShapeDtypeStruct((clat + 2, GROUPS, width), f32)
    ext = jax.ShapeDtypeStruct((round_up((clat + 2) * wide, LANES), width), bf16)
    return pl.pallas_call(
        functools.partial(mix_kernel, clat, clon, wide),
        out_shape=(ext, jax.ShapeDtypeStruct((16, width), f32), ext, column, column),
        in_specs=[vmem()] * 3 + [anywhere()],
        out_specs=(vmem(),) * 2 + (anywhere(),) * 3,
        scratch_shapes=[pltpu.VMEM(column.shape, column.dtype)] * 2
        + [pltpu.VMEM((72, width), f32), pltpu.SemaphoreType.DMA((3,))],
        compiler_params=params(8),
        cost_estimate=cost(8),
        name="mix",
    )(grid, w_depth, g_mixed, after)


def point_kernel(
    ids_ref, cott_ref, mix_ref, gd_ref, mine_rest, other_rest, after_ref, mine_ref, other_ref, gp
):
    core = ids_ref[0]
    width = mix_ref.shape[1]
    rest = mine_rest.shape[1]
    gp[...] = dot(cott_ref[...], mix_ref[...]).T
    write_halves(core, gp, 0, mine_ref, other_ref)
    mine_ref[:, width : width + rest, :] = mine_rest[...]
    other_ref[:, width : width + rest, :] = other_rest[...]
    write_halves(core, gd_ref, width + rest, mine_ref, other_ref, 0, 16)
    clear_tail(width + rest + 16, mine_ref, other_ref)


def point(ids, cot_t, mix_ext, grad_depth, rest, after, out_rows):
    width = mix_ext.shape[1]
    half = jax.ShapeDtypeStruct((width // LANES // 2, out_rows, LANES), bf16)
    return pl.pallas_call(
        point_kernel,
        out_shape=(half, half),
        in_specs=[smem()] + [vmem()] * 5 + [anywhere()],
        out_specs=(vmem(),) * 2,
        scratch_shapes=[pltpu.VMEM((width, width), f32)],
        compiler_params=params(12),
        cost_estimate=cost(3),
        name="point",
    )(ids, cot_t, mix_ext, grad_depth, *rest, after)


def latent_kernel(
    clat, clon, wide, grid_ref, mix_ref, top_ref, bottom_ref, left_ref, right_ref, wp_ref, out_ref
):
    width = wp_ref.shape[0]
    w_point = wp_ref[...]
    line = lax.broadcasted_iota(i32, (clon, width), 0)
    column = lax.broadcasted_iota(i32, (clon, 1), 0)
    natural_order = one_hot(place_of(column, clon // GROUPS), clon)

    def body(i, carry):
        at = pl.ds(pl.multiple_of(i * clon, 16), clon)
        mixed = mix_ref[pl.ds(pl.multiple_of((i + 1) * wide, 16), clon), :].astype(f32)
        mixed = mixed + (i == 0).astype(f32) * top_ref[:clon, :].astype(f32)
        mixed = mixed + (i == clat - 1).astype(f32) * bottom_ref[:clon, :].astype(f32)
        mixed = mixed + jnp.where(
            line == 0, left_ref[pl.ds(i, 1), :], jnp.where(line == clon - 1, right_ref[pl.ds(i, 1), :], 0.0)
        )
        out = grid_ref[at, :].astype(f32) + dot(mixed.astype(bf16), w_point)
        out_ref[at, :] = dot(natural_order, out.astype(bf16)).astype(bf16)
        return carry

    lax.fori_loop(0, clat, body, 0)


def finish_latent(grid, mix_ext, sides, w_point, clat, clon, wide):
    return pl.pallas_call(
        functools.partial(latent_kernel, clat, clon, wide),
        out_shape=jax.ShapeDtypeStruct(grid.shape, bf16),
        in_specs=[vmem()] * 7,
        out_specs=vmem(),
        compiler_params=params(6),
        cost_estimate=cost(5),
        name="latent",
    )(grid, mix_ext, *sides, w_point)


def split_kernel(ids_ref, mine_ref, got_ref, keep_ref, send_ref):
    x = ids_ref[1]
    for ref, i in ((keep_ref, x), (send_ref, 1 - x)):
        at = pl.ds(i, 1)
        ref[...] = (mine_ref[at].astype(f32) + got_ref[at].astype(f32))[0].astype(bf16)


def split(ids, mine, got):
    half = jax.ShapeDtypeStruct(mine.shape[1:], bf16)
    return pl.pallas_call(
        split_kernel,
        out_shape=(half, half),
        in_specs=[smem()] + [vmem()] * 2,
        out_specs=(vmem(),) * 2,
        compiler_params=params(8),
        cost_estimate=cost(1),
        name="split",
    )(ids, mine, got)


def merge_kernel(a_keep, a_got, b_keep, b_got, *refs):
    out_ref = refs[-1]
    count = out_ref.shape[0]
    start = 0
    for keep, got in ((a_keep, a_got), (b_keep, b_got)):
        total = (keep[...].astype(f32) + got[...].astype(f32)).astype(bf16)
        size = total.shape[0] // count
        out_ref[:, start : start + size, :] = total.reshape(count, size, LANES)
        start += size


def merge(a_keep, a_got, b_keep, b_got, count, *after):
    rows = (a_keep.shape[0] + b_keep.shape[0]) // count
    return pl.pallas_call(
        merge_kernel,
        out_shape=jax.ShapeDtypeStruct((count, rows, LANES), bf16),
        in_specs=[vmem()] * 4 + [anywhere()] * len(after),
        out_specs=vmem(),
        compiler_params=params(8),
        cost_estimate=cost(1),
        name="merge",
    )(a_keep, a_got, b_keep, b_got, *after)


def totals_kernel(parts_ref, *refs):
    out_ref = refs[-1]
    total = jnp.sum(parts_ref[...].astype(f32), axis=0).astype(bf16)
    out_ref[...] = jnp.broadcast_to(total[None], out_ref.shape)


def totals(parts, chips, *after):
    return pl.pallas_call(
        totals_kernel,
        out_shape=jax.ShapeDtypeStruct((chips,) + parts.shape[1:], bf16),
        in_specs=[vmem()] + [anywhere()] * len(after),
        out_specs=vmem(),
        compiler_params=params(8),
        cost_estimate=cost(1),
        name="totals",
    )(parts, *after)


def unpack_kernel(
    rows_a, rest, obs_scale, cell_scale, ids_ref, own_ref, sibling_ref, gi_ref, go_ref, gp_ref, gd_ref
):
    spec, width = gi_ref.shape
    chips = own_ref.shape[0]
    count = width // (2 * LANES)
    per = chips // count
    core = ids_ref[0]
    cut = rows_a // per
    head = spec - spec % LANES
    for ref, half in ((own_ref, core), (sibling_ref, 1 - core)):
        for n in range(count):
            cols = pl.ds(pl.multiple_of((half * count + n) * LANES, LANES), LANES)
            block = ref[n * per : (n + 1) * per].astype(f32)
            a = block[:, :cut].reshape(rows_a, LANES)
            b = block[:, cut:].reshape(per * (block.shape[1] - cut), LANES)
            go_ref[:, cols] = a[:width] * obs_scale
            gi_ref[:head, cols] = a[width : width + head] * obs_scale
            gp_ref[:, cols] = b[:width] * cell_scale
            gi_ref[head:, cols] = b[width : width + spec - head] * obs_scale
            gd_ref[:, cols] = b[width + rest : width + rest + gd_ref.shape[0]] * cell_scale


def unpack(ids, own, sibling, spec, width, rows_a, rest, obs_scale, cell_scale):
    return pl.pallas_call(
        functools.partial(unpack_kernel, rows_a, rest, obs_scale, cell_scale),
        out_shape=tuple(
            jax.ShapeDtypeStruct((rows, width), f32) for rows in (spec, width, width, 9)
        ),
        in_specs=[smem()] + [vmem()] * 2,
        out_specs=(vmem(),) * 4,
        compiler_params=params(8),
        cost_estimate=cost(3),
        name="unpack",
    )(ids, own, sibling)


def neighbours(axes, periodic):
    count = lax.axis_size(axes)
    up = [(i, i + 1) for i in range(count - 1)]
    if periodic:
        up.append((count - 1, 0))
    return up, [(t, s) for s, t in up]


LAT = ("x", "core")
CHIPS = ("x", "lon")


SWAP = [(0, 1), (1, 0)]


def spread(values, axes):
    return lax.all_to_all(values, axes, split_axis=0, concat_axis=0, tiled=True)


def on_device(spectra, owner, cell, w_in, w_out, w_point, w_depth, cotangent):
    tiles = lax.axis_size(LAT) * lax.axis_size("lon")
    rows_here, spec = spectra.shape
    cap = max(2, 2 * rows_here // tiles)
    clat, clon, width = cotangent.shape
    cells = clat * clon
    wide = clon + 16
    spec_wide = round_up(spec + 2, LANES)
    ids = jnp.stack([lax.axis_index("core"), lax.axis_index("x")])
    east_way, west_way = neighbours("lon", True)
    south_way, north_way = neighbours(LAT, False)

    from_west = lax.ppermute(cotangent[:, -1], "lon", east_way)
    from_east = lax.ppermute(cotangent[:, 0], "lon", west_way)

    places = jnp.concatenate([owner.reshape(1, rows_here), cell.reshape(1, rows_here)], axis=0)
    outgoing = route(places, spectra.T, tiles, cap, clon, spec_wide)
    outgoing, from_west, from_east, w_in, w_out = lax.optimization_barrier(
        (outgoing, from_west, from_east, w_in, w_out)
    )
    arrived = lax.all_to_all(
        outgoing.reshape(tiles, cap, spec_wide), ("x", "core", "lon"), 0, 0, tiled=True
    ).reshape(tiles * cap, spec_wide)

    fill = jnp.zeros((wide - clon - 2, width), bf16)

    def edge_row(i):
        return jnp.concatenate([cotangent[i], from_east[i, None], fill, from_west[i, None]], axis=0)

    from_north = lax.ppermute(edge_row(clat - 1), LAT, south_way)
    from_south = lax.ppermute(edge_row(0), LAT, north_way)
    cot_t, g_mixed, g_grid = grid_grad(
        cotangent.reshape(cells, width),
        (from_east, from_west, from_north, from_south),
        w_point, w_depth, clat, clon, wide,
    )
    w_in_t = jnp.pad(w_in.T, ((0, 0), (0, spec_wide - spec)))

    chips, pairs = lax.axis_size(CHIPS), lax.axis_size("x") == 2
    align = 16 * tiles * LANES // width
    head = spec - spec % LANES
    rest = round_up(spec - head, 16)
    rows_a = round_up(width + head, align)
    rows_b = round_up(width + rest + 16, align)
    emb, mine_a, other_a, *rest_halves = encode(
        ids, arrived, (w_in_t, w_out.T, g_grid, w_out), spec, clon, rows_a, rest
    )
    got_a = lax.ppermute(other_a, "core", SWAP)
    grid_here, grid = bins(arrived, emb, spec, clat, clon, wide)
    keep_a, send_a = split(ids, mine_a, got_a) if pairs else (mine_a, got_a)

    mix_here, grad_depth, mix_ext, east, west = mix(
        grid_here, w_depth, g_mixed, keep_a, clat, clon, wide
    )
    got_a = lax.ppermute(send_a, "x", SWAP) if pairs else send_a
    mine_b, other_b = point(ids, cot_t, mix_here, grad_depth, rest_halves, got_a, rows_b)
    got_b = lax.ppermute(other_b, "core", SWAP)
    if pairs:
        keep_b, send_b = split(ids, mine_b, got_b)
        send_b, mix_ext = lax.optimization_barrier((send_b, mix_ext))
        got_b = lax.ppermute(send_b, "x", SWAP)

    top = lax.ppermute(mix_ext[(clat + 1) * wide : (clat + 2) * wide], LAT, south_way)
    bottom = lax.ppermute(mix_ext[:wide], LAT, north_way)
    if pairs:
        summed = merge(keep_a, got_a, keep_b, got_b, lax.axis_size("lon"), top, bottom)
    else:
        sums = [
            (mine.astype(f32) + got.astype(f32)).astype(bf16).reshape(chips, -1, LANES)
            for mine, got in ((keep_a, send_a), (mine_b, got_b))
        ]
        summed = jnp.concatenate(sums, axis=1)
    summed, top, bottom, east, west = lax.optimization_barrier((summed, top, bottom, east, west))
    parts = spread(summed, "lon" if pairs else CHIPS)

    def edge_column(own, at):
        return own[1:-1].at[0].add(top[at].astype(f32)).at[-1].add(bottom[at].astype(f32))

    left = lax.ppermute(edge_column(east[:, GROUPS - 1], clon + GROUPS - 1), "lon", east_way)
    right = lax.ppermute(edge_column(west[:, 0], clon + GROUPS), "lon", west_way)
    full = spread(totals(parts, chips, left, right), CHIPS)
    latent = finish_latent(grid, mix_ext, (top, bottom, left, right), w_point, clat, clon, wide)

    obs_scale = float((rows_here * tiles) ** -0.5)
    cell_scale = float((cells * tiles) ** -0.5)
    full, latent = lax.optimization_barrier((full, latent))
    sibling = lax.ppermute(full, "core", SWAP)
    grad_in, grad_out, grad_point, grad_depth = unpack(
        ids, full, sibling, spec, width, rows_a, rest, obs_scale, cell_scale
    )
    return latent.reshape(clat, clon, width), grad_in, grad_out, grad_point, grad_depth


def solution(mesh):
    lat, lon = mesh.devices.shape
    fine = Mesh(mesh.devices.reshape(lat // 2, 2, lon), ("x", "core", "lon"))
    everyone = P(("x", "core", "lon"))
    field = P(LAT, "lon", None)
    in_specs = (everyone, everyone, everyone, P(), P(), P(), P(), field)
    out_specs = (field, P(), P(), P(), P())
    return jax.shard_map(
        on_device, mesh=fine, in_specs=in_specs, out_specs=out_specs, check_vma=False
    )
```

```python
import functools

import jax
import jax.numpy as jnp
from jax import lax
from jax.experimental import pallas as pl
from jax.experimental.pallas import tpu as pltpu
from jax.sharding import Mesh
from jax.sharding import PartitionSpec as P

LANES = 128
bf16 = jnp.bfloat16
f32 = jnp.float32
i32 = jnp.int32


def params(mib):
    return pltpu.CompilerParams(vmem_limit_bytes=mib * 1024 * 1024)


def round_up(n, m):
    return -(-n // m) * m


def dot(a, b, dims=(1, 0)):
    return lax.dot_general(
        a, b, (((dims[0],), (dims[1],)), ((), ())), preferred_element_type=f32
    )


def cost(us):
    return pl.CostEstimate(flops=us * 1153500000, bytes_accessed=0, transcendentals=0)


def smem():
    return pl.BlockSpec(memory_space=pltpu.SMEM)


def anywhere():
    return pl.BlockSpec(memory_space=pl.ANY)


def vmem():
    return pl.BlockSpec(memory_space=pltpu.VMEM)


def route_kernel(tiles, cap, clon, places_ref, rows_ref, out_ref):
    spec, n = rows_ref.shape
    head = out_ref.shape[1] - LANES
    owner = places_ref[0:1, :]
    hits = owner == lax.broadcasted_iota(i32, (tiles, n), 0)
    above = lax.broadcasted_iota(i32, (n, n), 0) < lax.broadcasted_iota(i32, (n, n), 1)
    count = dot(hits.astype(f32).astype(bf16), above.astype(f32).astype(bf16))
    rank = jnp.sum(jnp.where(hits, count, 0.0), axis=0, keepdims=True)
    slot = owner * cap + rank.astype(i32)
    cell = places_ref[1:2, :]
    line = lax.broadcasted_iota(i32, (LANES - (spec - head), n), 0)
    high = cell // clon
    spots = jnp.where(line == 0, high, jnp.where(line == 1, cell - high * clon, 0)).astype(f32)
    last = jnp.concatenate([rows_ref[head:, :].astype(f32), spots], axis=0).astype(bf16)
    first = rows_ref[:head, :]
    step = min(256, tiles * cap)

    def body(t, carry):
        base = t * step
        place = lax.broadcasted_iota(i32, (step, n), 0) + base
        pick = (slot == place).astype(f32).astype(bf16)
        at = pl.ds(pl.multiple_of(base, step), step)
        out_ref[at, :head] = dot(pick, first, (1, 1)).astype(bf16)
        out_ref[at, head:] = dot(pick, last, (1, 1)).astype(bf16)
        return carry

    lax.fori_loop(0, tiles * cap // step, body, 0)


def route(places, rows, tiles, cap, clon, spec_wide):
    return pl.pallas_call(
        functools.partial(route_kernel, tiles, cap, clon),
        out_shape=jax.ShapeDtypeStruct((tiles * cap, spec_wide), bf16),
        in_specs=[vmem()] * 2,
        out_specs=vmem(),
        compiler_params=params(12),
        cost_estimate=cost(3),
        name="route",
    )(places, rows)


GROUPS = 8
CHUNK = 8 * GROUPS


def column_of(place, per):
    return per * (place % GROUPS) + place // GROUPS


def place_of(column, per):
    return GROUPS * (column % per) + column // per


def one_hot(wanted, count):
    hit = wanted == lax.broadcasted_iota(i32, (wanted.shape[0], count), 1)
    return hit.astype(f32).astype(bf16)


def grid_grad_kernel(
    clat, clon, wide, cot_ref, east_ref, west_ref, north_ref, south_ref, wp_ref, wd_ref,
    cott_hbm, gm_hbm, gg_hbm, cott_ref, gm_ref, gg_ref, cot_ext, cot_own, east, west, sems,
):
    width = wp_ref.shape[0]
    per = clon // GROUPS
    w_point = wp_ref[...]
    east[...] = east_ref[...].astype(f32)
    west[...] = west_ref[...].astype(f32)
    line = lax.broadcasted_iota(i32, (wide - clon, width), 0)
    place = lax.broadcasted_iota(i32, (wide, 1), 0)
    column = column_of(place, per) - 1
    spread_order = one_hot(jnp.where(column < 0, wide - 1, column), wide)
    ends = jnp.where(place == clon + GROUPS - 1, clon, jnp.where(place == clon + GROUPS, wide - 1, -1))
    point_order = one_hot(jnp.where(place < clon, column_of(place, per), ends), wide)
    puts = [
        pltpu.make_async_copy(source, target, sems.at[i])
        for i, (source, target) in enumerate(
            ((gg_ref, gg_hbm), (gm_ref, gm_hbm), (cott_ref, cott_hbm))
        )
    ]

    def reorder(e, rows):
        ordered = dot(spread_order, rows)
        g = dot(ordered.astype(bf16), w_point, (1, 1)).astype(bf16).astype(f32)
        for n in range(width // LANES):
            gm_ref[n, e] = g[:, n * LANES : (n + 1) * LANES]
        cot_ext[pl.ds(pl.multiple_of(e * wide, 16), wide), :] = dot(point_order, rows).astype(bf16)
        return ordered

    def matmul(i, carry):
        at = pl.ds(pl.multiple_of(i * clon, 16), clon)
        tail = jnp.where(
            line == 0, east[pl.ds(i, 1), :], jnp.where(line == wide - clon - 1, west[pl.ds(i, 1), :], 0.0)
        )
        ordered = reorder(i + 1, jnp.concatenate([cot_ref[at, :], tail.astype(bf16)], axis=0))
        cot_own[at, :] = ordered[GROUPS : GROUPS + clon].astype(bf16)
        return carry

    reorder(0, north_ref[...])
    reorder(clat + 1, south_ref[...])
    used = (clat + 2) * wide
    cot_ext[used:, :] = jnp.zeros((cot_ext.shape[0] - used, width), bf16)
    lax.fori_loop(0, clat, matmul, 0)
    puts[1].start()

    def conv(i, carry):
        for n in range(width // LANES):
            cols = slice(n * LANES, (n + 1) * LANES)
            for c in range(0, clon, CHUNK):
                at = pl.ds(pl.multiple_of(i * clon + c, 16), CHUNK)
                out = cot_own[at, cols].astype(f32)
                for a in range(3):
                    g = gm_ref[n, i + 2 - a, c : c + CHUNK + 2 * GROUPS, :]
                    for b in range(3):
                        k = 3 * a + b
                        first = GROUPS * (2 - b)
                        out = out + wd_ref[k : k + 1, cols] * g[first : first + CHUNK]
                gg_ref[at, cols] = out.astype(bf16)
        return carry

    lax.fori_loop(0, clat, conv, 0)
    puts[0].start()

    def transpose(k, carry):
        at = pl.ds(pl.multiple_of(k * LANES, LANES), LANES)
        cott_ref[:, at] = cot_ext[at, :].T
        return carry

    lax.fori_loop(0, cot_ext.shape[0] // LANES, transpose, 0)
    puts[2].start()
    for put in puts:
        put.wait()


def grid_grad(cot, sides, w_point, w_depth, clat, clon, wide):
    width = w_point.shape[0]
    ext_rows = round_up((clat + 2) * wide, LANES)
    outs = (
        jax.ShapeDtypeStruct((width, ext_rows), bf16),
        jax.ShapeDtypeStruct((width // LANES, clat + 2, wide, LANES), f32),
        jax.ShapeDtypeStruct((clat * clon, width), bf16),
    )
    return pl.pallas_call(
        functools.partial(grid_grad_kernel, clat, clon, wide),
        out_shape=outs,
        in_specs=[vmem()] * 7,
        out_specs=(anywhere(),) * 3,
        scratch_shapes=[pltpu.VMEM(x.shape, x.dtype) for x in outs]
        + [pltpu.VMEM((ext_rows, width), bf16), pltpu.VMEM((clat * clon, width), bf16)]
        + [pltpu.VMEM((clat, width), f32)] * 2
        + [pltpu.SemaphoreType.DMA((3,))],
        compiler_params=params(58),
        cost_estimate=cost(10),
        name="grid_grad",
    )(cot, *sides, w_point, w_depth)


def write_halves(core, total, start, mine_ref, other_ref, first=0, size=None):
    size = total.shape[0] if size is None else size
    half = total.shape[1] // 2
    for ref, base in ((mine_ref, core * half), (other_ref, (1 - core) * half)):
        for n in range(half // LANES):
            cols = pl.ds(pl.multiple_of(base + n * LANES, LANES), LANES)
            ref[n, start : start + size, :] = total[first : first + size, cols].astype(bf16)


def clear_tail(start, *refs):
    for ref in refs:
        unused = ref.shape[1] - start
        if unused:
            ref[:, start:, :] = jnp.zeros((ref.shape[0], unused, LANES), bf16)


def start_loads(sources, targets, sems):
    loads = [
        pltpu.make_async_copy(source, target, sems.at[i])
        for i, (source, target) in enumerate(zip(sources, targets))
    ]
    for load in loads:
        load.start()
    return loads


def encode_kernel(
    spec, clon, ids_ref, rows_ref, wit_hbm, wot_hbm, gg_hbm, wo_hbm,
    emb_ref, mine_ref, other_ref, mine_rest, other_rest,
    wit_ref, wot_ref, gg_ref, wo_ref, gi, gi_out, go, sems,
):
    loads = start_loads((wit_hbm, wot_hbm, gg_hbm, wo_hbm), (wit_ref, wot_ref, gg_ref, wo_ref), sems)
    core = ids_ref[0]
    slots, spec_wide = rows_ref.shape
    cells, width = gg_ref.shape
    step = min(512, slots)

    for t in range(slots // step):
        at = slice(t * step, (t + 1) * step)
        rows = rows_ref[at, :]
        line = rows[:, spec : spec + 1].astype(f32).astype(i32)
        column = rows[:, spec + 1 : spec + 2].astype(f32).astype(i32)
        hits = one_hot(line * clon + place_of(column, clon // GROUPS), cells)
        if t == 0:
            loads[0].wait()
        preact = dot(wit_ref[...], rows, (1, 1))
        sig = 1.0 / (1.0 + jnp.exp(-preact))
        hidden = (preact * sig).astype(bf16)
        if t == 0:
            loads[1].wait()
        emb_ref[:, at] = dot(wot_ref[...], hidden).astype(bf16)
        if t == 0:
            loads[2].wait()
        g_emb = dot(hits, gg_ref[...]).astype(bf16)
        g_out = dot(hidden, g_emb)
        if t == 0:
            loads[3].wait()
        g_hid = dot(wo_ref[...], g_emb, (1, 1))
        g_pre = (g_hid * (sig * (1.0 + preact * (1.0 - sig)))).astype(bf16)
        g_in = dot(g_pre, rows)
        if t == 0:
            go[...] = g_out
            gi[...] = g_in
        else:
            go[...] += g_out
            gi[...] += g_in

    gi_out[...] = gi[...].T
    head = spec_wide - LANES
    write_halves(core, go, 0, mine_ref, other_ref)
    write_halves(core, gi_out, width, mine_ref, other_ref, 0, head)
    write_halves(core, gi_out, 0, mine_rest, other_rest, head, mine_rest.shape[1])
    clear_tail(width + head, mine_ref, other_ref)


def encode(ids, rows, weights, spec, clon, out_rows, rest_rows):
    slots, spec_wide = rows.shape
    width = weights[-1].shape[0]
    half = jax.ShapeDtypeStruct((width // LANES // 2, out_rows, LANES), bf16)
    rest = jax.ShapeDtypeStruct((width // LANES // 2, rest_rows, LANES), bf16)
    return pl.pallas_call(
        functools.partial(encode_kernel, spec, clon),
        out_shape=(jax.ShapeDtypeStruct((width, slots), bf16), half, half, rest, rest),
        in_specs=[smem(), vmem()] + [anywhere()] * len(weights),
        out_specs=(vmem(),) * 5,
        scratch_shapes=[pltpu.VMEM(x.shape, x.dtype) for x in weights]
        + [
            pltpu.VMEM((width, spec_wide), f32),
            pltpu.VMEM((spec_wide, width), f32),
            pltpu.VMEM((width, width), f32),
            pltpu.SemaphoreType.DMA((len(weights),)),
        ],
        compiler_params=params(48),
        cost_estimate=cost(10),
        name="encode",
    )(ids, rows, *weights)


def bins_kernel(spec, clat, clon, wide, rows_ref, emb_ref, wide_ref, grid_hbm, grid_ref, sem):
    slots, spec_wide = rows_ref.shape
    width = emb_ref.shape[0]
    blocks = width // LANES
    last = rows_ref[:, spec_wide - LANES :]
    col = spec - (spec_wide - LANES)
    lane = lax.broadcasted_iota(i32, (16, LANES), 1)
    pick = jnp.where(lane == col, float(clon), jnp.where(lane == col + 1, 1.0, 0.0)).astype(bf16)
    cell = dot(pick, last, (1, 1))[0:1, :].astype(i32)
    lines = 4
    place = lax.broadcasted_iota(i32, (wide, 1), 0)
    column = column_of(place, clon // GROUPS) - 1
    inside = (column >= 0) & (column < clon)
    wanted = [jnp.where(inside, column + k * clon, -clat * clon) for k in range(lines)]
    wanted = jnp.concatenate(wanted, axis=0)
    empty = jnp.zeros((blocks, 2, wide, LANES), f32)
    wide_ref[:, 0:2] = empty
    wide_ref[:, clat + 2 :] = empty

    def body(t, carry):
        hits = (cell == wanted + t * (lines * clon)).astype(f32).astype(bf16)
        grid = dot(hits, emb_ref[...], (1, 1)).astype(bf16).astype(f32)
        for k in range(lines):
            line = grid[k * wide : (k + 1) * wide]
            for n in range(blocks):
                wide_ref[n, t * lines + k + 2] = line[:, n * LANES : (n + 1) * LANES]
            at = pl.ds(pl.multiple_of((t * lines + k) * clon, 16), clon)
            grid_ref[at, :] = line[GROUPS : GROUPS + clon].astype(bf16)
        return carry

    lax.fori_loop(0, clat // lines, body, 0)
    put = pltpu.make_async_copy(grid_ref, grid_hbm, sem)
    put.start()
    put.wait()


def bins(rows, emb, spec, clat, clon, wide):
    width = emb.shape[0]
    grid = jax.ShapeDtypeStruct((clat * clon, width), bf16)
    wide_grid = jax.ShapeDtypeStruct((width // LANES, clat + 4, wide, LANES), f32)
    return pl.pallas_call(
        functools.partial(bins_kernel, spec, clat, clon, wide),
        out_shape=(wide_grid, grid),
        in_specs=[vmem()] * 2,
        out_specs=(vmem(), anywhere()),
        scratch_shapes=[pltpu.VMEM(grid.shape, bf16), pltpu.SemaphoreType.DMA],
        compiler_params=params(12),
        cost_estimate=cost(4),
        name="bins",
    )(rows, emb)


def mix_kernel(
    clat, clon, wide, grid_ref, wd_ref, gm_ref, after_ref,
    mix_ref, gd_ref, mix_hbm, east_out, west_out, east_ref, west_ref, gd, sem,
):
    width = wd_ref.shape[1]
    blocks = width // LANES
    put = pltpu.make_async_copy(mix_ref, mix_hbm, sem)
    gd[...] = jnp.zeros_like(gd)
    used = (clat + 2) * wide
    mix_ref[used:, :] = jnp.zeros((mix_ref.shape[0] - used, width), bf16)
    group = lax.broadcasted_iota(i32, (GROUPS, LANES), 0)

    def conv(e, carry):
        for n in range(blocks):
            cols = slice(n * LANES, (n + 1) * LANES)
            weights = [wd_ref[k : k + 1, cols] for k in range(9)]
            taps = [gd[8 * k : 8 * k + 8, cols] for k in range(9)]
            for c in range(0, clon, CHUNK):
                grads = gm_ref[n, e, c : c + CHUNK + 2 * GROUPS, :]
                mixed = None
                for a in range(3):
                    cells = grid_ref[n, e + a, c : c + CHUNK + 2 * GROUPS, :]
                    middle = cells[GROUPS : GROUPS + CHUNK]
                    for b in range(3):
                        k = 3 * a + b
                        term = weights[k] * cells[GROUPS * b : GROUPS * b + CHUNK]
                        mixed = term if mixed is None else mixed + term
                        first = GROUPS * (2 - b)
                        part = (grads[first : first + CHUNK] * middle).reshape(CHUNK // 8, 8, LANES)
                        taps[k] = taps[k] + jnp.sum(part, axis=0)
                out_at = pl.ds(pl.multiple_of(e * wide + c, 16), CHUNK)
                mix_ref[out_at, cols] = mixed.astype(bf16)
            for k in range(9):
                gd[8 * k : 8 * k + 8, cols] = taps[k]
            ends = []
            for b, at, valid in ((0, clon, GROUPS - 1), (2, GROUPS, 0)):
                end = None
                for a in range(3):
                    term = weights[3 * a + b] * grid_ref[n, e + a, at : at + GROUPS, :]
                    end = term if end is None else end + term
                ends.append(jnp.where(group == valid, end, 0.0))
            east_ref[e, :, cols] = ends[0]
            west_ref[e, :, cols] = ends[1]
            out_at = pl.ds(pl.multiple_of(e * wide + clon, 16), wide - clon)
            mix_ref[out_at, cols] = jnp.concatenate(ends, axis=0).astype(bf16)
        return carry

    lax.fori_loop(0, clat + 2, conv, 0)
    put.start()
    east_out[...] = east_ref[:, GROUPS - 1, :]
    west_out[...] = west_ref[:, 0, :]
    taps = [jnp.sum(gd[8 * k : 8 * k + 8, :], axis=0, keepdims=True) for k in range(9)]
    gd_ref[...] = jnp.concatenate(taps + [jnp.zeros((7, width), f32)], axis=0)
    put.wait()


def mix(grid, w_depth, g_mixed, after, clat, clon, wide):
    width = w_depth.shape[1]
    column = jax.ShapeDtypeStruct((clat + 2, width), f32)
    ext = jax.ShapeDtypeStruct((round_up((clat + 2) * wide, LANES), width), bf16)
    return pl.pallas_call(
        functools.partial(mix_kernel, clat, clon, wide),
        out_shape=(ext, jax.ShapeDtypeStruct((16, width), f32), ext, column, column),
        in_specs=[vmem()] * 3 + [anywhere()],
        out_specs=(vmem(),) * 2 + (anywhere(),) + (vmem(),) * 2,
        scratch_shapes=[pltpu.VMEM((clat + 2, GROUPS, width), f32)] * 2
        + [pltpu.VMEM((72, width), f32), pltpu.SemaphoreType.DMA],
        compiler_params=params(8),
        cost_estimate=cost(8),
        name="mix",
    )(grid, w_depth, g_mixed, after)


def point_kernel(
    ids_ref, cott_ref, mix_ref, gd_ref, mine_rest, other_rest, after_ref, mine_ref, other_ref, gp
):
    core = ids_ref[0]
    width = mix_ref.shape[1]
    rest = mine_rest.shape[1]
    gp[...] = dot(cott_ref[...], mix_ref[...]).T
    write_halves(core, gp, 0, mine_ref, other_ref)
    mine_ref[:, width : width + rest, :] = mine_rest[...]
    other_ref[:, width : width + rest, :] = other_rest[...]
    write_halves(core, gd_ref, width + rest, mine_ref, other_ref, 0, 16)
    clear_tail(width + rest + 16, mine_ref, other_ref)


def point(ids, cot_t, mix_ext, grad_depth, rest, after, out_rows):
    width = mix_ext.shape[1]
    half = jax.ShapeDtypeStruct((width // LANES // 2, out_rows, LANES), bf16)
    return pl.pallas_call(
        point_kernel,
        out_shape=(half, half),
        in_specs=[smem()] + [vmem()] * 5 + [anywhere()],
        out_specs=(vmem(),) * 2,
        scratch_shapes=[pltpu.VMEM((width, width), f32)],
        compiler_params=params(12),
        cost_estimate=cost(3),
        name="point",
    )(ids, cot_t, mix_ext, grad_depth, *rest, after)


def latent_kernel(
    clat, clon, wide, grid_ref, mix_ref, top_ref, bottom_ref, left_ref, right_ref, wp_ref, out_ref
):
    width = wp_ref.shape[0]
    w_point = wp_ref[...]
    line = lax.broadcasted_iota(i32, (clon, width), 0)
    column = lax.broadcasted_iota(i32, (clon, 1), 0)
    natural_order = one_hot(place_of(column, clon // GROUPS), clon)

    def body(i, carry):
        at = pl.ds(pl.multiple_of(i * clon, 16), clon)
        mixed = mix_ref[pl.ds(pl.multiple_of((i + 1) * wide, 16), clon), :].astype(f32)
        mixed = mixed + (i == 0).astype(f32) * top_ref[...].astype(f32)
        mixed = mixed + (i == clat - 1).astype(f32) * bottom_ref[...].astype(f32)
        mixed = mixed + jnp.where(
            line == 0, left_ref[pl.ds(i + 1, 1), :], jnp.where(line == clon - 1, right_ref[pl.ds(i + 1, 1), :], 0.0)
        )
        out = grid_ref[at, :].astype(f32) + dot(mixed.astype(bf16), w_point)
        out_ref[at, :] = dot(natural_order, out.astype(bf16)).astype(bf16)
        return carry

    lax.fori_loop(0, clat, body, 0)


def finish_latent(grid, mix_ext, sides, w_point, clat, clon, wide):
    return pl.pallas_call(
        functools.partial(latent_kernel, clat, clon, wide),
        out_shape=jax.ShapeDtypeStruct(grid.shape, bf16),
        in_specs=[vmem()] * 7,
        out_specs=vmem(),
        compiler_params=params(6),
        cost_estimate=cost(5),
        name="latent",
    )(grid, mix_ext, *sides, w_point)


def split_kernel(ids_ref, mine_ref, got_ref, keep_ref, send_ref):
    x = ids_ref[1]
    for ref, i in ((keep_ref, x), (send_ref, 1 - x)):
        at = pl.ds(i, 1)
        ref[...] = (mine_ref[at].astype(f32) + got_ref[at].astype(f32))[0].astype(bf16)


def split(ids, mine, got):
    half = jax.ShapeDtypeStruct(mine.shape[1:], bf16)
    return pl.pallas_call(
        split_kernel,
        out_shape=(half, half),
        in_specs=[smem()] + [vmem()] * 2,
        out_specs=(vmem(),) * 2,
        compiler_params=params(8),
        cost_estimate=cost(1),
        name="split",
    )(ids, mine, got)


def merge_kernel(a_keep, a_got, b_keep, b_got, *refs):
    out_ref = refs[-1]
    count = out_ref.shape[0]
    start = 0
    for keep, got in ((a_keep, a_got), (b_keep, b_got)):
        total = (keep[...].astype(f32) + got[...].astype(f32)).astype(bf16)
        size = total.shape[0] // count
        out_ref[:, start : start + size, :] = total.reshape(count, size, LANES)
        start += size


def merge(a_keep, a_got, b_keep, b_got, count, *after):
    rows = (a_keep.shape[0] + b_keep.shape[0]) // count
    return pl.pallas_call(
        merge_kernel,
        out_shape=jax.ShapeDtypeStruct((count, rows, LANES), bf16),
        in_specs=[vmem()] * 4 + [anywhere()] * len(after),
        out_specs=vmem(),
        compiler_params=params(8),
        cost_estimate=cost(1),
        name="merge",
    )(a_keep, a_got, b_keep, b_got, *after)


def totals_kernel(parts_ref, *refs):
    out_ref = refs[-1]
    total = jnp.sum(parts_ref[...].astype(f32), axis=0).astype(bf16)
    out_ref[...] = jnp.broadcast_to(total[None], out_ref.shape)


def totals(parts, chips, *after):
    return pl.pallas_call(
        totals_kernel,
        out_shape=jax.ShapeDtypeStruct((chips,) + parts.shape[1:], bf16),
        in_specs=[vmem()] + [anywhere()] * len(after),
        out_specs=vmem(),
        compiler_params=params(8),
        cost_estimate=cost(1),
        name="totals",
    )(parts, *after)


def unpack_kernel(
    rows_a, rest, obs_scale, cell_scale, ids_ref, own_ref, sibling_ref, gi_ref, go_ref, gp_ref, gd_ref
):
    spec, width = gi_ref.shape
    chips = own_ref.shape[0]
    count = width // (2 * LANES)
    per = chips // count
    core = ids_ref[0]
    cut = rows_a // per
    head = spec - spec % LANES
    for ref, half in ((own_ref, core), (sibling_ref, 1 - core)):
        for n in range(count):
            cols = pl.ds(pl.multiple_of((half * count + n) * LANES, LANES), LANES)
            block = ref[n * per : (n + 1) * per].astype(f32)
            a = block[:, :cut].reshape(rows_a, LANES)
            b = block[:, cut:].reshape(per * (block.shape[1] - cut), LANES)
            go_ref[:, cols] = a[:width] * obs_scale
            gi_ref[:head, cols] = a[width : width + head] * obs_scale
            gp_ref[:, cols] = b[:width] * cell_scale
            gi_ref[head:, cols] = b[width : width + spec - head] * obs_scale
            gd_ref[:, cols] = b[width + rest : width + rest + gd_ref.shape[0]] * cell_scale


def unpack(ids, own, sibling, spec, width, rows_a, rest, obs_scale, cell_scale):
    return pl.pallas_call(
        functools.partial(unpack_kernel, rows_a, rest, obs_scale, cell_scale),
        out_shape=tuple(
            jax.ShapeDtypeStruct((rows, width), f32) for rows in (spec, width, width, 9)
        ),
        in_specs=[smem()] + [vmem()] * 2,
        out_specs=(vmem(),) * 4,
        compiler_params=params(8),
        cost_estimate=cost(3),
        name="unpack",
    )(ids, own, sibling)


def neighbours(axes, periodic):
    count = lax.axis_size(axes)
    up = [(i, i + 1) for i in range(count - 1)]
    if periodic:
        up.append((count - 1, 0))
    return up, [(t, s) for s, t in up]


LAT = ("x", "core")
CHIPS = ("x", "lon")


SWAP = [(0, 1), (1, 0)]


def spread(values, axes):
    return lax.all_to_all(values, axes, split_axis=0, concat_axis=0, tiled=True)


def on_device(spectra, owner, cell, w_in, w_out, w_point, w_depth, cotangent):
    tiles = lax.axis_size(LAT) * lax.axis_size("lon")
    rows_here, spec = spectra.shape
    cap = max(2, 2 * rows_here // tiles)
    clat, clon, width = cotangent.shape
    cells = clat * clon
    wide = clon + 16
    spec_wide = round_up(spec + 2, LANES)
    ids = jnp.stack([lax.axis_index("core"), lax.axis_index("x")])
    east_way, west_way = neighbours("lon", True)
    south_way, north_way = neighbours(LAT, False)

    from_west = lax.ppermute(cotangent[:, -1], "lon", east_way)
    from_east = lax.ppermute(cotangent[:, 0], "lon", west_way)

    places = jnp.concatenate([owner.reshape(1, rows_here), cell.reshape(1, rows_here)], axis=0)
    outgoing = route(places, spectra.T, tiles, cap, clon, spec_wide)
    outgoing, from_west, from_east, w_in, w_out = lax.optimization_barrier(
        (outgoing, from_west, from_east, w_in, w_out)
    )
    arrived = lax.all_to_all(
        outgoing.reshape(tiles, cap, spec_wide), ("x", "core", "lon"), 0, 0, tiled=True
    ).reshape(tiles * cap, spec_wide)

    fill = jnp.zeros((wide - clon - 2, width), bf16)

    def halo_row(i):
        return jnp.concatenate([cotangent[i], from_east[i, None], fill, from_west[i, None]], axis=0)

    from_north = lax.ppermute(halo_row(clat - 1), LAT, south_way)
    from_south = lax.ppermute(halo_row(0), LAT, north_way)
    cot_t, g_mixed, g_grid = grid_grad(
        cotangent.reshape(cells, width),
        (from_east, from_west, from_north, from_south),
        w_point, w_depth, clat, clon, wide,
    )
    w_in_t = jnp.pad(w_in.T, ((0, 0), (0, spec_wide - spec)))

    chips, pairs = lax.axis_size(CHIPS), lax.axis_size("x") == 2
    align = 16 * tiles * LANES // width
    head = spec - spec % LANES
    rest = round_up(spec - head, 16)
    rows_a = round_up(width + head, align)
    rows_b = round_up(width + rest + 16, align)
    emb, mine_a, other_a, *rest_halves = encode(
        ids, arrived, (w_in_t, w_out.T, g_grid, w_out), spec, clon, rows_a, rest
    )
    got_a = lax.ppermute(other_a, "core", SWAP)
    grid_here, grid = bins(arrived, emb, spec, clat, clon, wide)
    keep_a, send_a = split(ids, mine_a, got_a) if pairs else (mine_a, got_a)

    mix_here, grad_depth, mix_ext, east, west = mix(
        grid_here, w_depth, g_mixed, keep_a, clat, clon, wide
    )
    got_a = lax.ppermute(send_a, "x", SWAP) if pairs else send_a
    mine_b, other_b = point(ids, cot_t, mix_here, grad_depth, rest_halves, got_a, rows_b)
    got_b = lax.ppermute(other_b, "core", SWAP)
    if pairs:
        keep_b, send_b = split(ids, mine_b, got_b)
        send_b, east, west = lax.optimization_barrier((send_b, east, west))
        got_b = lax.ppermute(send_b, "x", SWAP)

    left = lax.ppermute(east, "lon", east_way)
    right = lax.ppermute(west, "lon", west_way)
    if pairs:
        summed = merge(keep_a, got_a, keep_b, got_b, lax.axis_size("lon"), left, right)
    else:
        sums = [
            (mine.astype(f32) + got.astype(f32)).astype(bf16).reshape(chips, -1, LANES)
            for mine, got in ((keep_a, send_a), (mine_b, got_b))
        ]
        summed = jnp.concatenate(sums, axis=1)
    summed, left, right, mix_ext = lax.optimization_barrier((summed, left, right, mix_ext))
    parts = spread(summed, "lon" if pairs else CHIPS)
    line = lax.broadcasted_iota(i32, (clon, width), 0)

    def edge_row(e):
        row = mix_ext[e * wide : e * wide + clon].astype(f32)
        sides = jnp.where(line == 0, left[e], jnp.where(line == clon - 1, right[e], 0.0))
        return (row + sides).astype(bf16)

    top = lax.ppermute(edge_row(clat + 1), LAT, south_way)
    bottom = lax.ppermute(edge_row(0), LAT, north_way)
    full = spread(totals(parts, chips, top, bottom), CHIPS)
    latent = finish_latent(grid, mix_ext, (top, bottom, left, right), w_point, clat, clon, wide)

    obs_scale = float((rows_here * tiles) ** -0.5)
    cell_scale = float((cells * tiles) ** -0.5)
    full, latent = lax.optimization_barrier((full, latent))
    sibling = lax.ppermute(full, "core", SWAP)
    grad_in, grad_out, grad_point, grad_depth = unpack(
        ids, full, sibling, spec, width, rows_a, rest, obs_scale, cell_scale
    )
    return latent.reshape(clat, clon, width), grad_in, grad_out, grad_point, grad_depth


def solution(mesh):
    lat, lon = mesh.devices.shape
    fine = Mesh(mesh.devices.reshape(lat // 2, 2, lon), ("x", "core", "lon"))
    everyone = P(("x", "core", "lon"))
    field = P(LAT, "lon", None)
    in_specs = (everyone, everyone, everyone, P(), P(), P(), P(), field)
    out_specs = (field, P(), P(), P(), P())
    return jax.shard_map(
        on_device, mesh=fine, in_specs=in_specs, out_specs=out_specs, check_vma=False
    )
```

```python
import functools

import jax
import jax.numpy as jnp
from jax import lax
from jax.experimental import pallas as pl
from jax.experimental.pallas import tpu as pltpu
from jax.sharding import Mesh
from jax.sharding import PartitionSpec as P

LANES = 128
bf16 = jnp.bfloat16
f32 = jnp.float32
i32 = jnp.int32


def params(mib):
    return pltpu.CompilerParams(vmem_limit_bytes=mib * 1024 * 1024)


def round_up(n, m):
    return -(-n // m) * m


def dot(a, b, dims=(1, 0)):
    return lax.dot_general(
        a, b, (((dims[0],), (dims[1],)), ((), ())), preferred_element_type=f32
    )


def cost(us):
    return pl.CostEstimate(flops=us * 1153500000, bytes_accessed=0, transcendentals=0)


def smem():
    return pl.BlockSpec(memory_space=pltpu.SMEM)


def anywhere():
    return pl.BlockSpec(memory_space=pl.ANY)


def vmem():
    return pl.BlockSpec(memory_space=pltpu.VMEM)


def route_kernel(tiles, cap, clon, places_ref, rows_ref, out_ref):
    spec, n = rows_ref.shape
    head = out_ref.shape[1] - LANES
    owner = places_ref[0:1, :]
    hits = owner == lax.broadcasted_iota(i32, (tiles, n), 0)
    above = lax.broadcasted_iota(i32, (n, n), 0) < lax.broadcasted_iota(i32, (n, n), 1)
    count = dot(hits.astype(f32).astype(bf16), above.astype(f32).astype(bf16))
    rank = jnp.sum(jnp.where(hits, count, 0.0), axis=0, keepdims=True)
    slot = owner * cap + rank.astype(i32)
    cell = places_ref[1:2, :]
    line = lax.broadcasted_iota(i32, (LANES - (spec - head), n), 0)
    high = cell // clon
    spots = jnp.where(line == 0, high, jnp.where(line == 1, cell - high * clon, 0)).astype(f32)
    last = jnp.concatenate([rows_ref[head:, :].astype(f32), spots], axis=0).astype(bf16)
    first = rows_ref[:head, :]
    step = min(256, tiles * cap)

    def body(t, carry):
        base = t * step
        place = lax.broadcasted_iota(i32, (step, n), 0) + base
        pick = (slot == place).astype(f32).astype(bf16)
        at = pl.ds(pl.multiple_of(base, step), step)
        out_ref[at, :head] = dot(pick, first, (1, 1)).astype(bf16)
        out_ref[at, head:] = dot(pick, last, (1, 1)).astype(bf16)
        return carry

    lax.fori_loop(0, tiles * cap // step, body, 0)


def route(places, rows, tiles, cap, clon, spec_wide):
    return pl.pallas_call(
        functools.partial(route_kernel, tiles, cap, clon),
        out_shape=jax.ShapeDtypeStruct((tiles * cap, spec_wide), bf16),
        in_specs=[vmem()] * 2,
        out_specs=vmem(),
        compiler_params=params(12),
        cost_estimate=cost(3),
        name="route",
    )(places, rows)


GROUPS = 8
CHUNK = 8 * GROUPS


def column_of(place, per):
    return per * (place % GROUPS) + place // GROUPS


def place_of(column, per):
    return GROUPS * (column % per) + column // per


def one_hot(wanted, count):
    hit = wanted == lax.broadcasted_iota(i32, (wanted.shape[0], count), 1)
    return hit.astype(f32).astype(bf16)


def grid_grad_kernel(
    clat, clon, wide, cot_ref, east_ref, west_ref, north_ref, south_ref, wp_ref, wd_ref,
    cott_hbm, gm_hbm, gg_hbm, cott_ref, gm_ref, gg_ref, cot_ext, cot_own, east, west, sems,
):
    width = wp_ref.shape[0]
    per = clon // GROUPS
    w_point = wp_ref[...]
    east[...] = east_ref[...].astype(f32)
    west[...] = west_ref[...].astype(f32)
    line = lax.broadcasted_iota(i32, (wide - clon, width), 0)
    place = lax.broadcasted_iota(i32, (wide, 1), 0)
    column = column_of(place, per) - 1
    spread_order = one_hot(jnp.where(column < 0, wide - 1, column), wide)
    ends = jnp.where(place == clon + GROUPS - 1, clon, jnp.where(place == clon + GROUPS, wide - 1, -1))
    point_order = one_hot(jnp.where(place < clon, column_of(place, per), ends), wide)
    puts = [
        pltpu.make_async_copy(source, target, sems.at[i])
        for i, (source, target) in enumerate(
            ((gg_ref, gg_hbm), (gm_ref, gm_hbm), (cott_ref, cott_hbm))
        )
    ]

    def reorder(e, rows):
        ordered = dot(spread_order, rows)
        g = dot(ordered.astype(bf16), w_point, (1, 1)).astype(bf16).astype(f32)
        for n in range(width // LANES):
            gm_ref[n, e] = g[:, n * LANES : (n + 1) * LANES]
        cot_ext[pl.ds(pl.multiple_of(e * wide, 16), wide), :] = dot(point_order, rows).astype(bf16)
        return ordered

    def matmul(i, carry):
        at = pl.ds(pl.multiple_of(i * clon, 16), clon)
        tail = jnp.where(
            line == 0, east[pl.ds(i, 1), :], jnp.where(line == wide - clon - 1, west[pl.ds(i, 1), :], 0.0)
        )
        ordered = reorder(i + 1, jnp.concatenate([cot_ref[at, :], tail.astype(bf16)], axis=0))
        cot_own[at, :] = ordered[GROUPS : GROUPS + clon].astype(bf16)
        return carry

    reorder(0, north_ref[...])
    reorder(clat + 1, south_ref[...])
    used = (clat + 2) * wide
    cot_ext[used:, :] = jnp.zeros((cot_ext.shape[0] - used, width), bf16)
    lax.fori_loop(0, clat, matmul, 0)
    puts[1].start()

    def conv(i, carry):
        for n in range(width // LANES):
            cols = slice(n * LANES, (n + 1) * LANES)
            for c in range(0, clon, CHUNK):
                at = pl.ds(pl.multiple_of(i * clon + c, 16), CHUNK)
                out = cot_own[at, cols].astype(f32)
                for a in range(3):
                    g = gm_ref[n, i + 2 - a, c : c + CHUNK + 2 * GROUPS, :]
                    for b in range(3):
                        k = 3 * a + b
                        first = GROUPS * (2 - b)
                        out = out + wd_ref[k : k + 1, cols] * g[first : first + CHUNK]
                gg_ref[at, cols] = out.astype(bf16)
        return carry

    lax.fori_loop(0, clat, conv, 0)
    puts[0].start()

    def transpose(k, carry):
        at = pl.ds(pl.multiple_of(k * LANES, LANES), LANES)
        cott_ref[:, at] = cot_ext[at, :].T
        return carry

    lax.fori_loop(0, cot_ext.shape[0] // LANES, transpose, 0)
    puts[2].start()
    for put in puts:
        put.wait()


def grid_grad(cot, sides, w_point, w_depth, clat, clon, wide):
    width = w_point.shape[0]
    ext_rows = round_up((clat + 2) * wide, LANES)
    outs = (
        jax.ShapeDtypeStruct((width, ext_rows), bf16),
        jax.ShapeDtypeStruct((width // LANES, clat + 2, wide, LANES), f32),
        jax.ShapeDtypeStruct((clat * clon, width), bf16),
    )
    return pl.pallas_call(
        functools.partial(grid_grad_kernel, clat, clon, wide),
        out_shape=outs,
        in_specs=[vmem()] * 7,
        out_specs=(anywhere(),) * 3,
        scratch_shapes=[pltpu.VMEM(x.shape, x.dtype) for x in outs]
        + [pltpu.VMEM((ext_rows, width), bf16), pltpu.VMEM((clat * clon, width), bf16)]
        + [pltpu.VMEM((clat, width), f32)] * 2
        + [pltpu.SemaphoreType.DMA((3,))],
        compiler_params=params(58),
        cost_estimate=cost(10),
        name="grid_grad",
    )(cot, *sides, w_point, w_depth)


def write_halves(core, total, start, mine_ref, other_ref, first=0, size=None):
    size = total.shape[0] if size is None else size
    half = total.shape[1] // 2
    for ref, base in ((mine_ref, core * half), (other_ref, (1 - core) * half)):
        for n in range(half // LANES):
            cols = pl.ds(pl.multiple_of(base + n * LANES, LANES), LANES)
            ref[n, start : start + size, :] = total[first : first + size, cols].astype(bf16)


def clear_tail(start, *refs):
    for ref in refs:
        unused = ref.shape[1] - start
        if unused:
            ref[:, start:, :] = jnp.zeros((ref.shape[0], unused, LANES), bf16)


def start_loads(sources, targets, sems):
    loads = [
        pltpu.make_async_copy(source, target, sems.at[i])
        for i, (source, target) in enumerate(zip(sources, targets))
    ]
    for load in loads:
        load.start()
    return loads


def encode_kernel(
    spec, clon, ids_ref, rows_ref, wit_hbm, wot_hbm, gg_hbm, wo_hbm,
    emb_hbm, cell_ref, mine_ref, other_ref, mine_rest, other_rest,
    wit_ref, wot_ref, gg_ref, wo_ref, emb_ref, gi, gi_out, go, sems,
):
    loads = start_loads((wit_hbm, wot_hbm, gg_hbm, wo_hbm), (wit_ref, wot_ref, gg_ref, wo_ref), sems)
    core = ids_ref[0]
    slots, spec_wide = rows_ref.shape
    cells, width = gg_ref.shape
    step = min(512, slots)
    put_emb = pltpu.make_async_copy(emb_ref, emb_hbm, sems.at[len(loads)])
    last = rows_ref[:, spec_wide - LANES :]
    col = spec - (spec_wide - LANES)
    lane = lax.broadcasted_iota(i32, (16, LANES), 1)
    pick = jnp.where(lane == col, float(clon), jnp.where(lane == col + 1, 1.0, 0.0)).astype(bf16)
    cell_ref[...] = dot(pick, last, (1, 1))[0:8, :].astype(i32)

    for t in range(slots // step):
        at = slice(t * step, (t + 1) * step)
        rows = rows_ref[at, :]
        line = rows[:, spec : spec + 1].astype(f32).astype(i32)
        column = rows[:, spec + 1 : spec + 2].astype(f32).astype(i32)
        hits = one_hot(line * clon + place_of(column, clon // GROUPS), cells)
        if t == 0:
            loads[0].wait()
        preact = dot(wit_ref[...], rows, (1, 1))
        sig = 1.0 / (1.0 + jnp.exp(-preact))
        hidden = (preact * sig).astype(bf16)
        if t == 0:
            loads[1].wait()
        emb_ref[:, at] = dot(wot_ref[...], hidden).astype(bf16)
        if t == slots // step - 1:
            put_emb.start()
        if t == 0:
            loads[2].wait()
        g_emb = dot(hits, gg_ref[...]).astype(bf16)
        g_out = dot(hidden, g_emb)
        if t == 0:
            loads[3].wait()
        g_hid = dot(wo_ref[...], g_emb, (1, 1))
        g_pre = (g_hid * (sig * (1.0 + preact * (1.0 - sig)))).astype(bf16)
        g_in = dot(g_pre, rows)
        if t == 0:
            go[...] = g_out
            gi[...] = g_in
        else:
            go[...] += g_out
            gi[...] += g_in

    gi_out[...] = gi[...].T
    head = spec_wide - LANES
    write_halves(core, go, 0, mine_ref, other_ref)
    write_halves(core, gi_out, width, mine_ref, other_ref, 0, head)
    write_halves(core, gi_out, 0, mine_rest, other_rest, head, mine_rest.shape[1])
    clear_tail(width + head, mine_ref, other_ref)
    put_emb.wait()


def encode(ids, rows, weights, spec, clon, out_rows, rest_rows):
    slots, spec_wide = rows.shape
    width = weights[-1].shape[0]
    half = jax.ShapeDtypeStruct((width // LANES // 2, out_rows, LANES), bf16)
    rest = jax.ShapeDtypeStruct((width // LANES // 2, rest_rows, LANES), bf16)
    return pl.pallas_call(
        functools.partial(encode_kernel, spec, clon),
        out_shape=(
            jax.ShapeDtypeStruct((width, slots), bf16),
            jax.ShapeDtypeStruct((8, slots), i32),
            half,
            half,
            rest,
            rest,
        ),
        in_specs=[smem(), vmem()] + [anywhere()] * len(weights),
        out_specs=(anywhere(),) + (vmem(),) * 5,
        scratch_shapes=[pltpu.VMEM(x.shape, x.dtype) for x in weights]
        + [
            pltpu.VMEM((width, slots), bf16),
            pltpu.VMEM((width, spec_wide), f32),
            pltpu.VMEM((spec_wide, width), f32),
            pltpu.VMEM((width, width), f32),
            pltpu.SemaphoreType.DMA((len(weights) + 1,)),
        ],
        compiler_params=params(48),
        cost_estimate=cost(10),
        name="encode",
    )(ids, rows, *weights)


def bins_kernel(clat, clon, wide, cell_ref, emb_ref, after_ref, wide_ref, grid_hbm, grid_ref, sem):
    width = emb_ref.shape[0]
    blocks = width // LANES
    cell = cell_ref[0:1, :]
    lines = 4
    place = lax.broadcasted_iota(i32, (wide, 1), 0)
    column = column_of(place, clon // GROUPS) - 1
    inside = (column >= 0) & (column < clon)
    wanted = [jnp.where(inside, column + k * clon, -clat * clon) for k in range(lines)]
    wanted = jnp.concatenate(wanted, axis=0)
    empty = jnp.zeros((blocks, 2, wide, LANES), f32)
    wide_ref[:, 0:2] = empty
    wide_ref[:, clat + 2 :] = empty

    def body(t, carry):
        hits = (cell == wanted + t * (lines * clon)).astype(f32).astype(bf16)
        grid = dot(hits, emb_ref[...], (1, 1)).astype(bf16).astype(f32)
        for k in range(lines):
            line = grid[k * wide : (k + 1) * wide]
            for n in range(blocks):
                wide_ref[n, t * lines + k + 2] = line[:, n * LANES : (n + 1) * LANES]
            at = pl.ds(pl.multiple_of((t * lines + k) * clon, 16), clon)
            grid_ref[at, :] = line[GROUPS : GROUPS + clon].astype(bf16)
        return carry

    lax.fori_loop(0, clat // lines, body, 0)
    put = pltpu.make_async_copy(grid_ref, grid_hbm, sem)
    put.start()
    put.wait()


def bins(cell, emb, after, clat, clon, wide):
    width = emb.shape[0]
    grid = jax.ShapeDtypeStruct((clat * clon, width), bf16)
    wide_grid = jax.ShapeDtypeStruct((width // LANES, clat + 4, wide, LANES), f32)
    return pl.pallas_call(
        functools.partial(bins_kernel, clat, clon, wide),
        out_shape=(wide_grid, grid),
        in_specs=[vmem()] * 2 + [anywhere()],
        out_specs=(vmem(), anywhere()),
        scratch_shapes=[pltpu.VMEM(grid.shape, bf16), pltpu.SemaphoreType.DMA],
        compiler_params=params(12),
        cost_estimate=cost(4),
        name="bins",
    )(cell, emb, after)


def mix_kernel(
    clat, clon, wide, grid_ref, wd_ref, gm_ref,
    mix_ref, gd_ref, mix_hbm, east_out, west_out, east_ref, west_ref, gd, sem,
):
    width = wd_ref.shape[1]
    blocks = width // LANES
    put = pltpu.make_async_copy(mix_ref, mix_hbm, sem)
    gd[...] = jnp.zeros_like(gd)
    used = (clat + 2) * wide
    mix_ref[used:, :] = jnp.zeros((mix_ref.shape[0] - used, width), bf16)
    group = lax.broadcasted_iota(i32, (GROUPS, LANES), 0)

    def conv(e, carry):
        for n in range(blocks):
            cols = slice(n * LANES, (n + 1) * LANES)
            weights = [wd_ref[k : k + 1, cols] for k in range(9)]
            taps = [gd[8 * k : 8 * k + 8, cols] for k in range(9)]
            for c in range(0, clon, CHUNK):
                grads = gm_ref[n, e, c : c + CHUNK + 2 * GROUPS, :]
                mixed = None
                for a in range(3):
                    cells = grid_ref[n, e + a, c : c + CHUNK + 2 * GROUPS, :]
                    middle = cells[GROUPS : GROUPS + CHUNK]
                    for b in range(3):
                        k = 3 * a + b
                        term = weights[k] * cells[GROUPS * b : GROUPS * b + CHUNK]
                        mixed = term if mixed is None else mixed + term
                        first = GROUPS * (2 - b)
                        part = (grads[first : first + CHUNK] * middle).reshape(CHUNK // 8, 8, LANES)
                        taps[k] = taps[k] + jnp.sum(part, axis=0)
                out_at = pl.ds(pl.multiple_of(e * wide + c, 16), CHUNK)
                mix_ref[out_at, cols] = mixed.astype(bf16)
            for k in range(9):
                gd[8 * k : 8 * k + 8, cols] = taps[k]
            ends = []
            for b, at, valid in ((0, clon, GROUPS - 1), (2, GROUPS, 0)):
                end = None
                for a in range(3):
                    term = weights[3 * a + b] * grid_ref[n, e + a, at : at + GROUPS, :]
                    end = term if end is None else end + term
                ends.append(jnp.where(group == valid, end, 0.0))
            east_ref[e, :, cols] = ends[0]
            west_ref[e, :, cols] = ends[1]
            out_at = pl.ds(pl.multiple_of(e * wide + clon, 16), wide - clon)
            mix_ref[out_at, cols] = jnp.concatenate(ends, axis=0).astype(bf16)
        return carry

    lax.fori_loop(0, clat + 2, conv, 0)
    put.start()
    east_out[...] = east_ref[:, GROUPS - 1, :]
    west_out[...] = west_ref[:, 0, :]
    taps = [jnp.sum(gd[8 * k : 8 * k + 8, :], axis=0, keepdims=True) for k in range(9)]
    gd_ref[...] = jnp.concatenate(taps + [jnp.zeros((7, width), f32)], axis=0)
    put.wait()


def mix(grid, w_depth, g_mixed, clat, clon, wide):
    width = w_depth.shape[1]
    column = jax.ShapeDtypeStruct((clat + 2, width), f32)
    ext = jax.ShapeDtypeStruct((round_up((clat + 2) * wide, LANES), width), bf16)
    return pl.pallas_call(
        functools.partial(mix_kernel, clat, clon, wide),
        out_shape=(ext, jax.ShapeDtypeStruct((16, width), f32), ext, column, column),
        in_specs=[vmem()] * 3,
        out_specs=(vmem(),) * 2 + (anywhere(),) + (vmem(),) * 2,
        scratch_shapes=[pltpu.VMEM((clat + 2, GROUPS, width), f32)] * 2
        + [pltpu.VMEM((72, width), f32), pltpu.SemaphoreType.DMA],
        compiler_params=params(8),
        cost_estimate=cost(8),
        name="mix",
    )(grid, w_depth, g_mixed)


def point_kernel(
    ids_ref, cott_ref, mix_ref, gd_ref, mine_rest, other_rest, mine_ref, other_ref, gp
):
    core = ids_ref[0]
    width = mix_ref.shape[1]
    rest = mine_rest.shape[1]
    gp[...] = dot(cott_ref[...], mix_ref[...]).T
    write_halves(core, gp, 0, mine_ref, other_ref)
    mine_ref[:, width : width + rest, :] = mine_rest[...]
    other_ref[:, width : width + rest, :] = other_rest[...]
    write_halves(core, gd_ref, width + rest, mine_ref, other_ref, 0, 16)
    clear_tail(width + rest + 16, mine_ref, other_ref)


def point(ids, cot_t, mix_ext, grad_depth, rest, out_rows):
    width = mix_ext.shape[1]
    half = jax.ShapeDtypeStruct((width // LANES // 2, out_rows, LANES), bf16)
    return pl.pallas_call(
        point_kernel,
        out_shape=(half, half),
        in_specs=[smem()] + [vmem()] * 5,
        out_specs=(vmem(),) * 2,
        scratch_shapes=[pltpu.VMEM((width, width), f32)],
        compiler_params=params(12),
        cost_estimate=cost(3),
        name="point",
    )(ids, cot_t, mix_ext, grad_depth, *rest)


def latent_kernel(
    clat, clon, wide, grid_ref, mix_ref, top_ref, bottom_ref, left_ref, right_ref, wp_ref, out_ref
):
    width = wp_ref.shape[0]
    w_point = wp_ref[...]
    line = lax.broadcasted_iota(i32, (clon, width), 0)
    column = lax.broadcasted_iota(i32, (clon, 1), 0)
    natural_order = one_hot(place_of(column, clon // GROUPS), clon)

    def body(i, carry):
        at = pl.ds(pl.multiple_of(i * clon, 16), clon)
        mixed = mix_ref[pl.ds(pl.multiple_of((i + 1) * wide, 16), clon), :].astype(f32)
        mixed = mixed + (i == 0).astype(f32) * top_ref[...].astype(f32)
        mixed = mixed + (i == clat - 1).astype(f32) * bottom_ref[...].astype(f32)
        mixed = mixed + jnp.where(
            line == 0, left_ref[pl.ds(i + 1, 1), :], jnp.where(line == clon - 1, right_ref[pl.ds(i + 1, 1), :], 0.0)
        )
        out = grid_ref[at, :].astype(f32) + dot(mixed.astype(bf16), w_point)
        out_ref[at, :] = dot(natural_order, out.astype(bf16)).astype(bf16)
        return carry

    lax.fori_loop(0, clat, body, 0)


def finish_latent(grid, mix_ext, sides, w_point, clat, clon, wide):
    return pl.pallas_call(
        functools.partial(latent_kernel, clat, clon, wide),
        out_shape=jax.ShapeDtypeStruct(grid.shape, bf16),
        in_specs=[vmem()] * 7,
        out_specs=vmem(),
        compiler_params=params(6),
        cost_estimate=cost(5),
        name="latent",
    )(grid, mix_ext, *sides, w_point)


SWAP = [(0, 1), (1, 0)]


def add_kernel(mine_ref, got_ref, out_ref):
    out_ref[...] = (mine_ref[...].astype(f32) + got_ref[...].astype(f32)).astype(bf16)


def core_sum(mine, other):
    return pl.pallas_call(
        add_kernel,
        out_shape=jax.ShapeDtypeStruct(mine.shape, bf16),
        in_specs=[vmem()] * 2,
        out_specs=vmem(),
        compiler_params=params(8),
        cost_estimate=cost(1),
        name="core_sum",
    )(mine, lax.ppermute(other, "core", SWAP))


def totals_kernel(a_ref, b_ref, *refs):
    out_ref = refs[-1]
    start = 0
    for ref in (a_ref, b_ref):
        size = ref.shape[1]
        total = jnp.sum(ref[...].astype(f32), axis=0).astype(bf16)
        out_ref[:, start : start + size, :] = jnp.broadcast_to(total[None], ref.shape)
        start += size


def totals(parts_a, parts_b, *after):
    chips, rows_a, _ = parts_a.shape
    return pl.pallas_call(
        totals_kernel,
        out_shape=jax.ShapeDtypeStruct((chips, rows_a + parts_b.shape[1], LANES), bf16),
        in_specs=[vmem()] * 2 + [anywhere()] * len(after),
        out_specs=vmem(),
        compiler_params=params(8),
        cost_estimate=cost(1),
        name="totals",
    )(parts_a, parts_b, *after)


def unpack_kernel(
    rows_a, rest, obs_scale, cell_scale, ids_ref, own_ref, sibling_ref, gi_ref, go_ref, gp_ref, gd_ref
):
    spec, width = gi_ref.shape
    chips = own_ref.shape[0]
    count = width // (2 * LANES)
    per = chips // count
    core = ids_ref[0]
    cut = rows_a // per
    head = spec - spec % LANES
    for ref, half in ((own_ref, core), (sibling_ref, 1 - core)):
        for n in range(count):
            cols = pl.ds(pl.multiple_of((half * count + n) * LANES, LANES), LANES)
            block = ref[n * per : (n + 1) * per].astype(f32)
            a = block[:, :cut].reshape(rows_a, LANES)
            b = block[:, cut:].reshape(per * (block.shape[1] - cut), LANES)
            go_ref[:, cols] = a[:width] * obs_scale
            gi_ref[:head, cols] = a[width : width + head] * obs_scale
            gp_ref[:, cols] = b[:width] * cell_scale
            gi_ref[head:, cols] = b[width : width + spec - head] * obs_scale
            gd_ref[:, cols] = b[width + rest : width + rest + gd_ref.shape[0]] * cell_scale


def unpack(ids, own, sibling, spec, width, rows_a, rest, obs_scale, cell_scale):
    return pl.pallas_call(
        functools.partial(unpack_kernel, rows_a, rest, obs_scale, cell_scale),
        out_shape=tuple(
            jax.ShapeDtypeStruct((rows, width), f32) for rows in (spec, width, width, 9)
        ),
        in_specs=[smem()] + [vmem()] * 2,
        out_specs=(vmem(),) * 4,
        compiler_params=params(8),
        cost_estimate=cost(3),
        name="unpack",
    )(ids, own, sibling)


def neighbours(axes, periodic):
    count = lax.axis_size(axes)
    up = [(i, i + 1) for i in range(count - 1)]
    if periodic:
        up.append((count - 1, 0))
    return up, [(t, s) for s, t in up]


LAT = ("x", "core")
CHIPS = ("x", "lon")


def spread(values):
    chips = lax.axis_size(CHIPS)
    values = values.reshape(chips, values.size // (chips * LANES), LANES)
    return lax.all_to_all(values, CHIPS, split_axis=0, concat_axis=0, tiled=True)


def on_device(spectra, owner, cell, w_in, w_out, w_point, w_depth, cotangent):
    tiles = lax.axis_size(LAT) * lax.axis_size("lon")
    rows_here, spec = spectra.shape
    cap = max(2, 2 * rows_here // tiles)
    clat, clon, width = cotangent.shape
    cells = clat * clon
    wide = clon + 16
    spec_wide = round_up(spec + 2, LANES)
    ids = lax.axis_index("core").reshape(1)
    east_way, west_way = neighbours("lon", True)
    south_way, north_way = neighbours(LAT, False)

    from_west = lax.ppermute(cotangent[:, -1], "lon", east_way)
    from_east = lax.ppermute(cotangent[:, 0], "lon", west_way)

    places = jnp.concatenate([owner.reshape(1, rows_here), cell.reshape(1, rows_here)], axis=0)
    outgoing = route(places, spectra.T, tiles, cap, clon, spec_wide)
    outgoing, from_west, from_east, w_in, w_out = lax.optimization_barrier(
        (outgoing, from_west, from_east, w_in, w_out)
    )
    arrived = lax.all_to_all(
        outgoing.reshape(tiles, cap, spec_wide), ("x", "core", "lon"), 0, 0, tiled=True
    ).reshape(tiles * cap, spec_wide)

    fill = jnp.zeros((wide - clon - 2, width), bf16)

    def halo_row(i):
        return jnp.concatenate([cotangent[i], from_east[i, None], fill, from_west[i, None]], axis=0)

    from_north = lax.ppermute(halo_row(clat - 1), LAT, south_way)
    from_south = lax.ppermute(halo_row(0), LAT, north_way)
    cot_t, g_mixed, g_grid = grid_grad(
        cotangent.reshape(cells, width),
        (from_east, from_west, from_north, from_south),
        w_point, w_depth, clat, clon, wide,
    )
    w_in_t = jnp.pad(w_in.T, ((0, 0), (0, spec_wide - spec)))

    align = 16 * tiles * LANES // width
    head = spec - spec % LANES
    rest = round_up(spec - head, 16)
    rows_a = round_up(width + head, align)
    rows_b = round_up(width + rest + 16, align)
    emb, cells_got, mine, other, *rest_halves = encode(
        ids, arrived, (w_in_t, w_out.T, g_grid, w_out), spec, clon, rows_a, rest
    )
    sum_a = core_sum(mine, other)
    parts_a = spread(sum_a)

    grid_here, grid = bins(cells_got, emb, sum_a, clat, clon, wide)
    mix_here, grad_depth, mix_ext, east, west = mix(
        grid_here, w_depth, g_mixed, clat, clon, wide
    )
    mine, other = point(ids, cot_t, mix_here, grad_depth, rest_halves, rows_b)
    sum_b = core_sum(mine, other)
    sum_b, parts_a, east, west, mix_ext = lax.optimization_barrier(
        (sum_b, parts_a, east, west, mix_ext)
    )
    parts_b = spread(sum_b)

    left = lax.ppermute(east, "lon", east_way)
    right = lax.ppermute(west, "lon", west_way)
    sent = totals(parts_a, parts_b, left, right)
    full = spread(sent)
    line = lax.broadcasted_iota(i32, (clon, width), 0)

    def edge_row(e):
        row = mix_ext[e * wide : e * wide + clon].astype(f32)
        sides = jnp.where(line == 0, left[e], jnp.where(line == clon - 1, right[e], 0.0))
        return (row + sides).astype(bf16)

    top = lax.ppermute(edge_row(clat + 1), LAT, south_way)
    bottom = lax.ppermute(edge_row(0), LAT, north_way)
    latent = finish_latent(grid, mix_ext, (top, bottom, left, right), w_point, clat, clon, wide)

    obs_scale = float((rows_here * tiles) ** -0.5)
    cell_scale = float((cells * tiles) ** -0.5)
    full, latent = lax.optimization_barrier((full, latent))
    sibling = lax.ppermute(full, "core", SWAP)
    grad_in, grad_out, grad_point, grad_depth = unpack(
        ids, full, sibling, spec, width, rows_a, rest, obs_scale, cell_scale
    )
    return latent.reshape(clat, clon, width), grad_in, grad_out, grad_point, grad_depth


def solution(mesh):
    lat, lon = mesh.devices.shape
    fine = Mesh(mesh.devices.reshape(lat // 2, 2, lon), ("x", "core", "lon"))
    everyone = P(("x", "core", "lon"))
    field = P(LAT, "lon", None)
    in_specs = (everyone, everyone, everyone, P(), P(), P(), P(), field)
    out_specs = (field, P(), P(), P(), P())
    return jax.shard_map(
        on_device, mesh=fine, in_specs=in_specs, out_specs=out_specs, check_vma=False
    )
```

```python
import functools

import jax
import jax.numpy as jnp
from jax import lax
from jax.experimental import pallas as pl
from jax.experimental.pallas import tpu as pltpu
from jax.sharding import Mesh
from jax.sharding import PartitionSpec as P

LANES = 128
bf16 = jnp.bfloat16
f32 = jnp.float32
i32 = jnp.int32


def params(mib):
    return pltpu.CompilerParams(vmem_limit_bytes=mib * 1024 * 1024)


def round_up(n, m):
    return -(-n // m) * m


def dot(a, b, dims=(1, 0)):
    return lax.dot_general(
        a, b, (((dims[0],), (dims[1],)), ((), ())), preferred_element_type=f32
    )


def cost(us):
    return pl.CostEstimate(flops=us * 1153500000, bytes_accessed=0, transcendentals=0)


def smem():
    return pl.BlockSpec(memory_space=pltpu.SMEM)


def anywhere():
    return pl.BlockSpec(memory_space=pl.ANY)


def vmem():
    return pl.BlockSpec(memory_space=pltpu.VMEM)


def route_kernel(tiles, cap, clon, places_ref, rows_ref, out_ref):
    spec, n = rows_ref.shape
    head = out_ref.shape[1] - LANES
    owner = places_ref[0:1, :]
    hits = owner == lax.broadcasted_iota(i32, (tiles, n), 0)
    above = lax.broadcasted_iota(i32, (n, n), 0) < lax.broadcasted_iota(i32, (n, n), 1)
    count = dot(hits.astype(f32).astype(bf16), above.astype(f32).astype(bf16))
    rank = jnp.sum(jnp.where(hits, count, 0.0), axis=0, keepdims=True)
    slot = owner * cap + rank.astype(i32)
    cell = places_ref[1:2, :]
    line = lax.broadcasted_iota(i32, (LANES - (spec - head), n), 0)
    high = cell // clon
    spots = jnp.where(line == 0, high, jnp.where(line == 1, cell - high * clon, 0)).astype(f32)
    last = jnp.concatenate([rows_ref[head:, :].astype(f32), spots], axis=0).astype(bf16)
    first = rows_ref[:head, :]
    step = min(256, tiles * cap)

    def body(t, carry):
        base = t * step
        place = lax.broadcasted_iota(i32, (step, n), 0) + base
        pick = (slot == place).astype(f32).astype(bf16)
        at = pl.ds(pl.multiple_of(base, step), step)
        out_ref[at, :head] = dot(pick, first, (1, 1)).astype(bf16)
        out_ref[at, head:] = dot(pick, last, (1, 1)).astype(bf16)
        return carry

    lax.fori_loop(0, tiles * cap // step, body, 0)


def route(places, rows, tiles, cap, clon, spec_wide):
    return pl.pallas_call(
        functools.partial(route_kernel, tiles, cap, clon),
        out_shape=jax.ShapeDtypeStruct((tiles * cap, spec_wide), bf16),
        in_specs=[vmem()] * 2,
        out_specs=vmem(),
        compiler_params=params(12),
        cost_estimate=cost(3),
        name="route",
    )(places, rows)


GROUPS = 8
CHUNK = 8 * GROUPS


def column_of(place, per):
    return per * (place % GROUPS) + place // GROUPS


def place_of(column, per):
    return GROUPS * (column % per) + column // per


def one_hot(wanted, count):
    hit = wanted == lax.broadcasted_iota(i32, (wanted.shape[0], count), 1)
    return hit.astype(f32).astype(bf16)


def grid_grad_kernel(
    clat, clon, wide, cot_ref, east_ref, west_ref, north_ref, south_ref, wp_ref, wd_ref,
    cott_hbm, gm_hbm, gg_hbm, cott_ref, gm_ref, gg_ref, cot_ext, cot_own, east, west, sems,
):
    width = wp_ref.shape[0]
    per = clon // GROUPS
    w_point = wp_ref[...]
    east[...] = east_ref[...].astype(f32)
    west[...] = west_ref[...].astype(f32)
    line = lax.broadcasted_iota(i32, (wide - clon, width), 0)
    place = lax.broadcasted_iota(i32, (wide, 1), 0)
    column = column_of(place, per) - 1
    spread_order = one_hot(jnp.where(column < 0, wide - 1, column), wide)
    ends = jnp.where(place == clon + GROUPS - 1, clon, jnp.where(place == clon + GROUPS, wide - 1, -1))
    point_order = one_hot(jnp.where(place < clon, column_of(place, per), ends), wide)
    puts = [
        pltpu.make_async_copy(source, target, sems.at[i])
        for i, (source, target) in enumerate(
            ((gg_ref, gg_hbm), (gm_ref, gm_hbm), (cott_ref, cott_hbm))
        )
    ]

    def reorder(e, rows):
        ordered = dot(spread_order, rows)
        g = dot(ordered.astype(bf16), w_point, (1, 1)).astype(bf16).astype(f32)
        for n in range(width // LANES):
            gm_ref[n, e] = g[:, n * LANES : (n + 1) * LANES]
        cot_ext[pl.ds(pl.multiple_of(e * wide, 16), wide), :] = dot(point_order, rows).astype(bf16)
        return ordered

    def matmul(i, carry):
        at = pl.ds(pl.multiple_of(i * clon, 16), clon)
        tail = jnp.where(
            line == 0, east[pl.ds(i, 1), :], jnp.where(line == wide - clon - 1, west[pl.ds(i, 1), :], 0.0)
        )
        ordered = reorder(i + 1, jnp.concatenate([cot_ref[at, :], tail.astype(bf16)], axis=0))
        cot_own[at, :] = ordered[GROUPS : GROUPS + clon].astype(bf16)
        return carry

    reorder(0, north_ref[...])
    reorder(clat + 1, south_ref[...])
    used = (clat + 2) * wide
    cot_ext[used:, :] = jnp.zeros((cot_ext.shape[0] - used, width), bf16)
    lax.fori_loop(0, clat, matmul, 0)
    puts[1].start()

    def conv(i, carry):
        for n in range(width // LANES):
            cols = slice(n * LANES, (n + 1) * LANES)
            for c in range(0, clon, CHUNK):
                at = pl.ds(pl.multiple_of(i * clon + c, 16), CHUNK)
                out = cot_own[at, cols].astype(f32)
                for a in range(3):
                    g = gm_ref[n, i + 2 - a, c : c + CHUNK + 2 * GROUPS, :]
                    for b in range(3):
                        k = 3 * a + b
                        first = GROUPS * (2 - b)
                        out = out + wd_ref[k : k + 1, cols] * g[first : first + CHUNK]
                gg_ref[at, cols] = out.astype(bf16)
        return carry

    lax.fori_loop(0, clat, conv, 0)
    puts[0].start()

    def transpose(k, carry):
        at = pl.ds(pl.multiple_of(k * LANES, LANES), LANES)
        cott_ref[:, at] = cot_ext[at, :].T
        return carry

    lax.fori_loop(0, cot_ext.shape[0] // LANES, transpose, 0)
    puts[2].start()
    for put in puts:
        put.wait()


def grid_grad(cot, sides, w_point, w_depth, clat, clon, wide):
    width = w_point.shape[0]
    ext_rows = round_up((clat + 2) * wide, LANES)
    outs = (
        jax.ShapeDtypeStruct((width, ext_rows), bf16),
        jax.ShapeDtypeStruct((width // LANES, clat + 2, wide, LANES), f32),
        jax.ShapeDtypeStruct((clat * clon, width), bf16),
    )
    return pl.pallas_call(
        functools.partial(grid_grad_kernel, clat, clon, wide),
        out_shape=outs,
        in_specs=[vmem()] * 7,
        out_specs=(anywhere(),) * 3,
        scratch_shapes=[pltpu.VMEM(x.shape, x.dtype) for x in outs]
        + [pltpu.VMEM((ext_rows, width), bf16), pltpu.VMEM((clat * clon, width), bf16)]
        + [pltpu.VMEM((clat, width), f32)] * 2
        + [pltpu.SemaphoreType.DMA((3,))],
        compiler_params=params(58),
        cost_estimate=cost(10),
        name="grid_grad",
    )(cot, *sides, w_point, w_depth)


def write_halves(core, total, start, mine_ref, other_ref, first=0, size=None):
    size = total.shape[0] if size is None else size
    half = total.shape[1] // 2
    for ref, base in ((mine_ref, core * half), (other_ref, (1 - core) * half)):
        for n in range(half // LANES):
            cols = pl.ds(pl.multiple_of(base + n * LANES, LANES), LANES)
            ref[n, start : start + size, :] = total[first : first + size, cols].astype(bf16)


def clear_tail(start, *refs):
    for ref in refs:
        unused = ref.shape[1] - start
        if unused:
            ref[:, start:, :] = jnp.zeros((ref.shape[0], unused, LANES), bf16)


def start_loads(sources, targets, sems):
    loads = [
        pltpu.make_async_copy(source, target, sems.at[i])
        for i, (source, target) in enumerate(zip(sources, targets))
    ]
    for load in loads:
        load.start()
    return loads


def encode_kernel(
    spec, clon, ids_ref, rows_ref, wit_hbm, wot_hbm, gg_hbm, wo_hbm,
    emb_hbm, cell_ref, mine_ref, other_ref, mine_rest, other_rest,
    wit_ref, wot_ref, gg_ref, wo_ref, emb_ref, gi, gi_out, go, sems,
):
    loads = start_loads((wit_hbm, wot_hbm, gg_hbm, wo_hbm), (wit_ref, wot_ref, gg_ref, wo_ref), sems)
    core = ids_ref[0]
    slots, spec_wide = rows_ref.shape
    cells, width = gg_ref.shape
    step = min(512, slots)
    put_emb = pltpu.make_async_copy(emb_ref, emb_hbm, sems.at[len(loads)])
    last = rows_ref[:, spec_wide - LANES :]
    col = spec - (spec_wide - LANES)
    lane = lax.broadcasted_iota(i32, (16, LANES), 1)
    pick = jnp.where(lane == col, float(clon), jnp.where(lane == col + 1, 1.0, 0.0)).astype(bf16)
    cell_ref[...] = dot(pick, last, (1, 1))[0:8, :].astype(i32)

    for t in range(slots // step):
        at = slice(t * step, (t + 1) * step)
        rows = rows_ref[at, :]
        line = rows[:, spec : spec + 1].astype(f32).astype(i32)
        column = rows[:, spec + 1 : spec + 2].astype(f32).astype(i32)
        hits = one_hot(line * clon + place_of(column, clon // GROUPS), cells)
        if t == 0:
            loads[0].wait()
        preact = dot(wit_ref[...], rows, (1, 1))
        sig = 1.0 / (1.0 + jnp.exp(-preact))
        hidden = (preact * sig).astype(bf16)
        if t == 0:
            loads[1].wait()
        emb_ref[:, at] = dot(wot_ref[...], hidden).astype(bf16)
        if t == slots // step - 1:
            put_emb.start()
        if t == 0:
            loads[2].wait()
        g_emb = dot(hits, gg_ref[...]).astype(bf16)
        g_out = dot(hidden, g_emb)
        if t == 0:
            loads[3].wait()
        g_hid = dot(wo_ref[...], g_emb, (1, 1))
        g_pre = (g_hid * (sig * (1.0 + preact * (1.0 - sig)))).astype(bf16)
        g_in = dot(g_pre, rows)
        if t == 0:
            go[...] = g_out
            gi[...] = g_in
        else:
            go[...] += g_out
            gi[...] += g_in

    gi_out[...] = gi[...].T
    head = spec_wide - LANES
    write_halves(core, go, 0, mine_ref, other_ref)
    write_halves(core, gi_out, width, mine_ref, other_ref, 0, head)
    write_halves(core, gi_out, 0, mine_rest, other_rest, head, mine_rest.shape[1])
    clear_tail(width + head, mine_ref, other_ref)
    put_emb.wait()


def encode(ids, rows, weights, spec, clon, out_rows, rest_rows):
    slots, spec_wide = rows.shape
    width = weights[-1].shape[0]
    half = jax.ShapeDtypeStruct((width // LANES // 2, out_rows, LANES), bf16)
    rest = jax.ShapeDtypeStruct((width // LANES // 2, rest_rows, LANES), bf16)
    return pl.pallas_call(
        functools.partial(encode_kernel, spec, clon),
        out_shape=(
            jax.ShapeDtypeStruct((width, slots), bf16),
            jax.ShapeDtypeStruct((8, slots), i32),
            half,
            half,
            rest,
            rest,
        ),
        in_specs=[smem(), vmem()] + [anywhere()] * len(weights),
        out_specs=(anywhere(),) + (vmem(),) * 5,
        scratch_shapes=[pltpu.VMEM(x.shape, x.dtype) for x in weights]
        + [
            pltpu.VMEM((width, slots), bf16),
            pltpu.VMEM((width, spec_wide), f32),
            pltpu.VMEM((spec_wide, width), f32),
            pltpu.VMEM((width, width), f32),
            pltpu.SemaphoreType.DMA((len(weights) + 1,)),
        ],
        compiler_params=params(48),
        cost_estimate=cost(10),
        name="encode",
    )(ids, rows, *weights)


def mix_kernel(
    clat, clon, wide, ids_ref, cell_ref, wd_ref, mine_rest, other_rest,
    emb_hbm, gm_hbm, cott_hbm, after_ref,
    mine_ref, other_ref, east_out, west_out, grid_hbm, mix_hbm,
    emb_ref, gm_ref, cott_ref, wide_ref, grid_ref, mix_ref, east_ref, west_ref, gp, gd, sems,
):
    loads = start_loads((emb_hbm, gm_hbm, cott_hbm), (emb_ref, gm_ref, cott_ref), sems)
    put_grid = pltpu.make_async_copy(grid_ref, grid_hbm, sems.at[3])
    put_mix = pltpu.make_async_copy(mix_ref, mix_hbm, sems.at[4])
    core = ids_ref[0]
    width = emb_ref.shape[0]
    blocks = width // LANES

    cell = cell_ref[0:1, :]
    lines = 4
    place = lax.broadcasted_iota(i32, (wide, 1), 0)
    column = column_of(place, clon // GROUPS) - 1
    inside = (column >= 0) & (column < clon)
    wanted = [jnp.where(inside, column + k * clon, -clat * clon) for k in range(lines)]
    wanted = jnp.concatenate(wanted, axis=0)
    empty = jnp.zeros((blocks, 2, wide, LANES), f32)
    wide_ref[:, 0:2] = empty
    wide_ref[:, clat + 2 :] = empty
    gd[...] = jnp.zeros_like(gd)
    used = (clat + 2) * wide
    mix_ref[used:, :] = jnp.zeros((mix_ref.shape[0] - used, width), bf16)
    loads[0].wait()

    def bins(t, carry):
        hits = (cell == wanted + t * (lines * clon)).astype(f32).astype(bf16)
        grid = dot(hits, emb_ref[...], (1, 1)).astype(bf16).astype(f32)
        for k in range(lines):
            line = grid[k * wide : (k + 1) * wide]
            for n in range(blocks):
                wide_ref[n, t * lines + k + 2] = line[:, n * LANES : (n + 1) * LANES]
            at = pl.ds(pl.multiple_of((t * lines + k) * clon, 16), clon)
            grid_ref[at, :] = line[GROUPS : GROUPS + clon].astype(bf16)
        return carry

    lax.fori_loop(0, clat // lines, bins, 0)
    put_grid.start()
    loads[1].wait()
    group = lax.broadcasted_iota(i32, (GROUPS, LANES), 0)

    def conv(e, carry):
        for n in range(blocks):
            cols = slice(n * LANES, (n + 1) * LANES)
            weights = [wd_ref[k : k + 1, cols] for k in range(9)]
            taps = [gd[8 * k : 8 * k + 8, cols] for k in range(9)]
            for c in range(0, clon, CHUNK):
                grads = gm_ref[n, e, c : c + CHUNK + 2 * GROUPS, :]
                mixed = None
                for a in range(3):
                    cells = wide_ref[n, e + a, c : c + CHUNK + 2 * GROUPS, :]
                    middle = cells[GROUPS : GROUPS + CHUNK]
                    for b in range(3):
                        k = 3 * a + b
                        term = weights[k] * cells[GROUPS * b : GROUPS * b + CHUNK]
                        mixed = term if mixed is None else mixed + term
                        first = GROUPS * (2 - b)
                        part = (grads[first : first + CHUNK] * middle).reshape(CHUNK // 8, 8, LANES)
                        taps[k] = taps[k] + jnp.sum(part, axis=0)
                out_at = pl.ds(pl.multiple_of(e * wide + c, 16), CHUNK)
                mix_ref[out_at, cols] = mixed.astype(bf16)
            for k in range(9):
                gd[8 * k : 8 * k + 8, cols] = taps[k]
            ends = []
            for b, at, valid in ((0, clon, GROUPS - 1), (2, GROUPS, 0)):
                end = None
                for a in range(3):
                    term = weights[3 * a + b] * wide_ref[n, e + a, at : at + GROUPS, :]
                    end = term if end is None else end + term
                ends.append(jnp.where(group == valid, end, 0.0))
            east_ref[e, :, cols] = ends[0]
            west_ref[e, :, cols] = ends[1]
            out_at = pl.ds(pl.multiple_of(e * wide + clon, 16), wide - clon)
            mix_ref[out_at, cols] = jnp.concatenate(ends, axis=0).astype(bf16)
        return carry

    lax.fori_loop(0, clat + 2, conv, 0)
    put_mix.start()
    loads[2].wait()
    gp[...] = dot(cott_ref[...], mix_ref[...]).T
    east_out[...] = east_ref[:, GROUPS - 1, :]
    west_out[...] = west_ref[:, 0, :]
    taps = [jnp.sum(gd[8 * k : 8 * k + 8, :], axis=0, keepdims=True) for k in range(9)]
    gd[0:16, :] = jnp.concatenate(taps + [jnp.zeros((7, width), f32)], axis=0)
    rest = mine_rest.shape[1]
    write_halves(core, gp, 0, mine_ref, other_ref)
    mine_ref[:, width : width + rest, :] = mine_rest[...]
    other_ref[:, width : width + rest, :] = other_rest[...]
    write_halves(core, gd, width + rest, mine_ref, other_ref, 0, 16)
    clear_tail(width + rest + 16, mine_ref, other_ref)
    put_grid.wait()
    put_mix.wait()


def mix(ids, cell, w_depth, rest, emb, g_mixed, cot_t, after, clat, clon, wide, out_rows):
    width = w_depth.shape[1]
    half = jax.ShapeDtypeStruct((width // LANES // 2, out_rows, LANES), bf16)
    column = jax.ShapeDtypeStruct((clat + 2, width), f32)
    grid = jax.ShapeDtypeStruct((clat * clon, width), bf16)
    ext = jax.ShapeDtypeStruct(cot_t.shape[::-1], bf16)
    return pl.pallas_call(
        functools.partial(mix_kernel, clat, clon, wide),
        out_shape=(half, half, column, column, grid, ext),
        in_specs=[smem()] + [vmem()] * 4 + [anywhere()] * 4,
        out_specs=(vmem(),) * 4 + (anywhere(),) * 2,
        scratch_shapes=[pltpu.VMEM(x.shape, x.dtype) for x in (emb, g_mixed, cot_t)]
        + [
            pltpu.VMEM((width // LANES, clat + 4, wide, LANES), f32),
            pltpu.VMEM(grid.shape, bf16),
            pltpu.VMEM(ext.shape, bf16),
            pltpu.VMEM((clat + 2, GROUPS, width), f32),
            pltpu.VMEM((clat + 2, GROUPS, width), f32),
            pltpu.VMEM((width, width), f32),
            pltpu.VMEM((72, width), f32),
            pltpu.SemaphoreType.DMA((5,)),
        ],
        compiler_params=params(56),
        cost_estimate=cost(13),
        name="mix",
    )(ids, cell, w_depth, *rest, emb, g_mixed, cot_t, after)


def latent_kernel(
    clat, clon, wide, grid_ref, mix_ref, top_ref, bottom_ref, left_ref, right_ref, wp_ref, out_ref
):
    width = wp_ref.shape[0]
    w_point = wp_ref[...]
    line = lax.broadcasted_iota(i32, (clon, width), 0)
    column = lax.broadcasted_iota(i32, (clon, 1), 0)
    natural_order = one_hot(place_of(column, clon // GROUPS), clon)

    def body(i, carry):
        at = pl.ds(pl.multiple_of(i * clon, 16), clon)
        mixed = mix_ref[pl.ds(pl.multiple_of((i + 1) * wide, 16), clon), :].astype(f32)
        mixed = mixed + (i == 0).astype(f32) * top_ref[...].astype(f32)
        mixed = mixed + (i == clat - 1).astype(f32) * bottom_ref[...].astype(f32)
        mixed = mixed + jnp.where(
            line == 0, left_ref[pl.ds(i + 1, 1), :], jnp.where(line == clon - 1, right_ref[pl.ds(i + 1, 1), :], 0.0)
        )
        out = grid_ref[at, :].astype(f32) + dot(mixed.astype(bf16), w_point)
        out_ref[at, :] = dot(natural_order, out.astype(bf16)).astype(bf16)
        return carry

    lax.fori_loop(0, clat, body, 0, unroll=2)


def finish_latent(grid, mix_ext, sides, w_point, clat, clon, wide):
    return pl.pallas_call(
        functools.partial(latent_kernel, clat, clon, wide),
        out_shape=jax.ShapeDtypeStruct(grid.shape, bf16),
        in_specs=[vmem()] * 7,
        out_specs=vmem(),
        compiler_params=params(6),
        cost_estimate=cost(5),
        name="latent",
    )(grid, mix_ext, *sides, w_point)


SWAP = [(0, 1), (1, 0)]


def add_kernel(mine_ref, got_ref, out_ref):
    out_ref[...] = (mine_ref[...].astype(f32) + got_ref[...].astype(f32)).astype(bf16)


def core_sum(mine, other):
    return pl.pallas_call(
        add_kernel,
        out_shape=jax.ShapeDtypeStruct(mine.shape, bf16),
        in_specs=[vmem()] * 2,
        out_specs=vmem(),
        compiler_params=params(8),
        cost_estimate=cost(1),
        name="core_sum",
    )(mine, lax.ppermute(other, "core", SWAP))


def totals_kernel(a_ref, b_ref, *refs):
    out_ref = refs[-1]
    start = 0
    for ref in (a_ref, b_ref):
        size = ref.shape[1]
        total = jnp.sum(ref[...].astype(f32), axis=0).astype(bf16)
        out_ref[:, start : start + size, :] = jnp.broadcast_to(total[None], ref.shape)
        start += size


def totals(parts_a, parts_b, *after):
    chips, rows_a, _ = parts_a.shape
    return pl.pallas_call(
        totals_kernel,
        out_shape=jax.ShapeDtypeStruct((chips, rows_a + parts_b.shape[1], LANES), bf16),
        in_specs=[vmem()] * 2 + [anywhere()] * len(after),
        out_specs=vmem(),
        compiler_params=params(8),
        cost_estimate=cost(1),
        name="totals",
    )(parts_a, parts_b, *after)


def unpack_kernel(
    rows_a, rest, obs_scale, cell_scale, ids_ref, own_ref, sibling_ref, gi_ref, go_ref, gp_ref, gd_ref
):
    spec, width = gi_ref.shape
    chips = own_ref.shape[0]
    count = width // (2 * LANES)
    per = chips // count
    core = ids_ref[0]
    cut = rows_a // per
    head = spec - spec % LANES
    for ref, half in ((own_ref, core), (sibling_ref, 1 - core)):
        for n in range(count):
            cols = pl.ds(pl.multiple_of((half * count + n) * LANES, LANES), LANES)
            block = ref[n * per : (n + 1) * per].astype(f32)
            a = block[:, :cut].reshape(rows_a, LANES)
            b = block[:, cut:].reshape(per * (block.shape[1] - cut), LANES)
            go_ref[:, cols] = a[:width] * obs_scale
            gi_ref[:head, cols] = a[width : width + head] * obs_scale
            gp_ref[:, cols] = b[:width] * cell_scale
            gi_ref[head:, cols] = b[width : width + spec - head] * obs_scale
            gd_ref[:, cols] = b[width + rest : width + rest + gd_ref.shape[0]] * cell_scale


def unpack(ids, own, sibling, spec, width, rows_a, rest, obs_scale, cell_scale):
    return pl.pallas_call(
        functools.partial(unpack_kernel, rows_a, rest, obs_scale, cell_scale),
        out_shape=tuple(
            jax.ShapeDtypeStruct((rows, width), f32) for rows in (spec, width, width, 9)
        ),
        in_specs=[smem()] + [vmem()] * 2,
        out_specs=(vmem(),) * 4,
        compiler_params=params(8),
        cost_estimate=cost(3),
        name="unpack",
    )(ids, own, sibling)


def neighbours(axes, periodic):
    count = lax.axis_size(axes)
    up = [(i, i + 1) for i in range(count - 1)]
    if periodic:
        up.append((count - 1, 0))
    return up, [(t, s) for s, t in up]


LAT = ("x", "core")
CHIPS = ("x", "lon")


def spread(values):
    chips = lax.axis_size(CHIPS)
    values = values.reshape(chips, values.size // (chips * LANES), LANES)
    return lax.all_to_all(values, CHIPS, split_axis=0, concat_axis=0, tiled=True)


def on_device(spectra, owner, cell, w_in, w_out, w_point, w_depth, cotangent):
    tiles = lax.axis_size(LAT) * lax.axis_size("lon")
    rows_here, spec = spectra.shape
    cap = max(2, 2 * rows_here // tiles)
    clat, clon, width = cotangent.shape
    cells = clat * clon
    wide = clon + 16
    spec_wide = round_up(spec + 2, LANES)
    ids = lax.axis_index("core").reshape(1)
    east_way, west_way = neighbours("lon", True)
    south_way, north_way = neighbours(LAT, False)

    from_west = lax.ppermute(cotangent[:, -1], "lon", east_way)
    from_east = lax.ppermute(cotangent[:, 0], "lon", west_way)

    places = jnp.concatenate([owner.reshape(1, rows_here), cell.reshape(1, rows_here)], axis=0)
    outgoing = route(places, spectra.T, tiles, cap, clon, spec_wide)
    outgoing, from_west, from_east, w_in, w_out = lax.optimization_barrier(
        (outgoing, from_west, from_east, w_in, w_out)
    )
    arrived = lax.all_to_all(
        outgoing.reshape(tiles, cap, spec_wide), ("x", "core", "lon"), 0, 0, tiled=True
    ).reshape(tiles * cap, spec_wide)

    fill = jnp.zeros((wide - clon - 2, width), bf16)

    def halo_row(i):
        return jnp.concatenate([cotangent[i], from_east[i, None], fill, from_west[i, None]], axis=0)

    from_north = lax.ppermute(halo_row(clat - 1), LAT, south_way)
    from_south = lax.ppermute(halo_row(0), LAT, north_way)
    cot_t, g_mixed, g_grid = grid_grad(
        cotangent.reshape(cells, width),
        (from_east, from_west, from_north, from_south),
        w_point, w_depth, clat, clon, wide,
    )
    w_in_t = jnp.pad(w_in.T, ((0, 0), (0, spec_wide - spec)))

    align = 16 * tiles * LANES // width
    head = spec - spec % LANES
    rest = round_up(spec - head, 16)
    rows_a = round_up(width + head, align)
    rows_b = round_up(width + rest + 16, align)
    emb, cells_got, mine, other, *rest_halves = encode(
        ids, arrived, (w_in_t, w_out.T, g_grid, w_out), spec, clon, rows_a, rest
    )
    sum_a = core_sum(mine, other)
    parts_a = spread(sum_a)

    mine, other, east, west, grid, mix_ext = mix(
        ids, cells_got, w_depth, rest_halves, emb, g_mixed, cot_t, sum_a,
        clat, clon, wide, rows_b,
    )
    sum_b = core_sum(mine, other)
    sum_b, parts_a, east, west, mix_ext = lax.optimization_barrier(
        (sum_b, parts_a, east, west, mix_ext)
    )
    parts_b = spread(sum_b)

    left = lax.ppermute(east, "lon", east_way)
    right = lax.ppermute(west, "lon", west_way)
    sent = totals(parts_a, parts_b, left, right)
    full = spread(sent)
    line = lax.broadcasted_iota(i32, (clon, width), 0)

    def edge_row(e):
        row = mix_ext[e * wide : e * wide + clon].astype(f32)
        sides = jnp.where(line == 0, left[e], jnp.where(line == clon - 1, right[e], 0.0))
        return (row + sides).astype(bf16)

    top = lax.ppermute(edge_row(clat + 1), LAT, south_way)
    bottom = lax.ppermute(edge_row(0), LAT, north_way)
    latent = finish_latent(grid, mix_ext, (top, bottom, left, right), w_point, clat, clon, wide)

    obs_scale = float((rows_here * tiles) ** -0.5)
    cell_scale = float((cells * tiles) ** -0.5)
    full, latent = lax.optimization_barrier((full, latent))
    sibling = lax.ppermute(full, "core", SWAP)
    grad_in, grad_out, grad_point, grad_depth = unpack(
        ids, full, sibling, spec, width, rows_a, rest, obs_scale, cell_scale
    )
    return latent.reshape(clat, clon, width), grad_in, grad_out, grad_point, grad_depth


def solution(mesh):
    lat, lon = mesh.devices.shape
    fine = Mesh(mesh.devices.reshape(lat // 2, 2, lon), ("x", "core", "lon"))
    everyone = P(("x", "core", "lon"))
    field = P(LAT, "lon", None)
    in_specs = (everyone, everyone, everyone, P(), P(), P(), P(), field)
    out_specs = (field, P(), P(), P(), P())
    return jax.shard_map(
        on_device, mesh=fine, in_specs=in_specs, out_specs=out_specs, check_vma=False
    )
```

```python
import functools

import jax
import jax.numpy as jnp
from jax import lax
from jax.experimental import pallas as pl
from jax.experimental.pallas import tpu as pltpu
from jax.sharding import Mesh
from jax.sharding import PartitionSpec as P

LANES = 128
bf16 = jnp.bfloat16
f32 = jnp.float32
i32 = jnp.int32


def params(mib):
    return pltpu.CompilerParams(vmem_limit_bytes=mib * 1024 * 1024)


def round_up(n, m):
    return -(-n // m) * m


def dot(a, b, dims=(1, 0)):
    return lax.dot_general(
        a, b, (((dims[0],), (dims[1],)), ((), ())), preferred_element_type=f32
    )


def cost(us):
    return pl.CostEstimate(flops=us * 1153500000, bytes_accessed=0, transcendentals=0)


def smem():
    return pl.BlockSpec(memory_space=pltpu.SMEM)


def anywhere():
    return pl.BlockSpec(memory_space=pl.ANY)


def vmem():
    return pl.BlockSpec(memory_space=pltpu.VMEM)


def route_kernel(tiles, cap, clon, places_ref, rows_ref, out_ref):
    spec, n = rows_ref.shape
    head = out_ref.shape[1] - LANES
    owner = places_ref[0:1, :]
    hits = owner == lax.broadcasted_iota(i32, (tiles, n), 0)
    above = lax.broadcasted_iota(i32, (n, n), 0) < lax.broadcasted_iota(i32, (n, n), 1)
    count = dot(hits.astype(f32).astype(bf16), above.astype(f32).astype(bf16))
    rank = jnp.sum(jnp.where(hits, count, 0.0), axis=0, keepdims=True)
    slot = owner * cap + rank.astype(i32)
    cell = places_ref[1:2, :]
    line = lax.broadcasted_iota(i32, (LANES - (spec - head), n), 0)
    high = cell // clon
    spots = jnp.where(line == 0, high, jnp.where(line == 1, cell - high * clon, 0)).astype(f32)
    last = jnp.concatenate([rows_ref[head:, :].astype(f32), spots], axis=0).astype(bf16)
    first = rows_ref[:head, :]
    step = min(256, tiles * cap)

    def body(t, carry):
        base = t * step
        place = lax.broadcasted_iota(i32, (step, n), 0) + base
        pick = (slot == place).astype(f32).astype(bf16)
        at = pl.ds(pl.multiple_of(base, step), step)
        out_ref[at, :head] = dot(pick, first, (1, 1)).astype(bf16)
        out_ref[at, head:] = dot(pick, last, (1, 1)).astype(bf16)
        return carry

    lax.fori_loop(0, tiles * cap // step, body, 0)


def route(places, rows, tiles, cap, clon, spec_wide):
    return pl.pallas_call(
        functools.partial(route_kernel, tiles, cap, clon),
        out_shape=jax.ShapeDtypeStruct((tiles * cap, spec_wide), bf16),
        in_specs=[vmem()] * 2,
        out_specs=vmem(),
        compiler_params=params(12),
        cost_estimate=cost(3),
        name="route",
    )(places, rows)


GROUPS = 8
CHUNK = 8 * GROUPS


def column_of(place, per):
    return per * (place % GROUPS) + place // GROUPS


def place_of(column, per):
    return GROUPS * (column % per) + column // per


def one_hot(wanted, count):
    hit = wanted == lax.broadcasted_iota(i32, (wanted.shape[0], count), 1)
    return hit.astype(f32).astype(bf16)


def grid_grad_kernel(
    clat, clon, wide, cot_ref, east_ref, west_ref, north_ref, south_ref, wp_ref, wd_ref,
    cott_hbm, gm_hbm, gg_hbm, cott_ref, gm_ref, gg_ref, cot_ext, cot_own, east, west, sems,
):
    width = wp_ref.shape[0]
    per = clon // GROUPS
    w_point = wp_ref[...]
    east[...] = east_ref[...].astype(f32)
    west[...] = west_ref[...].astype(f32)
    line = lax.broadcasted_iota(i32, (wide - clon, width), 0)
    place = lax.broadcasted_iota(i32, (wide, 1), 0)
    column = column_of(place, per) - 1
    spread_order = one_hot(jnp.where(column < 0, wide - 1, column), wide)
    ends = jnp.where(place == clon + GROUPS - 1, clon, jnp.where(place == clon + GROUPS, wide - 1, -1))
    point_order = one_hot(jnp.where(place < clon, column_of(place, per), ends), wide)
    puts = [
        pltpu.make_async_copy(source, target, sems.at[i])
        for i, (source, target) in enumerate(
            ((gg_ref, gg_hbm), (gm_ref, gm_hbm), (cott_ref, cott_hbm))
        )
    ]

    def reorder(e, rows):
        ordered = dot(spread_order, rows)
        g = dot(ordered.astype(bf16), w_point, (1, 1)).astype(bf16).astype(f32)
        for n in range(width // LANES):
            gm_ref[n, e] = g[:, n * LANES : (n + 1) * LANES]
        cot_ext[pl.ds(pl.multiple_of(e * wide, 16), wide), :] = dot(point_order, rows).astype(bf16)
        return ordered

    def matmul(i, carry):
        at = pl.ds(pl.multiple_of(i * clon, 16), clon)
        tail = jnp.where(
            line == 0, east[pl.ds(i, 1), :], jnp.where(line == wide - clon - 1, west[pl.ds(i, 1), :], 0.0)
        )
        ordered = reorder(i + 1, jnp.concatenate([cot_ref[at, :], tail.astype(bf16)], axis=0))
        cot_own[at, :] = ordered[GROUPS : GROUPS + clon].astype(bf16)
        return carry

    reorder(0, north_ref[...])
    reorder(clat + 1, south_ref[...])
    used = (clat + 2) * wide
    cot_ext[used:, :] = jnp.zeros((cot_ext.shape[0] - used, width), bf16)
    lax.fori_loop(0, clat, matmul, 0)
    puts[1].start()

    def conv(i, carry):
        for n in range(width // LANES):
            cols = slice(n * LANES, (n + 1) * LANES)
            for c in range(0, clon, CHUNK):
                at = pl.ds(pl.multiple_of(i * clon + c, 16), CHUNK)
                out = cot_own[at, cols].astype(f32)
                for a in range(3):
                    g = gm_ref[n, i + 2 - a, c : c + CHUNK + 2 * GROUPS, :]
                    for b in range(3):
                        k = 3 * a + b
                        first = GROUPS * (2 - b)
                        out = out + wd_ref[k : k + 1, cols] * g[first : first + CHUNK]
                gg_ref[at, cols] = out.astype(bf16)
        return carry

    lax.fori_loop(0, clat, conv, 0)
    puts[0].start()

    def transpose(k, carry):
        at = pl.ds(pl.multiple_of(k * LANES, LANES), LANES)
        cott_ref[:, at] = cot_ext[at, :].T
        return carry

    lax.fori_loop(0, cot_ext.shape[0] // LANES, transpose, 0)
    puts[2].start()
    for put in puts:
        put.wait()


def grid_grad(cot, sides, w_point, w_depth, clat, clon, wide):
    width = w_point.shape[0]
    ext_rows = round_up((clat + 2) * wide, LANES)
    outs = (
        jax.ShapeDtypeStruct((width, ext_rows), bf16),
        jax.ShapeDtypeStruct((width // LANES, clat + 2, wide, LANES), f32),
        jax.ShapeDtypeStruct((clat * clon, width), bf16),
    )
    return pl.pallas_call(
        functools.partial(grid_grad_kernel, clat, clon, wide),
        out_shape=outs,
        in_specs=[vmem()] * 7,
        out_specs=(anywhere(),) * 3,
        scratch_shapes=[pltpu.VMEM(x.shape, x.dtype) for x in outs]
        + [pltpu.VMEM((ext_rows, width), bf16), pltpu.VMEM((clat * clon, width), bf16)]
        + [pltpu.VMEM((clat, width), f32)] * 2
        + [pltpu.SemaphoreType.DMA((3,))],
        compiler_params=params(58),
        cost_estimate=cost(10),
        name="grid_grad",
    )(cot, *sides, w_point, w_depth)


def write_halves(core, total, start, mine_ref, other_ref, first=0, size=None):
    size = total.shape[0] if size is None else size
    half = total.shape[1] // 2
    for ref, base in ((mine_ref, core * half), (other_ref, (1 - core) * half)):
        for n in range(half // LANES):
            cols = pl.ds(pl.multiple_of(base + n * LANES, LANES), LANES)
            ref[n, start : start + size, :] = total[first : first + size, cols].astype(bf16)


def clear_tail(start, *refs):
    for ref in refs:
        unused = ref.shape[1] - start
        if unused:
            ref[:, start:, :] = jnp.zeros((ref.shape[0], unused, LANES), bf16)


def start_loads(sources, targets, sems):
    loads = [
        pltpu.make_async_copy(source, target, sems.at[i])
        for i, (source, target) in enumerate(zip(sources, targets))
    ]
    for load in loads:
        load.start()
    return loads


def owner_kernel(
    spec, clat, clon, wide, core_ref, rows_ref, wd_ref, wit_hbm, wot_hbm, gg_hbm, wo_hbm, gm_hbm, cott_hbm,
    mine_ref, other_ref, east_out, west_out, grid_hbm, mix_hbm,
    wit_ref, wot_ref, gg_ref, wo_ref, gm_ref, cott_ref,
    emb_ref, gi, gi_out, go, wide_ref, grid_ref, mix_ref, east_ref, west_ref, gp, gd, sems,
):
    loads = start_loads((wit_hbm, wot_hbm, gg_hbm, wo_hbm), (wit_ref, wot_ref, gg_ref, wo_ref), sems)
    put_grid = pltpu.make_async_copy(grid_ref, grid_hbm, sems.at[6])
    put_mix = pltpu.make_async_copy(mix_ref, mix_hbm, sems.at[7])
    core = core_ref[0]
    slots, spec_wide = rows_ref.shape
    cells, width = gg_ref.shape
    blocks = width // LANES
    step = min(512, slots)

    for t in range(slots // step):
        at = slice(t * step, (t + 1) * step)
        rows = rows_ref[at, :]
        line = rows[:, spec : spec + 1].astype(f32).astype(i32)
        column = rows[:, spec + 1 : spec + 2].astype(f32).astype(i32)
        hits = one_hot(line * clon + place_of(column, clon // GROUPS), cells)
        if t == 0:
            loads[0].wait()
        preact = dot(wit_ref[...], rows, (1, 1))
        sig = 1.0 / (1.0 + jnp.exp(-preact))
        hidden = (preact * sig).astype(bf16)
        if t == 0:
            loads[1].wait()
        emb_ref[:, at] = dot(wot_ref[...], hidden).astype(bf16)
        if t == 0:
            loads[2].wait()
        g_emb = dot(hits, gg_ref[...]).astype(bf16)
        g_out = dot(hidden, g_emb)
        if t == 0:
            loads[3].wait()
            late = start_loads((gm_hbm, cott_hbm), (gm_ref, cott_ref), sems.at[pl.ds(4, 2)])
        g_hid = dot(wo_ref[...], g_emb, (1, 1))
        g_pre = (g_hid * (sig * (1.0 + preact * (1.0 - sig)))).astype(bf16)
        g_in = dot(g_pre, rows)
        if t == 0:
            go[...] = g_out
            gi[...] = g_in
        else:
            go[...] += g_out
            gi[...] += g_in

    last = rows_ref[:, spec_wide - LANES :]
    col = spec - (spec_wide - LANES)
    lane = lax.broadcasted_iota(i32, (16, LANES), 1)
    pick = jnp.where(lane == col, float(clon), jnp.where(lane == col + 1, 1.0, 0.0)).astype(bf16)
    cell = dot(pick, last, (1, 1))[0:1, :].astype(i32)
    lines = 4
    place = lax.broadcasted_iota(i32, (wide, 1), 0)
    column = column_of(place, clon // GROUPS) - 1
    inside = (column >= 0) & (column < clon)
    wanted = [jnp.where(inside, column + k * clon, -clat * clon) for k in range(lines)]
    wanted = jnp.concatenate(wanted, axis=0)
    empty = jnp.zeros((blocks, 2, wide, LANES), f32)
    wide_ref[:, 0:2] = empty
    wide_ref[:, clat + 2 :] = empty
    gd[...] = jnp.zeros_like(gd)
    used = (clat + 2) * wide
    mix_ref[used:, :] = jnp.zeros((mix_ref.shape[0] - used, width), bf16)

    def bins(t, carry):
        hits = (cell == wanted + t * (lines * clon)).astype(f32).astype(bf16)
        grid = dot(hits, emb_ref[...], (1, 1)).astype(bf16).astype(f32)
        for k in range(lines):
            line = grid[k * wide : (k + 1) * wide]
            for n in range(blocks):
                wide_ref[n, t * lines + k + 2] = line[:, n * LANES : (n + 1) * LANES]
            at = pl.ds(pl.multiple_of((t * lines + k) * clon, 16), clon)
            grid_ref[at, :] = line[GROUPS : GROUPS + clon].astype(bf16)
        return carry

    lax.fori_loop(0, clat // lines, bins, 0)
    put_grid.start()
    late[0].wait()
    group = lax.broadcasted_iota(i32, (GROUPS, LANES), 0)

    def conv(e, carry):
        for n in range(blocks):
            cols = slice(n * LANES, (n + 1) * LANES)
            weights = [wd_ref[k : k + 1, cols] for k in range(9)]
            taps = [gd[8 * k : 8 * k + 8, cols] for k in range(9)]
            for c in range(0, clon, CHUNK):
                grads = gm_ref[n, e, c : c + CHUNK + 2 * GROUPS, :]
                mixed = None
                for a in range(3):
                    cells = wide_ref[n, e + a, c : c + CHUNK + 2 * GROUPS, :]
                    middle = cells[GROUPS : GROUPS + CHUNK]
                    for b in range(3):
                        k = 3 * a + b
                        term = weights[k] * cells[GROUPS * b : GROUPS * b + CHUNK]
                        mixed = term if mixed is None else mixed + term
                        first = GROUPS * (2 - b)
                        part = (grads[first : first + CHUNK] * middle).reshape(CHUNK // 8, 8, LANES)
                        taps[k] = taps[k] + jnp.sum(part, axis=0)
                out_at = pl.ds(pl.multiple_of(e * wide + c, 16), CHUNK)
                mix_ref[out_at, cols] = mixed.astype(bf16)
            for k in range(9):
                gd[8 * k : 8 * k + 8, cols] = taps[k]
            ends = []
            for b, at, valid in ((0, clon, GROUPS - 1), (2, GROUPS, 0)):
                end = None
                for a in range(3):
                    term = weights[3 * a + b] * wide_ref[n, e + a, at : at + GROUPS, :]
                    end = term if end is None else end + term
                ends.append(jnp.where(group == valid, end, 0.0))
            east_ref[e, :, cols] = ends[0]
            west_ref[e, :, cols] = ends[1]
            out_at = pl.ds(pl.multiple_of(e * wide + clon, 16), wide - clon)
            mix_ref[out_at, cols] = jnp.concatenate(ends, axis=0).astype(bf16)
        return carry

    lax.fori_loop(0, clat + 2, conv, 0)
    put_mix.start()
    late[1].wait()
    gp[...] = dot(cott_ref[...], mix_ref[...]).T
    gi_out[...] = gi[...].T
    east_out[...] = east_ref[:, GROUPS - 1, :]
    west_out[...] = west_ref[:, 0, :]
    taps = [jnp.sum(gd[8 * k : 8 * k + 8, :], axis=0, keepdims=True) for k in range(9)]
    gd[0:16, :] = jnp.concatenate(taps + [jnp.zeros((7, width), f32)], axis=0)
    start = 0
    for total, size in ((go, width), (gi_out, round_up(spec, 16)), (gp, width), (gd, 16)):
        write_halves(core, total, start, mine_ref, other_ref, 0, size)
        start += size
    clear_tail(start, mine_ref, other_ref)
    put_grid.wait()
    put_mix.wait()


def owner_part(core, rows, w_depth, operands, spec, clat, clon, wide, out_rows):
    slots, spec_wide = rows.shape
    width = w_depth.shape[1]
    half = jax.ShapeDtypeStruct((width // LANES // 2, out_rows, LANES), bf16)
    column = jax.ShapeDtypeStruct((clat + 2, width), f32)
    grid = jax.ShapeDtypeStruct((clat * clon, width), bf16)
    ext = jax.ShapeDtypeStruct(operands[-1].shape[::-1], bf16)
    return pl.pallas_call(
        functools.partial(owner_kernel, spec, clat, clon, wide),
        out_shape=(half, half, column, column, grid, ext),
        in_specs=[smem()] + [vmem()] * 2 + [anywhere()] * len(operands),
        out_specs=(vmem(),) * 4 + (anywhere(),) * 2,
        scratch_shapes=[pltpu.VMEM(x.shape, x.dtype) for x in operands]
        + [
            pltpu.VMEM((width, slots), bf16),
            pltpu.VMEM((width, spec_wide), f32),
            pltpu.VMEM((spec_wide, width), f32),
            pltpu.VMEM((width, width), f32),
            pltpu.VMEM((width // LANES, clat + 4, wide, LANES), f32),
            pltpu.VMEM(grid.shape, bf16),
            pltpu.VMEM(ext.shape, bf16),
            pltpu.VMEM((clat + 2, GROUPS, width), f32),
            pltpu.VMEM((clat + 2, GROUPS, width), f32),
            pltpu.VMEM((width, width), f32),
            pltpu.VMEM((72, width), f32),
            pltpu.SemaphoreType.DMA((8,)),
        ],
        compiler_params=params(48),
        cost_estimate=cost(21),
        name="owner",
    )(core, rows, w_depth, *operands)


def latent_kernel(
    clat, clon, wide, grid_ref, mix_ref, top_ref, bottom_ref, left_ref, right_ref, wp_ref, out_ref
):
    width = wp_ref.shape[0]
    w_point = wp_ref[...]
    line = lax.broadcasted_iota(i32, (clon, width), 0)
    column = lax.broadcasted_iota(i32, (clon, 1), 0)
    natural_order = one_hot(place_of(column, clon // GROUPS), clon)

    def body(i, carry):
        at = pl.ds(pl.multiple_of(i * clon, 16), clon)
        mixed = mix_ref[pl.ds(pl.multiple_of((i + 1) * wide, 16), clon), :].astype(f32)
        mixed = mixed + (i == 0).astype(f32) * top_ref[...].astype(f32)
        mixed = mixed + (i == clat - 1).astype(f32) * bottom_ref[...].astype(f32)
        mixed = mixed + jnp.where(
            line == 0, left_ref[pl.ds(i + 1, 1), :], jnp.where(line == clon - 1, right_ref[pl.ds(i + 1, 1), :], 0.0)
        )
        out = grid_ref[at, :].astype(f32) + dot(mixed.astype(bf16), w_point)
        out_ref[at, :] = dot(natural_order, out.astype(bf16)).astype(bf16)
        return carry

    lax.fori_loop(0, clat, body, 0, unroll=2)


def finish_latent(grid, mix_ext, sides, w_point, clat, clon, wide):
    return pl.pallas_call(
        functools.partial(latent_kernel, clat, clon, wide),
        out_shape=jax.ShapeDtypeStruct(grid.shape, bf16),
        in_specs=[vmem()] * 7,
        out_specs=vmem(),
        compiler_params=params(6),
        cost_estimate=cost(5),
        name="latent",
    )(grid, mix_ext, *sides, w_point)


SWAP = [(0, 1), (1, 0)]


def add_kernel(mine_ref, got_ref, out_ref):
    out_ref[...] = (mine_ref[...].astype(f32) + got_ref[...].astype(f32)).astype(bf16)


def core_sum(mine, other):
    return pl.pallas_call(
        add_kernel,
        out_shape=jax.ShapeDtypeStruct(mine.shape, bf16),
        in_specs=[vmem()] * 2,
        out_specs=vmem(),
        compiler_params=params(8),
        cost_estimate=cost(1),
        name="core_sum",
    )(mine, lax.ppermute(other, "core", SWAP))


def totals_kernel(parts_ref, *refs):
    out_ref = refs[-1]
    total = jnp.sum(parts_ref[...].astype(f32), axis=0).astype(bf16)
    out_ref[...] = jnp.broadcast_to(total[None], parts_ref.shape)


def totals(parts, *after):
    return pl.pallas_call(
        totals_kernel,
        out_shape=jax.ShapeDtypeStruct(parts.shape, bf16),
        in_specs=[vmem()] + [anywhere()] * len(after),
        out_specs=vmem(),
        compiler_params=params(8),
        cost_estimate=cost(1),
        name="totals",
    )(parts, *after)


def unpack_kernel(
    obs_scale, cell_scale, core_ref, own_ref, sibling_ref, gi_ref, go_ref, gp_ref, gd_ref
):
    width = gi_ref.shape[1]
    chips = own_ref.shape[0]
    count = width // (2 * LANES)
    per = chips // count
    core = core_ref[0]
    for ref, half in ((own_ref, core), (sibling_ref, 1 - core)):
        for n in range(count):
            cols = pl.ds(pl.multiple_of((half * count + n) * LANES, LANES), LANES)
            block = ref[n * per : (n + 1) * per].astype(f32)
            block = block.reshape(per * block.shape[1], LANES)
            start = 0
            for out_ref, scale in (
                (go_ref, obs_scale), (gi_ref, obs_scale), (gp_ref, cell_scale), (gd_ref, cell_scale)
            ):
                size = out_ref.shape[0]
                out_ref[:, cols] = block[start : start + size] * scale
                start += round_up(size, 16)


def unpack(core, own, sibling, spec, width, obs_scale, cell_scale):
    return pl.pallas_call(
        functools.partial(unpack_kernel, obs_scale, cell_scale),
        out_shape=tuple(
            jax.ShapeDtypeStruct((rows, width), f32) for rows in (spec, width, width, 9)
        ),
        in_specs=[smem()] + [vmem()] * 2,
        out_specs=(vmem(),) * 4,
        compiler_params=params(8),
        cost_estimate=cost(3),
        name="unpack",
    )(core, own, sibling)


def neighbours(axes, periodic):
    count = lax.axis_size(axes)
    up = [(i, i + 1) for i in range(count - 1)]
    if periodic:
        up.append((count - 1, 0))
    return up, [(t, s) for s, t in up]


LAT = ("x", "core")
CHIPS = ("x", "lon")


def spread(values):
    chips = lax.axis_size(CHIPS)
    values = values.reshape(chips, values.size // (chips * LANES), LANES)
    return lax.all_to_all(values, CHIPS, split_axis=0, concat_axis=0, tiled=True)


def on_device(spectra, owner, cell, w_in, w_out, w_point, w_depth, cotangent):
    tiles = lax.axis_size(LAT) * lax.axis_size("lon")
    rows_here, spec = spectra.shape
    cap = max(2, 2 * rows_here // tiles)
    clat, clon, width = cotangent.shape
    cells = clat * clon
    wide = clon + 16
    spec_wide = round_up(spec + 2, LANES)
    core = lax.axis_index("core").reshape(1)
    east_way, west_way = neighbours("lon", True)
    south_way, north_way = neighbours(LAT, False)

    from_west = lax.ppermute(cotangent[:, -1], "lon", east_way)
    from_east = lax.ppermute(cotangent[:, 0], "lon", west_way)

    places = jnp.concatenate([owner.reshape(1, rows_here), cell.reshape(1, rows_here)], axis=0)
    outgoing = route(places, spectra.T, tiles, cap, clon, spec_wide)
    outgoing, from_west, from_east, w_in, w_out = lax.optimization_barrier(
        (outgoing, from_west, from_east, w_in, w_out)
    )
    arrived = lax.all_to_all(
        outgoing.reshape(tiles, cap, spec_wide), ("x", "core", "lon"), 0, 0, tiled=True
    ).reshape(tiles * cap, spec_wide)

    fill = jnp.zeros((wide - clon - 2, width), bf16)

    def halo_row(i):
        return jnp.concatenate([cotangent[i], from_east[i, None], fill, from_west[i, None]], axis=0)

    from_north = lax.ppermute(halo_row(clat - 1), LAT, south_way)
    from_south = lax.ppermute(halo_row(0), LAT, north_way)
    cot_t, g_mixed, g_grid = grid_grad(
        cotangent.reshape(cells, width),
        (from_east, from_west, from_north, from_south),
        w_point, w_depth, clat, clon, wide,
    )
    w_in_t = jnp.pad(w_in.T, ((0, 0), (0, spec_wide - spec)))

    out_rows = round_up(2 * width + round_up(spec, 16) + 16, 16 * tiles * LANES // width)
    operands = w_in_t, w_out.T, g_grid, w_out, g_mixed, cot_t
    mine, other, east, west, grid, mix_ext = owner_part(
        core, arrived, w_depth, operands, spec, clat, clon, wide, out_rows
    )
    summed = core_sum(mine, other)
    summed, east, west, mix_ext = lax.optimization_barrier((summed, east, west, mix_ext))
    parts = spread(summed)

    left = lax.ppermute(east, "lon", east_way)
    right = lax.ppermute(west, "lon", west_way)
    sent = totals(parts, left, right)
    full = spread(sent)
    line = lax.broadcasted_iota(i32, (clon, width), 0)

    def edge_row(e):
        row = mix_ext[e * wide : e * wide + clon].astype(f32)
        sides = jnp.where(line == 0, left[e], jnp.where(line == clon - 1, right[e], 0.0))
        return (row + sides).astype(bf16)

    top = lax.ppermute(edge_row(clat + 1), LAT, south_way)
    bottom = lax.ppermute(edge_row(0), LAT, north_way)
    latent = finish_latent(grid, mix_ext, (top, bottom, left, right), w_point, clat, clon, wide)

    obs_scale = float((rows_here * tiles) ** -0.5)
    cell_scale = float((cells * tiles) ** -0.5)
    full, latent = lax.optimization_barrier((full, latent))
    sibling = lax.ppermute(full, "core", SWAP)
    grad_in, grad_out, grad_point, grad_depth = unpack(
        core, full, sibling, spec, width, obs_scale, cell_scale
    )
    return latent.reshape(clat, clon, width), grad_in, grad_out, grad_point, grad_depth


def solution(mesh):
    lat, lon = mesh.devices.shape
    fine = Mesh(mesh.devices.reshape(lat // 2, 2, lon), ("x", "core", "lon"))
    everyone = P(("x", "core", "lon"))
    field = P(LAT, "lon", None)
    in_specs = (everyone, everyone, everyone, P(), P(), P(), P(), field)
    out_specs = (field, P(), P(), P(), P())
    return jax.shard_map(
        on_device, mesh=fine, in_specs=in_specs, out_specs=out_specs, check_vma=False
    )
```

```python
import functools

import jax
import jax.numpy as jnp
from jax import lax
from jax.experimental import pallas as pl
from jax.experimental.pallas import tpu as pltpu
from jax.sharding import Mesh
from jax.sharding import PartitionSpec as P

LANES = 128
bf16 = jnp.bfloat16
f32 = jnp.float32
i32 = jnp.int32


def params(mib):
    return pltpu.CompilerParams(vmem_limit_bytes=mib * 1024 * 1024)


def round_up(n, m):
    return -(-n // m) * m


def dot(a, b, dims=(1, 0)):
    return lax.dot_general(
        a, b, (((dims[0],), (dims[1],)), ((), ())), preferred_element_type=f32
    )


def cost(us):
    return pl.CostEstimate(flops=us * 1153500000, bytes_accessed=0, transcendentals=0)


def smem():
    return pl.BlockSpec(memory_space=pltpu.SMEM)


def anywhere():
    return pl.BlockSpec(memory_space=pl.ANY)


def vmem():
    return pl.BlockSpec(memory_space=pltpu.VMEM)


def route_kernel(tiles, cap, clon, places_ref, rows_ref, out_ref):
    spec, n = rows_ref.shape
    head = out_ref.shape[1] - LANES
    owner = places_ref[0:1, :]
    hits = owner == lax.broadcasted_iota(i32, (tiles, n), 0)
    above = lax.broadcasted_iota(i32, (n, n), 0) < lax.broadcasted_iota(i32, (n, n), 1)
    count = dot(hits.astype(f32).astype(bf16), above.astype(f32).astype(bf16))
    rank = jnp.sum(jnp.where(hits, count, 0.0), axis=0, keepdims=True)
    slot = owner * cap + rank.astype(i32)
    cell = places_ref[1:2, :]
    line = lax.broadcasted_iota(i32, (LANES - (spec - head), n), 0)
    high = cell // clon
    spots = jnp.where(line == 0, high, jnp.where(line == 1, cell - high * clon, 0)).astype(f32)
    last = jnp.concatenate([rows_ref[head:, :].astype(f32), spots], axis=0).astype(bf16)
    first = rows_ref[:head, :]
    step = min(256, tiles * cap)

    def body(t, carry):
        base = t * step
        place = lax.broadcasted_iota(i32, (step, n), 0) + base
        pick = (slot == place).astype(f32).astype(bf16)
        at = pl.ds(pl.multiple_of(base, step), step)
        out_ref[at, :head] = dot(pick, first, (1, 1)).astype(bf16)
        out_ref[at, head:] = dot(pick, last, (1, 1)).astype(bf16)
        return carry

    lax.fori_loop(0, tiles * cap // step, body, 0)


def route(places, rows, tiles, cap, clon, spec_wide):
    return pl.pallas_call(
        functools.partial(route_kernel, tiles, cap, clon),
        out_shape=jax.ShapeDtypeStruct((tiles * cap, spec_wide), bf16),
        in_specs=[vmem()] * 2,
        out_specs=vmem(),
        compiler_params=params(12),
        cost_estimate=cost(3),
        name="route",
    )(places, rows)


GROUPS = 8
CHUNK = 8 * GROUPS


def column_of(place, per):
    return per * (place % GROUPS) + place // GROUPS


def place_of(column, per):
    return GROUPS * (column % per) + column // per


def one_hot(wanted, count):
    hit = wanted == lax.broadcasted_iota(i32, (wanted.shape[0], count), 1)
    return hit.astype(f32).astype(bf16)


def grid_grad_kernel(
    clat, clon, wide, cot_ref, east_ref, west_ref, north_ref, south_ref, wp_ref, wd_ref,
    cott_hbm, gm_hbm, gg_hbm, cott_ref, gm_ref, gg_ref, cot_ext, cot_own, east, west, sems,
):
    width = wp_ref.shape[0]
    per = clon // GROUPS
    w_point = wp_ref[...]
    east[...] = east_ref[...].astype(f32)
    west[...] = west_ref[...].astype(f32)
    line = lax.broadcasted_iota(i32, (wide - clon, width), 0)
    place = lax.broadcasted_iota(i32, (wide, 1), 0)
    column = column_of(place, per) - 1
    spread_order = one_hot(jnp.where(column < 0, wide - 1, column), wide)
    ends = jnp.where(place == clon + GROUPS - 1, clon, jnp.where(place == clon + GROUPS, wide - 1, -1))
    point_order = one_hot(jnp.where(place < clon, column_of(place, per), ends), wide)
    puts = [
        pltpu.make_async_copy(source, target, sems.at[i])
        for i, (source, target) in enumerate(
            ((gg_ref, gg_hbm), (gm_ref, gm_hbm), (cott_ref, cott_hbm))
        )
    ]

    def reorder(e, rows):
        ordered = dot(spread_order, rows)
        g = dot(ordered.astype(bf16), w_point, (1, 1)).astype(bf16).astype(f32)
        for n in range(width // LANES):
            gm_ref[n, e] = g[:, n * LANES : (n + 1) * LANES]
        cot_ext[pl.ds(pl.multiple_of(e * wide, 16), wide), :] = dot(point_order, rows).astype(bf16)
        return ordered

    def matmul(i, carry):
        at = pl.ds(pl.multiple_of(i * clon, 16), clon)
        tail = jnp.where(
            line == 0, east[pl.ds(i, 1), :], jnp.where(line == wide - clon - 1, west[pl.ds(i, 1), :], 0.0)
        )
        ordered = reorder(i + 1, jnp.concatenate([cot_ref[at, :], tail.astype(bf16)], axis=0))
        cot_own[at, :] = ordered[GROUPS : GROUPS + clon].astype(bf16)
        return carry

    reorder(0, north_ref[...])
    reorder(clat + 1, south_ref[...])
    used = (clat + 2) * wide
    cot_ext[used:, :] = jnp.zeros((cot_ext.shape[0] - used, width), bf16)
    lax.fori_loop(0, clat, matmul, 0)
    puts[1].start()

    def conv(i, carry):
        for n in range(width // LANES):
            cols = slice(n * LANES, (n + 1) * LANES)
            for c in range(0, clon, CHUNK):
                at = pl.ds(pl.multiple_of(i * clon + c, 16), CHUNK)
                out = cot_own[at, cols].astype(f32)
                for a in range(3):
                    g = gm_ref[n, i + 2 - a, c : c + CHUNK + 2 * GROUPS, :]
                    for b in range(3):
                        k = 3 * a + b
                        first = GROUPS * (2 - b)
                        out = out + wd_ref[k : k + 1, cols] * g[first : first + CHUNK]
                gg_ref[at, cols] = out.astype(bf16)
        return carry

    lax.fori_loop(0, clat, conv, 0)
    puts[0].start()

    def transpose(k, carry):
        at = pl.ds(pl.multiple_of(k * LANES, LANES), LANES)
        cott_ref[:, at] = cot_ext[at, :].T
        return carry

    lax.fori_loop(0, cot_ext.shape[0] // LANES, transpose, 0)
    puts[2].start()
    for put in puts:
        put.wait()


def grid_grad(cot, sides, w_point, w_depth, clat, clon, wide):
    width = w_point.shape[0]
    ext_rows = round_up((clat + 2) * wide, LANES)
    outs = (
        jax.ShapeDtypeStruct((width, ext_rows), bf16),
        jax.ShapeDtypeStruct((width // LANES, clat + 2, wide, LANES), f32),
        jax.ShapeDtypeStruct((clat * clon, width), bf16),
    )
    return pl.pallas_call(
        functools.partial(grid_grad_kernel, clat, clon, wide),
        out_shape=outs,
        in_specs=[vmem()] * 7,
        out_specs=(anywhere(),) * 3,
        scratch_shapes=[pltpu.VMEM(x.shape, x.dtype) for x in outs]
        + [pltpu.VMEM((ext_rows, width), bf16), pltpu.VMEM((clat * clon, width), bf16)]
        + [pltpu.VMEM((clat, width), f32)] * 2
        + [pltpu.SemaphoreType.DMA((3,))],
        compiler_params=params(58),
        cost_estimate=cost(10),
        name="grid_grad",
    )(cot, *sides, w_point, w_depth)


def write_halves(core, total, start, mine_ref, other_ref, first=0, size=None):
    size = total.shape[0] if size is None else size
    half = total.shape[1] // 2
    for ref, base in ((mine_ref, core * half), (other_ref, (1 - core) * half)):
        for n in range(half // LANES):
            cols = pl.ds(pl.multiple_of(base + n * LANES, LANES), LANES)
            ref[n, start : start + size, :] = total[first : first + size, cols].astype(bf16)


def clear_tail(start, *refs):
    for ref in refs:
        unused = ref.shape[1] - start
        if unused:
            ref[:, start:, :] = jnp.zeros((ref.shape[0], unused, LANES), bf16)


def start_loads(sources, targets, sems):
    loads = [
        pltpu.make_async_copy(source, target, sems.at[i])
        for i, (source, target) in enumerate(zip(sources, targets))
    ]
    for load in loads:
        load.start()
    return loads


def owner_kernel(
    spec, clat, clon, wide, core_ref, rows_ref, wd_ref, wit_hbm, wot_hbm, gg_hbm, wo_hbm, gm_hbm, cott_hbm,
    mine_ref, other_ref, east_out, west_out, grid_hbm, mix_hbm,
    wit_ref, wot_ref, gg_ref, wo_ref, gm_ref, cott_ref,
    emb_ref, hid_ref, slope_ref, gi, gi_out, go, wide_ref, grid_ref, mix_ref, east_ref, west_ref, gp, gd, sems,
):
    first = start_loads((wit_hbm, wot_hbm), (wit_ref, wot_ref), sems)
    put_grid = pltpu.make_async_copy(grid_ref, grid_hbm, sems.at[6])
    put_mix = pltpu.make_async_copy(mix_ref, mix_hbm, sems.at[7])
    core = core_ref[0]
    slots, spec_wide = rows_ref.shape
    cells, width = gg_ref.shape
    blocks = width // LANES
    step = min(512, slots)

    go[...] = jnp.zeros_like(go)
    gi[...] = jnp.zeros_like(gi)
    for load in first:
        load.wait()
    late = start_loads(
        (gg_hbm, wo_hbm, gm_hbm, cott_hbm), (gg_ref, wo_ref, gm_ref, cott_ref), sems.at[pl.ds(2, 4)]
    )
    for t in range(slots // step):
        at = slice(t * step, (t + 1) * step)
        preact = dot(wit_ref[...], rows_ref[at, :], (1, 1))
        sig = 1.0 / (1.0 + jnp.exp(-preact))
        hidden = (preact * sig).astype(bf16)
        hid_ref[:, at] = hidden
        slope_ref[:, at] = sig * (1.0 + preact * (1.0 - sig))
        emb_ref[:, at] = dot(wot_ref[...], hidden).astype(bf16)

    last = rows_ref[:, spec_wide - LANES :]
    col = spec - (spec_wide - LANES)
    lane = lax.broadcasted_iota(i32, (16, LANES), 1)
    pick = jnp.where(lane == col, float(clon), jnp.where(lane == col + 1, 1.0, 0.0)).astype(bf16)
    cell = dot(pick, last, (1, 1))[0:1, :].astype(i32)
    lines = 4
    place = lax.broadcasted_iota(i32, (wide, 1), 0)
    column = column_of(place, clon // GROUPS) - 1
    inside = (column >= 0) & (column < clon)
    wanted = [jnp.where(inside, column + k * clon, -clat * clon) for k in range(lines)]
    wanted = jnp.concatenate(wanted, axis=0)
    empty = jnp.zeros((blocks, 2, wide, LANES), f32)
    wide_ref[:, 0:2] = empty
    wide_ref[:, clat + 2 :] = empty
    gd[...] = jnp.zeros_like(gd)
    used = (clat + 2) * wide
    mix_ref[used:, :] = jnp.zeros((mix_ref.shape[0] - used, width), bf16)

    def bins(t, carry):
        hits = (cell == wanted + t * (lines * clon)).astype(f32).astype(bf16)
        grid = dot(hits, emb_ref[...], (1, 1)).astype(bf16).astype(f32)
        for k in range(lines):
            line = grid[k * wide : (k + 1) * wide]
            for n in range(blocks):
                wide_ref[n, t * lines + k + 2] = line[:, n * LANES : (n + 1) * LANES]
            at = pl.ds(pl.multiple_of((t * lines + k) * clon, 16), clon)
            grid_ref[at, :] = line[GROUPS : GROUPS + clon].astype(bf16)
        return carry

    lax.fori_loop(0, clat // lines, bins, 0)
    put_grid.start()
    for load in late[:3]:
        load.wait()
    group = lax.broadcasted_iota(i32, (GROUPS, LANES), 0)

    def conv(e):
        for n in range(blocks):
            cols = slice(n * LANES, (n + 1) * LANES)
            weights = [wd_ref[k : k + 1, cols] for k in range(9)]
            taps = [gd[8 * k : 8 * k + 8, cols] for k in range(9)]
            for c in range(0, clon, CHUNK):
                grads = gm_ref[n, e, c : c + CHUNK + 2 * GROUPS, :]
                mixed = None
                for a in range(3):
                    cells = wide_ref[n, e + a, c : c + CHUNK + 2 * GROUPS, :]
                    middle = cells[GROUPS : GROUPS + CHUNK]
                    for b in range(3):
                        k = 3 * a + b
                        term = weights[k] * cells[GROUPS * b : GROUPS * b + CHUNK]
                        mixed = term if mixed is None else mixed + term
                        first = GROUPS * (2 - b)
                        part = (grads[first : first + CHUNK] * middle).reshape(CHUNK // 8, 8, LANES)
                        taps[k] = taps[k] + jnp.sum(part, axis=0)
                out_at = pl.ds(pl.multiple_of(e * wide + c, 16), CHUNK)
                mix_ref[out_at, cols] = mixed.astype(bf16)
            for k in range(9):
                gd[8 * k : 8 * k + 8, cols] = taps[k]
            ends = []
            for b, at, valid in ((0, clon, GROUPS - 1), (2, GROUPS, 0)):
                end = None
                for a in range(3):
                    term = weights[3 * a + b] * wide_ref[n, e + a, at : at + GROUPS, :]
                    end = term if end is None else end + term
                ends.append(jnp.where(group == valid, end, 0.0))
            east_ref[e, :, cols] = ends[0]
            west_ref[e, :, cols] = ends[1]
            out_at = pl.ds(pl.multiple_of(e * wide + clon, 16), wide - clon)
            mix_ref[out_at, cols] = jnp.concatenate(ends, axis=0).astype(bf16)

    part = min(256, slots)
    count = slots // part
    each = (clat + 2) // count

    def both(t, carry):
        at = pl.ds(pl.multiple_of(t * part, part), part)
        rows = rows_ref[at, :]
        line = rows[:, spec : spec + 1].astype(f32).astype(i32)
        column = rows[:, spec + 1 : spec + 2].astype(f32).astype(i32)
        hits = one_hot(line * clon + place_of(column, clon // GROUPS), cells)
        g_emb = dot(hits, gg_ref[...]).astype(bf16)
        done = each // 2
        for k in range(done):
            conv(t * each + k)
        go[...] += dot(hid_ref[:, at], g_emb)
        g_pre = (dot(wo_ref[...], g_emb, (1, 1)) * slope_ref[:, at]).astype(bf16)
        for k in range(done, each):
            conv(t * each + k)
        gi[...] += dot(g_pre, rows)
        return carry

    def remaining(e, carry):
        conv(e)
        return carry

    lax.fori_loop(0, count, both, 0)
    lax.fori_loop(count * each, clat + 2, remaining, 0)
    put_mix.start()
    late[3].wait()
    gp[...] = dot(cott_ref[...], mix_ref[...]).T
    gi_out[...] = gi[...].T
    east_out[...] = east_ref[:, GROUPS - 1, :]
    west_out[...] = west_ref[:, 0, :]
    taps = [jnp.sum(gd[8 * k : 8 * k + 8, :], axis=0, keepdims=True) for k in range(9)]
    gd[0:16, :] = jnp.concatenate(taps + [jnp.zeros((7, width), f32)], axis=0)
    start = 0
    for total, size in ((go, width), (gi_out, round_up(spec, 16)), (gp, width), (gd, 16)):
        write_halves(core, total, start, mine_ref, other_ref, 0, size)
        start += size
    clear_tail(start, mine_ref, other_ref)
    put_grid.wait()
    put_mix.wait()


def owner_part(core, rows, w_depth, operands, spec, clat, clon, wide, out_rows):
    slots, spec_wide = rows.shape
    width = w_depth.shape[1]
    half = jax.ShapeDtypeStruct((width // LANES // 2, out_rows, LANES), bf16)
    column = jax.ShapeDtypeStruct((clat + 2, width), f32)
    grid = jax.ShapeDtypeStruct((clat * clon, width), bf16)
    ext = jax.ShapeDtypeStruct(operands[-1].shape[::-1], bf16)
    return pl.pallas_call(
        functools.partial(owner_kernel, spec, clat, clon, wide),
        out_shape=(half, half, column, column, grid, ext),
        in_specs=[smem()] + [vmem()] * 2 + [anywhere()] * len(operands),
        out_specs=(vmem(),) * 4 + (anywhere(),) * 2,
        scratch_shapes=[pltpu.VMEM(x.shape, x.dtype) for x in operands]
        + [
            pltpu.VMEM((width, slots), bf16),
            pltpu.VMEM((width, slots), bf16),
            pltpu.VMEM((width, slots), f32),
            pltpu.VMEM((width, spec_wide), f32),
            pltpu.VMEM((spec_wide, width), f32),
            pltpu.VMEM((width, width), f32),
            pltpu.VMEM((width // LANES, clat + 4, wide, LANES), f32),
            pltpu.VMEM(grid.shape, bf16),
            pltpu.VMEM(ext.shape, bf16),
            pltpu.VMEM((clat + 2, GROUPS, width), f32),
            pltpu.VMEM((clat + 2, GROUPS, width), f32),
            pltpu.VMEM((width, width), f32),
            pltpu.VMEM((72, width), f32),
            pltpu.SemaphoreType.DMA((8,)),
        ],
        compiler_params=params(48),
        cost_estimate=cost(21),
        name="owner",
    )(core, rows, w_depth, *operands)


def latent_kernel(
    clat, clon, wide, grid_ref, mix_ref, top_ref, bottom_ref, left_ref, right_ref, wp_ref, out_ref
):
    width = wp_ref.shape[0]
    w_point = wp_ref[...]
    line = lax.broadcasted_iota(i32, (clon, width), 0)
    column = lax.broadcasted_iota(i32, (clon, 1), 0)
    natural_order = one_hot(place_of(column, clon // GROUPS), clon)

    def body(i, carry):
        at = pl.ds(pl.multiple_of(i * clon, 16), clon)
        mixed = mix_ref[pl.ds(pl.multiple_of((i + 1) * wide, 16), clon), :].astype(f32)
        mixed = mixed + (i == 0).astype(f32) * top_ref[...].astype(f32)
        mixed = mixed + (i == clat - 1).astype(f32) * bottom_ref[...].astype(f32)
        mixed = mixed + jnp.where(
            line == 0, left_ref[pl.ds(i + 1, 1), :], jnp.where(line == clon - 1, right_ref[pl.ds(i + 1, 1), :], 0.0)
        )
        out = grid_ref[at, :].astype(f32) + dot(mixed.astype(bf16), w_point)
        out_ref[at, :] = dot(natural_order, out.astype(bf16)).astype(bf16)
        return carry

    lax.fori_loop(0, clat, body, 0, unroll=2)


def finish_latent(grid, mix_ext, sides, w_point, clat, clon, wide):
    return pl.pallas_call(
        functools.partial(latent_kernel, clat, clon, wide),
        out_shape=jax.ShapeDtypeStruct(grid.shape, bf16),
        in_specs=[vmem()] * 7,
        out_specs=vmem(),
        compiler_params=params(6),
        cost_estimate=cost(5),
        name="latent",
    )(grid, mix_ext, *sides, w_point)


SWAP = [(0, 1), (1, 0)]


def add_kernel(mine_ref, got_ref, out_ref):
    out_ref[...] = (mine_ref[...].astype(f32) + got_ref[...].astype(f32)).astype(bf16)


def core_sum(mine, other):
    return pl.pallas_call(
        add_kernel,
        out_shape=jax.ShapeDtypeStruct(mine.shape, bf16),
        in_specs=[vmem()] * 2,
        out_specs=vmem(),
        compiler_params=params(8),
        cost_estimate=cost(1),
        name="core_sum",
    )(mine, lax.ppermute(other, "core", SWAP))


def totals_kernel(parts_ref, *refs):
    out_ref = refs[-1]
    total = jnp.sum(parts_ref[...].astype(f32), axis=0).astype(bf16)
    out_ref[...] = jnp.broadcast_to(total[None], parts_ref.shape)


def totals(parts, *after):
    return pl.pallas_call(
        totals_kernel,
        out_shape=jax.ShapeDtypeStruct(parts.shape, bf16),
        in_specs=[vmem()] + [anywhere()] * len(after),
        out_specs=vmem(),
        compiler_params=params(8),
        cost_estimate=cost(1),
        name="totals",
    )(parts, *after)


def unpack_kernel(
    obs_scale, cell_scale, core_ref, own_ref, sibling_ref, gi_ref, go_ref, gp_ref, gd_ref
):
    width = gi_ref.shape[1]
    chips = own_ref.shape[0]
    count = width // (2 * LANES)
    per = chips // count
    core = core_ref[0]
    for ref, half in ((own_ref, core), (sibling_ref, 1 - core)):
        for n in range(count):
            cols = pl.ds(pl.multiple_of((half * count + n) * LANES, LANES), LANES)
            block = ref[n * per : (n + 1) * per].astype(f32)
            block = block.reshape(per * block.shape[1], LANES)
            start = 0
            for out_ref, scale in (
                (go_ref, obs_scale), (gi_ref, obs_scale), (gp_ref, cell_scale), (gd_ref, cell_scale)
            ):
                size = out_ref.shape[0]
                out_ref[:, cols] = block[start : start + size] * scale
                start += round_up(size, 16)


def unpack(core, own, sibling, spec, width, obs_scale, cell_scale):
    return pl.pallas_call(
        functools.partial(unpack_kernel, obs_scale, cell_scale),
        out_shape=tuple(
            jax.ShapeDtypeStruct((rows, width), f32) for rows in (spec, width, width, 9)
        ),
        in_specs=[smem()] + [vmem()] * 2,
        out_specs=(vmem(),) * 4,
        compiler_params=params(8),
        cost_estimate=cost(3),
        name="unpack",
    )(core, own, sibling)


def neighbours(axes, periodic):
    count = lax.axis_size(axes)
    up = [(i, i + 1) for i in range(count - 1)]
    if periodic:
        up.append((count - 1, 0))
    return up, [(t, s) for s, t in up]


LAT = ("x", "core")
CHIPS = ("x", "lon")


def spread(values):
    chips = lax.axis_size(CHIPS)
    values = values.reshape(chips, values.size // (chips * LANES), LANES)
    return lax.all_to_all(values, CHIPS, split_axis=0, concat_axis=0, tiled=True)


def on_device(spectra, owner, cell, w_in, w_out, w_point, w_depth, cotangent):
    tiles = lax.axis_size(LAT) * lax.axis_size("lon")
    rows_here, spec = spectra.shape
    cap = max(2, 2 * rows_here // tiles)
    clat, clon, width = cotangent.shape
    cells = clat * clon
    wide = clon + 16
    spec_wide = round_up(spec + 2, LANES)
    core = lax.axis_index("core").reshape(1)
    east_way, west_way = neighbours("lon", True)
    south_way, north_way = neighbours(LAT, False)

    from_west = lax.ppermute(cotangent[:, -1], "lon", east_way)
    from_east = lax.ppermute(cotangent[:, 0], "lon", west_way)

    places = jnp.concatenate([owner.reshape(1, rows_here), cell.reshape(1, rows_here)], axis=0)
    outgoing = route(places, spectra.T, tiles, cap, clon, spec_wide)
    outgoing, from_west, from_east, w_in, w_out = lax.optimization_barrier(
        (outgoing, from_west, from_east, w_in, w_out)
    )
    arrived = lax.all_to_all(
        outgoing.reshape(tiles, cap, spec_wide), ("x", "core", "lon"), 0, 0, tiled=True
    ).reshape(tiles * cap, spec_wide)

    fill = jnp.zeros((wide - clon - 2, width), bf16)

    def halo_row(i):
        return jnp.concatenate([cotangent[i], from_east[i, None], fill, from_west[i, None]], axis=0)

    from_north = lax.ppermute(halo_row(clat - 1), LAT, south_way)
    from_south = lax.ppermute(halo_row(0), LAT, north_way)
    cot_t, g_mixed, g_grid = grid_grad(
        cotangent.reshape(cells, width),
        (from_east, from_west, from_north, from_south),
        w_point, w_depth, clat, clon, wide,
    )
    w_in_t = jnp.pad(w_in.T, ((0, 0), (0, spec_wide - spec)))

    out_rows = round_up(2 * width + round_up(spec, 16) + 16, 16 * tiles * LANES // width)
    operands = w_in_t, w_out.T, g_grid, w_out, g_mixed, cot_t
    mine, other, east, west, grid, mix_ext = owner_part(
        core, arrived, w_depth, operands, spec, clat, clon, wide, out_rows
    )
    summed = core_sum(mine, other)
    summed, east, west, mix_ext = lax.optimization_barrier((summed, east, west, mix_ext))
    parts = spread(summed)

    left = lax.ppermute(east, "lon", east_way)
    right = lax.ppermute(west, "lon", west_way)
    sent = totals(parts, left, right)
    full = spread(sent)
    line = lax.broadcasted_iota(i32, (clon, width), 0)

    def edge_row(e):
        row = mix_ext[e * wide : e * wide + clon].astype(f32)
        sides = jnp.where(line == 0, left[e], jnp.where(line == clon - 1, right[e], 0.0))
        return (row + sides).astype(bf16)

    top = lax.ppermute(edge_row(clat + 1), LAT, south_way)
    bottom = lax.ppermute(edge_row(0), LAT, north_way)
    latent = finish_latent(grid, mix_ext, (top, bottom, left, right), w_point, clat, clon, wide)

    obs_scale = float((rows_here * tiles) ** -0.5)
    cell_scale = float((cells * tiles) ** -0.5)
    full, latent = lax.optimization_barrier((full, latent))
    sibling = lax.ppermute(full, "core", SWAP)
    grad_in, grad_out, grad_point, grad_depth = unpack(
        core, full, sibling, spec, width, obs_scale, cell_scale
    )
    return latent.reshape(clat, clon, width), grad_in, grad_out, grad_point, grad_depth


def solution(mesh):
    lat, lon = mesh.devices.shape
    fine = Mesh(mesh.devices.reshape(lat // 2, 2, lon), ("x", "core", "lon"))
    everyone = P(("x", "core", "lon"))
    field = P(LAT, "lon", None)
    in_specs = (everyone, everyone, everyone, P(), P(), P(), P(), field)
    out_specs = (field, P(), P(), P(), P())
    return jax.shard_map(
        on_device, mesh=fine, in_specs=in_specs, out_specs=out_specs, check_vma=False
    )
```

```python
import functools

import jax
import jax.numpy as jnp
from jax import lax
from jax.experimental import pallas as pl
from jax.experimental.pallas import tpu as pltpu
from jax.sharding import Mesh
from jax.sharding import PartitionSpec as P

LANES = 128
bf16 = jnp.bfloat16
f32 = jnp.float32
i32 = jnp.int32


def params(mib):
    return pltpu.CompilerParams(vmem_limit_bytes=mib * 1024 * 1024)


def round_up(n, m):
    return -(-n // m) * m


def dot(a, b, dims=(1, 0)):
    return lax.dot_general(
        a, b, (((dims[0],), (dims[1],)), ((), ())), preferred_element_type=f32
    )


def cost(us):
    return pl.CostEstimate(flops=us * 1153500000, bytes_accessed=0, transcendentals=0)


def smem():
    return pl.BlockSpec(memory_space=pltpu.SMEM)


def anywhere():
    return pl.BlockSpec(memory_space=pl.ANY)


def vmem():
    return pl.BlockSpec(memory_space=pltpu.VMEM)


def route_kernel(tiles, cap, clon, owner_ref, cell_ref, rows_ref, out_ref):
    spec, n = rows_ref.shape
    head = out_ref.shape[1] - LANES
    owner = owner_ref[...]
    hits = owner == lax.broadcasted_iota(i32, (tiles, n), 0)
    above = lax.broadcasted_iota(i32, (n, n), 0) < lax.broadcasted_iota(i32, (n, n), 1)
    count = dot(hits.astype(f32).astype(bf16), above.astype(f32).astype(bf16))
    rank = jnp.sum(jnp.where(hits, count, 0.0), axis=0, keepdims=True)
    slot = owner * cap + rank.astype(i32)
    cell = cell_ref[...]
    line = lax.broadcasted_iota(i32, (LANES - (spec - head), n), 0)
    high = cell // clon
    spots = jnp.where(line == 0, high, jnp.where(line == 1, cell - high * clon, 0)).astype(f32)
    last = jnp.concatenate([rows_ref[head:, :].astype(f32), spots], axis=0).astype(bf16)
    first = rows_ref[:head, :]
    step = min(256, tiles * cap)

    def body(t, carry):
        base = t * step
        place = lax.broadcasted_iota(i32, (step, n), 0) + base
        pick = (slot == place).astype(f32).astype(bf16)
        at = pl.ds(pl.multiple_of(base, step), step)
        out_ref[at, :head] = dot(pick, first, (1, 1)).astype(bf16)
        out_ref[at, head:] = dot(pick, last, (1, 1)).astype(bf16)
        return carry

    lax.fori_loop(0, tiles * cap // step, body, 0)


def route(owner, cell, rows, tiles, cap, clon, spec_wide):
    return pl.pallas_call(
        functools.partial(route_kernel, tiles, cap, clon),
        out_shape=jax.ShapeDtypeStruct((tiles * cap, spec_wide), bf16),
        in_specs=[vmem()] * 3,
        out_specs=vmem(),
        compiler_params=params(60),
        cost_estimate=cost(3),
        name="route",
    )(owner, cell, rows)


GROUPS = 8
CHUNK = 8 * GROUPS


def column_of(place, per):
    return per * (place % GROUPS) + place // GROUPS


def place_of(column, per):
    return GROUPS * (column % per) + column // per


def one_hot(wanted, count):
    hit = wanted == lax.broadcasted_iota(i32, (wanted.shape[0], count), 1)
    return hit.astype(f32).astype(bf16)


def grid_grad_kernel(
    clat, clon, wide, cot_ref, east_ref, west_ref, north_ref, south_ref, wp_ref, wd_ref,
    cott_hbm, gm_hbm, gg_hbm, cott_ref, gm_ref, gg_ref, cot_ext, cot_own, east, west, sems,
):
    width = wp_ref.shape[0]
    per = clon // GROUPS
    w_point = wp_ref[...]
    east[...] = east_ref[...].astype(f32)
    west[...] = west_ref[...].astype(f32)
    line = lax.broadcasted_iota(i32, (wide - clon, width), 0)
    place = lax.broadcasted_iota(i32, (wide, 1), 0)
    column = column_of(place, per) - 1
    spread_order = one_hot(jnp.where(column < 0, wide - 1, column), wide)
    ends = jnp.where(place == clon + GROUPS - 1, clon, jnp.where(place == clon + GROUPS, wide - 1, -1))
    point_order = one_hot(jnp.where(place < clon, column_of(place, per), ends), wide)
    puts = [
        pltpu.make_async_copy(source, target, sems.at[i])
        for i, (source, target) in enumerate(
            ((gg_ref, gg_hbm), (gm_ref, gm_hbm), (cott_ref, cott_hbm))
        )
    ]

    def reorder(e, rows):
        ordered = dot(spread_order, rows)
        g = dot(ordered.astype(bf16), w_point, (1, 1)).astype(bf16).astype(f32)
        for n in range(width // LANES):
            gm_ref[n, e] = g[:, n * LANES : (n + 1) * LANES]
        cot_ext[pl.ds(pl.multiple_of(e * wide, 16), wide), :] = dot(point_order, rows).astype(bf16)
        return ordered

    def matmul(i, carry):
        at = pl.ds(pl.multiple_of(i * clon, 16), clon)
        tail = jnp.where(
            line == 0, east[pl.ds(i, 1), :], jnp.where(line == wide - clon - 1, west[pl.ds(i, 1), :], 0.0)
        )
        ordered = reorder(i + 1, jnp.concatenate([cot_ref[at, :], tail.astype(bf16)], axis=0))
        cot_own[at, :] = ordered[GROUPS : GROUPS + clon].astype(bf16)
        return carry

    reorder(0, north_ref[...])
    reorder(clat + 1, south_ref[...])
    used = (clat + 2) * wide
    cot_ext[used:, :] = jnp.zeros((cot_ext.shape[0] - used, width), bf16)
    lax.fori_loop(0, clat, matmul, 0)
    puts[1].start()

    def conv(i, carry):
        for n in range(width // LANES):
            cols = slice(n * LANES, (n + 1) * LANES)
            for c in range(0, clon, CHUNK):
                at = pl.ds(pl.multiple_of(i * clon + c, 16), CHUNK)
                out = cot_own[at, cols].astype(f32)
                for a in range(3):
                    g = gm_ref[n, i + 2 - a, c : c + CHUNK + 2 * GROUPS, :]
                    for b in range(3):
                        k = 3 * a + b
                        first = GROUPS * (2 - b)
                        out = out + wd_ref[k : k + 1, cols] * g[first : first + CHUNK]
                gg_ref[at, cols] = out.astype(bf16)
        return carry

    lax.fori_loop(0, clat, conv, 0)
    puts[0].start()

    def transpose(k, carry):
        at = pl.ds(pl.multiple_of(k * LANES, LANES), LANES)
        cott_ref[:, at] = cot_ext[at, :].T
        return carry

    lax.fori_loop(0, cot_ext.shape[0] // LANES, transpose, 0)
    puts[2].start()
    for put in puts:
        put.wait()


def grid_grad(cot, sides, w_point, w_depth, clat, clon, wide):
    width = w_point.shape[0]
    ext_rows = round_up((clat + 2) * wide, LANES)
    outs = (
        jax.ShapeDtypeStruct((width, ext_rows), bf16),
        jax.ShapeDtypeStruct((width // LANES, clat + 2, wide, LANES), f32),
        jax.ShapeDtypeStruct((clat * clon, width), bf16),
    )
    return pl.pallas_call(
        functools.partial(grid_grad_kernel, clat, clon, wide),
        out_shape=outs,
        in_specs=[vmem()] * 7,
        out_specs=(anywhere(),) * 3,
        scratch_shapes=[pltpu.VMEM(x.shape, x.dtype) for x in outs]
        + [pltpu.VMEM((ext_rows, width), bf16), pltpu.VMEM((clat * clon, width), bf16)]
        + [pltpu.VMEM((clat, width), f32)] * 2
        + [pltpu.SemaphoreType.DMA((3,))],
        compiler_params=params(58),
        cost_estimate=cost(10),
        name="grid_grad",
    )(cot, *sides, w_point, w_depth)


def write_halves(core, total, start, mine_ref, other_ref, first=0, size=None):
    size = total.shape[0] if size is None else size
    half = total.shape[1] // 2
    for ref, base in ((mine_ref, core * half), (other_ref, (1 - core) * half)):
        for n in range(half // LANES):
            cols = pl.ds(pl.multiple_of(base + n * LANES, LANES), LANES)
            ref[n, start : start + size, :] = total[first : first + size, cols].astype(bf16)


def clear_tail(start, *refs):
    for ref in refs:
        unused = ref.shape[1] - start
        if unused:
            ref[:, start:, :] = jnp.zeros((ref.shape[0], unused, LANES), bf16)


def start_loads(sources, targets, sems):
    loads = [
        pltpu.make_async_copy(source, target, sems.at[i])
        for i, (source, target) in enumerate(zip(sources, targets))
    ]
    for load in loads:
        load.start()
    return loads


def owner_kernel(
    spec, clat, clon, wide, core_ref, rows_ref, wd_ref, wit_hbm, wot_hbm, gg_hbm, wo_hbm, gm_hbm, cott_hbm,
    mine_ref, other_ref, east_out, west_out, grid_hbm, mix_hbm,
    wit_ref, wot_ref, gg_ref, wo_ref, gm_ref, cott_ref,
    emb_ref, gi, gi_out, go, wide_ref, grid_ref, mix_ref, east_ref, west_ref, gp, gd, sems,
):
    loads = start_loads((wit_hbm, wot_hbm), (wit_ref, wot_ref), sems)
    put_grid = pltpu.make_async_copy(grid_ref, grid_hbm, sems.at[6])
    put_mix = pltpu.make_async_copy(mix_ref, mix_hbm, sems.at[7])
    core = core_ref[0]
    slots, spec_wide = rows_ref.shape
    cells, width = gg_ref.shape
    blocks = width // LANES
    step = min(512, slots)

    for t in range(slots // step):
        at = slice(t * step, (t + 1) * step)
        rows = rows_ref[at, :]
        line = rows[:, spec : spec + 1].astype(f32).astype(i32)
        column = rows[:, spec + 1 : spec + 2].astype(f32).astype(i32)
        hits = one_hot(line * clon + place_of(column, clon // GROUPS), cells)
        if t == 0:
            loads[0].wait()
            loads += start_loads((gg_hbm, wo_hbm), (gg_ref, wo_ref), sems.at[pl.ds(2, 2)])
        preact = dot(wit_ref[...], rows, (1, 1))
        sig = 1.0 / (1.0 + jnp.exp(-preact))
        hidden = (preact * sig).astype(bf16)
        if t == 0:
            loads[1].wait()
        emb_ref[:, at] = dot(wot_ref[...], hidden).astype(bf16)
        if t == 0:
            loads[2].wait()
        g_emb = dot(hits, gg_ref[...]).astype(bf16)
        g_out = dot(hidden, g_emb)
        if t == 0:
            loads[3].wait()
            late = start_loads((gm_hbm, cott_hbm), (gm_ref, cott_ref), sems.at[pl.ds(4, 2)])
        g_hid = dot(wo_ref[...], g_emb, (1, 1))
        g_pre = (g_hid * (sig * (1.0 + preact * (1.0 - sig)))).astype(bf16)
        g_in = dot(g_pre, rows)
        if t == 0:
            go[...] = g_out
            gi[...] = g_in
        else:
            go[...] += g_out
            gi[...] += g_in

    last = rows_ref[:, spec_wide - LANES :]
    col = spec - (spec_wide - LANES)
    lane = lax.broadcasted_iota(i32, (16, LANES), 1)
    pick = jnp.where(lane == col, float(clon), jnp.where(lane == col + 1, 1.0, 0.0)).astype(bf16)
    cell = dot(pick, last, (1, 1))[0:1, :].astype(i32)
    lines = 4
    place = lax.broadcasted_iota(i32, (wide, 1), 0)
    column = column_of(place, clon // GROUPS) - 1
    inside = (column >= 0) & (column < clon)
    wanted = [jnp.where(inside, column + k * clon, -clat * clon) for k in range(lines)]
    wanted = jnp.concatenate(wanted, axis=0)
    empty = jnp.zeros((blocks, 2, wide, LANES), f32)
    wide_ref[:, 0:2] = empty
    wide_ref[:, clat + 2 :] = empty
    gd[...] = jnp.zeros_like(gd)
    used = (clat + 2) * wide
    mix_ref[used:, :] = jnp.zeros((mix_ref.shape[0] - used, width), bf16)

    def bins(t, carry):
        hits = (cell == wanted + t * (lines * clon)).astype(f32).astype(bf16)
        grid = dot(hits, emb_ref[...], (1, 1)).astype(bf16).astype(f32)
        for k in range(lines):
            line = grid[k * wide : (k + 1) * wide]
            for n in range(blocks):
                wide_ref[n, t * lines + k + 2] = line[:, n * LANES : (n + 1) * LANES]
            at = pl.ds(pl.multiple_of((t * lines + k) * clon, 16), clon)
            grid_ref[at, :] = line[GROUPS : GROUPS + clon].astype(bf16)
        return carry

    lax.fori_loop(0, clat // lines, bins, 0)
    put_grid.start()
    late[0].wait()
    group = lax.broadcasted_iota(i32, (GROUPS, LANES), 0)

    def conv(e, carry):
        for n in range(blocks):
            cols = slice(n * LANES, (n + 1) * LANES)
            weights = [wd_ref[k : k + 1, cols] for k in range(9)]
            taps = [gd[8 * k : 8 * k + 8, cols] for k in range(9)]
            for c in range(0, clon, CHUNK):
                grads = gm_ref[n, e, c : c + CHUNK + 2 * GROUPS, :]
                mixed = None
                for a in range(3):
                    cells = wide_ref[n, e + a, c : c + CHUNK + 2 * GROUPS, :]
                    middle = cells[GROUPS : GROUPS + CHUNK]
                    for b in range(3):
                        k = 3 * a + b
                        term = weights[k] * cells[GROUPS * b : GROUPS * b + CHUNK]
                        mixed = term if mixed is None else mixed + term
                        first = GROUPS * (2 - b)
                        part = (grads[first : first + CHUNK] * middle).reshape(CHUNK // 8, 8, LANES)
                        taps[k] = taps[k] + jnp.sum(part, axis=0)
                out_at = pl.ds(pl.multiple_of(e * wide + c, 16), CHUNK)
                mix_ref[out_at, cols] = mixed.astype(bf16)
            for k in range(9):
                gd[8 * k : 8 * k + 8, cols] = taps[k]
            ends = []
            for b, at, valid in ((0, clon, GROUPS - 1), (2, GROUPS, 0)):
                end = None
                for a in range(3):
                    term = weights[3 * a + b] * wide_ref[n, e + a, at : at + GROUPS, :]
                    end = term if end is None else end + term
                ends.append(jnp.where(group == valid, end, 0.0))
            east_ref[e, :, cols] = ends[0]
            west_ref[e, :, cols] = ends[1]
            out_at = pl.ds(pl.multiple_of(e * wide + clon, 16), wide - clon)
            mix_ref[out_at, cols] = jnp.concatenate(ends, axis=0).astype(bf16)
        return carry

    lax.fori_loop(0, clat + 2, conv, 0, unroll=2)
    put_mix.start()
    late[1].wait()
    gp[...] = dot(cott_ref[...], mix_ref[...]).astype(bf16).T
    gi_out[...] = gi[...].astype(bf16).T
    east_out[...] = east_ref[:, GROUPS - 1, :]
    west_out[...] = west_ref[:, 0, :]
    taps = [jnp.sum(gd[8 * k : 8 * k + 8, :], axis=0, keepdims=True) for k in range(9)]
    gd[0:16, :] = jnp.concatenate(taps + [jnp.zeros((7, width), f32)], axis=0)
    start = 0
    for total, size in ((go, width), (gi_out, round_up(spec, 16)), (gp, width), (gd, 16)):
        write_halves(core, total, start, mine_ref, other_ref, 0, size)
        start += size
    clear_tail(start, mine_ref, other_ref)
    put_grid.wait()
    put_mix.wait()


def owner_part(core, rows, w_depth, operands, spec, clat, clon, wide, out_rows):
    slots, spec_wide = rows.shape
    width = w_depth.shape[1]
    half = jax.ShapeDtypeStruct((width // LANES // 2, out_rows, LANES), bf16)
    column = jax.ShapeDtypeStruct((clat + 2, width), f32)
    grid = jax.ShapeDtypeStruct((clat * clon, width), bf16)
    ext = jax.ShapeDtypeStruct(operands[-1].shape[::-1], bf16)
    return pl.pallas_call(
        functools.partial(owner_kernel, spec, clat, clon, wide),
        out_shape=(half, half, column, column, grid, ext),
        in_specs=[smem()] + [vmem()] * 2 + [anywhere()] * len(operands),
        out_specs=(vmem(),) * 4 + (anywhere(),) * 2,
        scratch_shapes=[pltpu.VMEM(x.shape, x.dtype) for x in operands]
        + [
            pltpu.VMEM((width, slots), bf16),
            pltpu.VMEM((width, spec_wide), f32),
            pltpu.VMEM((spec_wide, width), bf16),
            pltpu.VMEM((width, width), f32),
            pltpu.VMEM((width // LANES, clat + 4, wide, LANES), f32),
            pltpu.VMEM(grid.shape, bf16),
            pltpu.VMEM(ext.shape, bf16),
            pltpu.VMEM((clat + 2, GROUPS, width), f32),
            pltpu.VMEM((clat + 2, GROUPS, width), f32),
            pltpu.VMEM((width, width), bf16),
            pltpu.VMEM((72, width), f32),
            pltpu.SemaphoreType.DMA((8,)),
        ],
        compiler_params=params(48),
        cost_estimate=cost(21),
        name="owner",
    )(core, rows, w_depth, *operands)


def latent_kernel(
    clat, clon, wide, grid_ref, mix_ref, top_ref, bottom_ref, left_ref, right_ref, wp_ref, out_ref
):
    width = wp_ref.shape[0]
    w_point = wp_ref[...]
    line = lax.broadcasted_iota(i32, (clon, width), 0)
    column = lax.broadcasted_iota(i32, (clon, 1), 0)
    natural_order = one_hot(place_of(column, clon // GROUPS), clon)

    def body(i, carry):
        at = pl.ds(pl.multiple_of(i * clon, 16), clon)
        mixed = mix_ref[pl.ds(pl.multiple_of((i + 1) * wide, 16), clon), :].astype(f32)
        mixed = mixed + (i == 0).astype(f32) * top_ref[...].astype(f32)
        mixed = mixed + (i == clat - 1).astype(f32) * bottom_ref[...].astype(f32)
        mixed = mixed + jnp.where(
            line == 0, left_ref[pl.ds(i + 1, 1), :], jnp.where(line == clon - 1, right_ref[pl.ds(i + 1, 1), :], 0.0)
        )
        out = grid_ref[at, :].astype(f32) + dot(mixed.astype(bf16), w_point)
        out_ref[at, :] = dot(natural_order, out.astype(bf16)).astype(bf16)
        return carry

    lax.fori_loop(0, clat, body, 0, unroll=2)


def finish_latent(grid, mix_ext, sides, w_point, clat, clon, wide):
    return pl.pallas_call(
        functools.partial(latent_kernel, clat, clon, wide),
        out_shape=jax.ShapeDtypeStruct(grid.shape, bf16),
        in_specs=[vmem()] * 7,
        out_specs=vmem(),
        compiler_params=params(6),
        cost_estimate=cost(5),
        name="latent",
    )(grid, mix_ext, *sides, w_point)


SWAP = [(0, 1), (1, 0)]


def add_kernel(mine_ref, got_ref, out_ref):
    out_ref[...] = (mine_ref[...].astype(f32) + got_ref[...].astype(f32)).astype(bf16)


def core_sum(mine, other):
    return pl.pallas_call(
        add_kernel,
        out_shape=jax.ShapeDtypeStruct(mine.shape, bf16),
        in_specs=[vmem()] * 2,
        out_specs=vmem(),
        compiler_params=params(8),
        cost_estimate=cost(1),
        name="core_sum",
    )(mine, lax.ppermute(other, "core", SWAP))


def totals_kernel(parts_ref, *refs):
    out_ref = refs[-1]
    total = jnp.sum(parts_ref[...].astype(f32), axis=0).astype(bf16)
    out_ref[...] = jnp.broadcast_to(total[None], parts_ref.shape)


def totals(parts, *after):
    return pl.pallas_call(
        totals_kernel,
        out_shape=jax.ShapeDtypeStruct(parts.shape, bf16),
        in_specs=[vmem()] + [anywhere()] * len(after),
        out_specs=vmem(),
        compiler_params=params(8),
        cost_estimate=cost(1),
        name="totals",
    )(parts, *after)


def unpack_kernel(
    obs_scale, cell_scale, core_ref, own_ref, sibling_ref, gi_ref, go_ref, gp_ref, gd_ref
):
    width = gi_ref.shape[1]
    chips = own_ref.shape[0]
    count = width // (2 * LANES)
    per = chips // count
    core = core_ref[0]
    for ref, half in ((own_ref, core), (sibling_ref, 1 - core)):
        for n in range(count):
            cols = pl.ds(pl.multiple_of((half * count + n) * LANES, LANES), LANES)
            block = ref[n * per : (n + 1) * per].astype(f32)
            block = block.reshape(per * block.shape[1], LANES)
            start = 0
            for out_ref, scale in (
                (go_ref, obs_scale), (gi_ref, obs_scale), (gp_ref, cell_scale), (gd_ref, cell_scale)
            ):
                size = out_ref.shape[0]
                out_ref[:, cols] = block[start : start + size] * scale
                start += round_up(size, 16)


def unpack(core, own, sibling, spec, width, obs_scale, cell_scale):
    return pl.pallas_call(
        functools.partial(unpack_kernel, obs_scale, cell_scale),
        out_shape=tuple(
            jax.ShapeDtypeStruct((rows, width), f32) for rows in (spec, width, width, 9)
        ),
        in_specs=[smem()] + [vmem()] * 2,
        out_specs=(vmem(),) * 4,
        compiler_params=params(8),
        cost_estimate=cost(3),
        name="unpack",
    )(core, own, sibling)


def neighbours(axes, periodic):
    count = lax.axis_size(axes)
    up = [(i, i + 1) for i in range(count - 1)]
    if periodic:
        up.append((count - 1, 0))
    return up, [(t, s) for s, t in up]


LAT = ("x", "core")
CHIPS = ("x", "lon")


def spread(values):
    chips = lax.axis_size(CHIPS)
    values = values.reshape(chips, values.size // (chips * LANES), LANES)
    return lax.all_to_all(values, CHIPS, split_axis=0, concat_axis=0, tiled=True)


def on_device(spectra, owner, cell, w_in, w_out, w_point, w_depth, cotangent):
    tiles = lax.axis_size(LAT) * lax.axis_size("lon")
    rows_here, spec = spectra.shape
    cap = max(2, 2 * rows_here // tiles)
    clat, clon, width = cotangent.shape
    cells = clat * clon
    wide = clon + 16
    spec_wide = round_up(spec + 2, LANES)
    core = lax.axis_index("core").reshape(1)
    east_way, west_way = neighbours("lon", True)
    south_way, north_way = neighbours(LAT, False)

    from_west = lax.ppermute(cotangent[:, -1], "lon", east_way)
    from_east = lax.ppermute(cotangent[:, 0], "lon", west_way)

    outgoing = route(
        owner.reshape(1, rows_here), cell.reshape(1, rows_here), spectra.T, tiles, cap, clon, spec_wide
    )
    outgoing, from_west, from_east, w_in, w_out = lax.optimization_barrier(
        (outgoing, from_west, from_east, w_in, w_out)
    )
    arrived = lax.all_to_all(
        outgoing.reshape(tiles, cap, spec_wide), ("x", "core", "lon"), 0, 0, tiled=True
    ).reshape(tiles * cap, spec_wide)

    fill = jnp.zeros((wide - clon - 2, width), bf16)

    def halo_row(i):
        return jnp.concatenate([cotangent[i], from_east[i, None], fill, from_west[i, None]], axis=0)

    from_north = lax.ppermute(halo_row(clat - 1), LAT, south_way)
    from_south = lax.ppermute(halo_row(0), LAT, north_way)
    cot_t, g_mixed, g_grid = grid_grad(
        cotangent.reshape(cells, width),
        (from_east, from_west, from_north, from_south),
        w_point, w_depth, clat, clon, wide,
    )
    w_in_t = jnp.pad(w_in.T, ((0, 0), (0, spec_wide - spec)))

    out_rows = round_up(2 * width + round_up(spec, 16) + 16, 16 * tiles * LANES // width)
    operands = w_in_t, w_out.T, g_grid, w_out, g_mixed, cot_t
    mine, other, east, west, grid, mix_ext = owner_part(
        core, arrived, w_depth, operands, spec, clat, clon, wide, out_rows
    )
    summed = core_sum(mine, other)
    summed, east, west, mix_ext = lax.optimization_barrier((summed, east, west, mix_ext))
    parts = spread(summed)

    left = lax.ppermute(east, "lon", east_way)
    right = lax.ppermute(west, "lon", west_way)
    sent = totals(parts, left, right)
    full = spread(sent)
    line = lax.broadcasted_iota(i32, (clon, width), 0)

    def edge_row(e):
        row = mix_ext[e * wide : e * wide + clon].astype(f32)
        sides = jnp.where(line == 0, left[e], jnp.where(line == clon - 1, right[e], 0.0))
        return (row + sides).astype(bf16)

    top = lax.ppermute(edge_row(clat + 1), LAT, south_way)
    bottom = lax.ppermute(edge_row(0), LAT, north_way)
    latent = finish_latent(grid, mix_ext, (top, bottom, left, right), w_point, clat, clon, wide)

    obs_scale = float((rows_here * tiles) ** -0.5)
    cell_scale = float((cells * tiles) ** -0.5)
    full, latent = lax.optimization_barrier((full, latent))
    sibling = lax.ppermute(full, "core", SWAP)
    grad_in, grad_out, grad_point, grad_depth = unpack(
        core, full, sibling, spec, width, obs_scale, cell_scale
    )
    return latent.reshape(clat, clon, width), grad_in, grad_out, grad_point, grad_depth


def solution(mesh):
    lat, lon = mesh.devices.shape
    fine = Mesh(mesh.devices.reshape(lat // 2, 2, lon), ("x", "core", "lon"))
    everyone = P(("x", "core", "lon"))
    field = P(LAT, "lon", None)
    in_specs = (everyone, everyone, everyone, P(), P(), P(), P(), field)
    out_specs = (field, P(), P(), P(), P())
    return jax.shard_map(
        on_device, mesh=fine, in_specs=in_specs, out_specs=out_specs, check_vma=False
    )
```

```python
import functools

import jax
import jax.numpy as jnp
from jax import lax
from jax.experimental import pallas as pl
from jax.experimental.pallas import tpu as pltpu
from jax.sharding import Mesh
from jax.sharding import PartitionSpec as P

LANES = 128
bf16 = jnp.bfloat16
f32 = jnp.float32
i32 = jnp.int32


def params(mib):
    return pltpu.CompilerParams(vmem_limit_bytes=mib * 1024 * 1024)


def round_up(n, m):
    return -(-n // m) * m


def dot(a, b, dims=(1, 0)):
    return lax.dot_general(
        a, b, (((dims[0],), (dims[1],)), ((), ())), preferred_element_type=f32
    )


def cost(us):
    return pl.CostEstimate(flops=us * 1153500000, bytes_accessed=0, transcendentals=0)


def smem():
    return pl.BlockSpec(memory_space=pltpu.SMEM)


def anywhere():
    return pl.BlockSpec(memory_space=pl.ANY)


def vmem():
    return pl.BlockSpec(memory_space=pltpu.VMEM)


def route_kernel(tiles, n_lon, cap, clon, owner_ref, cell_ref, rows_hbm, out_ref, rows_ref, sem):
    load = pltpu.make_async_copy(rows_hbm, rows_ref, sem)
    load.start()
    spec, n = rows_ref.shape
    head = out_ref.shape[1] - LANES
    owner = owner_ref[...]
    owner = (owner % n_lon) * (tiles // n_lon) + owner // n_lon
    hits = owner == lax.broadcasted_iota(i32, (tiles, n), 0)
    above = lax.broadcasted_iota(i32, (n, n), 0) < lax.broadcasted_iota(i32, (n, n), 1)
    count = dot(hits.astype(f32).astype(bf16), above.astype(f32).astype(bf16))
    rank = jnp.sum(jnp.where(hits, count, 0.0), axis=0, keepdims=True)
    slot = owner * cap + rank.astype(i32)
    cell = cell_ref[...]
    line = lax.broadcasted_iota(i32, (LANES - (spec - head), n), 0)
    high = cell // clon
    spots = jnp.where(line == 0, high, jnp.where(line == 1, cell - high * clon, 0)).astype(f32)
    load.wait()
    last = jnp.concatenate([rows_ref[head:, :].astype(f32), spots], axis=0).astype(bf16)
    first = rows_ref[:head, :]
    step = min(256, tiles * cap)

    def body(t, carry):
        base = t * step
        place = lax.broadcasted_iota(i32, (step, n), 0) + base
        pick = (slot == place).astype(f32).astype(bf16)
        at = pl.ds(pl.multiple_of(base, step), step)
        out_ref[at, :head] = dot(pick, first, (1, 1)).astype(bf16)
        out_ref[at, head:] = dot(pick, last, (1, 1)).astype(bf16)
        return carry

    lax.fori_loop(0, tiles * cap // step, body, 0)


def route(owner, cell, rows, tiles, n_lon, cap, clon, spec_wide):
    return pl.pallas_call(
        functools.partial(route_kernel, tiles, n_lon, cap, clon),
        out_shape=jax.ShapeDtypeStruct((tiles * cap, spec_wide), bf16),
        in_specs=[vmem()] * 2 + [anywhere()],
        out_specs=vmem(),
        scratch_shapes=[pltpu.VMEM(rows.shape, rows.dtype), pltpu.SemaphoreType.DMA],
        compiler_params=params(60),
        cost_estimate=cost(3),
        name="route",
    )(owner, cell, rows)


GROUPS = 8
CHUNK = 8 * GROUPS


def column_of(place, per):
    return per * (place % GROUPS) + place // GROUPS


def place_of(column, per):
    return GROUPS * (column % per) + column // per


def one_hot(wanted, count):
    hit = wanted == lax.broadcasted_iota(i32, (wanted.shape[0], count), 1)
    return hit.astype(f32).astype(bf16)


def grid_grad_kernel(
    clat, clon, wide, cot_ref, east_ref, west_ref, north_ref, south_ref, wp_ref, wd_ref,
    cott_hbm, gm_hbm, gg_hbm, cott_ref, gm_ref, gg_ref, cot_ext, cot_own, east, west, sems,
):
    width = wp_ref.shape[0]
    per = clon // GROUPS
    w_point = wp_ref[...]
    east[...] = east_ref[...].astype(f32)
    west[...] = west_ref[...].astype(f32)
    line = lax.broadcasted_iota(i32, (wide - clon, width), 0)
    place = lax.broadcasted_iota(i32, (wide, 1), 0)
    column = column_of(place, per) - 1
    spread_order = one_hot(jnp.where(column < 0, wide - 1, column), wide)
    ends = jnp.where(place == clon + GROUPS - 1, clon, jnp.where(place == clon + GROUPS, wide - 1, -1))
    point_order = one_hot(jnp.where(place < clon, column_of(place, per), ends), wide)
    puts = [
        pltpu.make_async_copy(source, target, sems.at[i])
        for i, (source, target) in enumerate(
            ((gg_ref, gg_hbm), (gm_ref, gm_hbm), (cott_ref, cott_hbm))
        )
    ]

    def reorder(e, rows):
        ordered = dot(spread_order, rows)
        g = dot(ordered.astype(bf16), w_point, (1, 1)).astype(bf16).astype(f32)
        for n in range(width // LANES):
            gm_ref[n, e] = g[:, n * LANES : (n + 1) * LANES]
        cot_ext[pl.ds(pl.multiple_of(e * wide, 16), wide), :] = dot(point_order, rows).astype(bf16)
        return ordered

    def matmul(i, carry):
        at = pl.ds(pl.multiple_of(i * clon, 16), clon)
        tail = jnp.where(
            line == 0, east[pl.ds(i, 1), :], jnp.where(line == wide - clon - 1, west[pl.ds(i, 1), :], 0.0)
        )
        ordered = reorder(i + 1, jnp.concatenate([cot_ref[at, :], tail.astype(bf16)], axis=0))
        cot_own[at, :] = ordered[GROUPS : GROUPS + clon].astype(bf16)
        return carry

    reorder(0, north_ref[...])
    reorder(clat + 1, south_ref[...])
    used = (clat + 2) * wide
    cot_ext[used:, :] = jnp.zeros((cot_ext.shape[0] - used, width), bf16)
    lax.fori_loop(0, clat, matmul, 0)
    puts[1].start()

    def conv(i, carry):
        for n in range(width // LANES):
            cols = slice(n * LANES, (n + 1) * LANES)
            for c in range(0, clon, CHUNK):
                at = pl.ds(pl.multiple_of(i * clon + c, 16), CHUNK)
                out = cot_own[at, cols].astype(f32)
                for a in range(3):
                    g = gm_ref[n, i + 2 - a, c : c + CHUNK + 2 * GROUPS, :]
                    for b in range(3):
                        k = 3 * a + b
                        first = GROUPS * (2 - b)
                        out = out + wd_ref[k : k + 1, cols] * g[first : first + CHUNK]
                gg_ref[at, cols] = out.astype(bf16)
        return carry

    lax.fori_loop(0, clat, conv, 0)
    puts[0].start()

    def transpose(k, carry):
        at = pl.ds(pl.multiple_of(k * LANES, LANES), LANES)
        cott_ref[:, at] = cot_ext[at, :].T
        return carry

    lax.fori_loop(0, cot_ext.shape[0] // LANES, transpose, 0)
    puts[2].start()
    for put in puts:
        put.wait()


def grid_grad(cot, sides, w_point, w_depth, clat, clon, wide):
    width = w_point.shape[0]
    ext_rows = round_up((clat + 2) * wide, LANES)
    outs = (
        jax.ShapeDtypeStruct((width, ext_rows), bf16),
        jax.ShapeDtypeStruct((width // LANES, clat + 2, wide, LANES), f32),
        jax.ShapeDtypeStruct((clat * clon, width), bf16),
    )
    return pl.pallas_call(
        functools.partial(grid_grad_kernel, clat, clon, wide),
        out_shape=outs,
        in_specs=[vmem()] * 7,
        out_specs=(anywhere(),) * 3,
        scratch_shapes=[pltpu.VMEM(x.shape, x.dtype) for x in outs]
        + [pltpu.VMEM((ext_rows, width), bf16), pltpu.VMEM((clat * clon, width), bf16)]
        + [pltpu.VMEM((clat, width), f32)] * 2
        + [pltpu.SemaphoreType.DMA((3,))],
        compiler_params=params(58),
        cost_estimate=cost(10),
        name="grid_grad",
    )(cot, *sides, w_point, w_depth)


def write_halves(core, total, start, mine_ref, other_ref, first=0, size=None):
    size = total.shape[0] if size is None else size
    half = total.shape[1] // 2
    for ref, base in ((mine_ref, core * half), (other_ref, (1 - core) * half)):
        for n in range(half // LANES):
            cols = pl.ds(pl.multiple_of(base + n * LANES, LANES), LANES)
            ref[n, start : start + size, :] = total[first : first + size, cols].astype(bf16)


def clear_tail(start, *refs):
    for ref in refs:
        unused = ref.shape[1] - start
        if unused:
            ref[:, start:, :] = jnp.zeros((ref.shape[0], unused, LANES), bf16)


def start_loads(sources, targets, sems):
    loads = [
        pltpu.make_async_copy(source, target, sems.at[i])
        for i, (source, target) in enumerate(zip(sources, targets))
    ]
    for load in loads:
        load.start()
    return loads


def owner_kernel(
    spec, clat, clon, wide, core_ref, rows_ref, wd_ref, wit_hbm, wot_hbm, gg_hbm, wo_hbm, gm_hbm, cott_hbm,
    mine_ref, other_ref, east_out, west_out, grid_hbm, mix_hbm,
    wit_ref, wot_ref, gg_ref, wo_ref, gm_ref, cott_ref,
    emb_ref, gi, gi_out, go, wide_ref, grid_ref, mix_ref, east_ref, west_ref, gp, gd, sems,
):
    loads = start_loads((wit_hbm, wot_hbm), (wit_ref, wot_ref), sems)
    put_grid = pltpu.make_async_copy(grid_ref, grid_hbm, sems.at[6])
    put_mix = pltpu.make_async_copy(mix_ref, mix_hbm, sems.at[7])
    core = core_ref[0]
    slots, spec_wide = rows_ref.shape
    cells, width = gg_ref.shape
    blocks = width // LANES
    step = min(512, slots)

    for t in range(slots // step):
        at = slice(t * step, (t + 1) * step)
        rows = rows_ref[at, :]
        line = rows[:, spec : spec + 1].astype(f32).astype(i32)
        column = rows[:, spec + 1 : spec + 2].astype(f32).astype(i32)
        hits = one_hot(line * clon + place_of(column, clon // GROUPS), cells)
        if t == 0:
            loads[0].wait()
            loads += start_loads((gg_hbm, wo_hbm), (gg_ref, wo_ref), sems.at[pl.ds(2, 2)])
        preact = dot(wit_ref[...], rows, (1, 1))
        sig = 1.0 / (1.0 + jnp.exp(-preact))
        hidden = (preact * sig).astype(bf16)
        if t == 0:
            loads[1].wait()
        emb_ref[:, at] = dot(wot_ref[...], hidden).astype(bf16)
        if t == 0:
            loads[2].wait()
        g_emb = dot(hits, gg_ref[...]).astype(bf16)
        g_out = dot(hidden, g_emb)
        if t == 0:
            loads[3].wait()
            late = start_loads((gm_hbm, cott_hbm), (gm_ref, cott_ref), sems.at[pl.ds(4, 2)])
        g_hid = dot(wo_ref[...], g_emb, (1, 1))
        g_pre = (g_hid * (sig * (1.0 + preact * (1.0 - sig)))).astype(bf16)
        g_in = dot(g_pre, rows)
        if t == 0:
            go[...] = g_out
            gi[...] = g_in
        else:
            go[...] += g_out
            gi[...] += g_in

    last = rows_ref[:, spec_wide - LANES :]
    col = spec - (spec_wide - LANES)
    lane = lax.broadcasted_iota(i32, (16, LANES), 1)
    pick = jnp.where(lane == col, float(clon), jnp.where(lane == col + 1, 1.0, 0.0)).astype(bf16)
    cell = dot(pick, last, (1, 1))[0:1, :].astype(i32)
    lines = 4
    place = lax.broadcasted_iota(i32, (wide, 1), 0)
    column = column_of(place, clon // GROUPS) - 1
    inside = (column >= 0) & (column < clon)
    wanted = [jnp.where(inside, column + k * clon, -clat * clon) for k in range(lines)]
    wanted = jnp.concatenate(wanted, axis=0)
    empty = jnp.zeros((blocks, 2, wide, LANES), f32)
    wide_ref[:, 0:2] = empty
    wide_ref[:, clat + 2 :] = empty
    gd[...] = jnp.zeros_like(gd)
    used = (clat + 2) * wide
    mix_ref[used:, :] = jnp.zeros((mix_ref.shape[0] - used, width), bf16)

    def bins(t, carry):
        hits = (cell == wanted + t * (lines * clon)).astype(f32).astype(bf16)
        grid = dot(hits, emb_ref[...], (1, 1)).astype(bf16).astype(f32)
        for k in range(lines):
            line = grid[k * wide : (k + 1) * wide]
            for n in range(blocks):
                wide_ref[n, t * lines + k + 2] = line[:, n * LANES : (n + 1) * LANES]
            at = pl.ds(pl.multiple_of((t * lines + k) * clon, 16), clon)
            grid_ref[at, :] = line[GROUPS : GROUPS + clon].astype(bf16)
        return carry

    lax.fori_loop(0, clat // lines, bins, 0)
    put_grid.start()
    late[0].wait()
    group = lax.broadcasted_iota(i32, (GROUPS, LANES), 0)

    def conv(e, carry):
        for n in range(blocks):
            cols = slice(n * LANES, (n + 1) * LANES)
            weights = [wd_ref[k : k + 1, cols] for k in range(9)]
            taps = [gd[8 * k : 8 * k + 8, cols] for k in range(9)]
            for c in range(0, clon, CHUNK):
                grads = gm_ref[n, e, c : c + CHUNK + 2 * GROUPS, :]
                mixed = None
                for a in range(3):
                    cells = wide_ref[n, e + a, c : c + CHUNK + 2 * GROUPS, :]
                    middle = cells[GROUPS : GROUPS + CHUNK]
                    for b in range(3):
                        k = 3 * a + b
                        term = weights[k] * cells[GROUPS * b : GROUPS * b + CHUNK]
                        mixed = term if mixed is None else mixed + term
                        first = GROUPS * (2 - b)
                        part = (grads[first : first + CHUNK] * middle).reshape(CHUNK // 8, 8, LANES)
                        taps[k] = taps[k] + jnp.sum(part, axis=0)
                out_at = pl.ds(pl.multiple_of(e * wide + c, 16), CHUNK)
                mix_ref[out_at, cols] = mixed.astype(bf16)
            for k in range(9):
                gd[8 * k : 8 * k + 8, cols] = taps[k]
            ends = []
            for b, at, valid in ((0, clon, GROUPS - 1), (2, GROUPS, 0)):
                end = None
                for a in range(3):
                    term = weights[3 * a + b] * wide_ref[n, e + a, at : at + GROUPS, :]
                    end = term if end is None else end + term
                ends.append(jnp.where(group == valid, end, 0.0))
            east_ref[e, :, cols] = ends[0]
            west_ref[e, :, cols] = ends[1]
            out_at = pl.ds(pl.multiple_of(e * wide + clon, 16), wide - clon)
            mix_ref[out_at, cols] = jnp.concatenate(ends, axis=0).astype(bf16)
        return carry

    lax.fori_loop(0, clat + 2, conv, 0, unroll=2)
    put_mix.start()
    late[1].wait()
    gp[...] = dot(cott_ref[...], mix_ref[...]).astype(bf16).T
    gi_out[...] = gi[...].astype(bf16).T
    east_out[...] = east_ref[:, GROUPS - 1, :]
    west_out[...] = west_ref[:, 0, :]
    taps = [jnp.sum(gd[8 * k : 8 * k + 8, :], axis=0, keepdims=True) for k in range(9)]
    gd[0:16, :] = jnp.concatenate(taps + [jnp.zeros((7, width), f32)], axis=0)
    start = 0
    for total, size in ((go, width), (gi_out, round_up(spec, 16)), (gp, width), (gd, 16)):
        write_halves(core, total, start, mine_ref, other_ref, 0, size)
        start += size
    clear_tail(start, mine_ref, other_ref)
    put_grid.wait()
    put_mix.wait()


def owner_part(core, rows, w_depth, operands, spec, clat, clon, wide, out_rows):
    slots, spec_wide = rows.shape
    width = w_depth.shape[1]
    half = jax.ShapeDtypeStruct((width // LANES // 2, out_rows, LANES), bf16)
    column = jax.ShapeDtypeStruct((clat + 2, width), f32)
    grid = jax.ShapeDtypeStruct((clat * clon, width), bf16)
    ext = jax.ShapeDtypeStruct(operands[-1].shape[::-1], bf16)
    return pl.pallas_call(
        functools.partial(owner_kernel, spec, clat, clon, wide),
        out_shape=(half, half, column, column, grid, ext),
        in_specs=[smem()] + [vmem()] * 2 + [anywhere()] * len(operands),
        out_specs=(vmem(),) * 4 + (anywhere(),) * 2,
        scratch_shapes=[pltpu.VMEM(x.shape, x.dtype) for x in operands]
        + [
            pltpu.VMEM((width, slots), bf16),
            pltpu.VMEM((width, spec_wide), f32),
            pltpu.VMEM((spec_wide, width), bf16),
            pltpu.VMEM((width, width), f32),
            pltpu.VMEM((width // LANES, clat + 4, wide, LANES), f32),
            pltpu.VMEM(grid.shape, bf16),
            pltpu.VMEM(ext.shape, bf16),
            pltpu.VMEM((clat + 2, GROUPS, width), f32),
            pltpu.VMEM((clat + 2, GROUPS, width), f32),
            pltpu.VMEM((width, width), bf16),
            pltpu.VMEM((72, width), f32),
            pltpu.SemaphoreType.DMA((8,)),
        ],
        compiler_params=params(48),
        cost_estimate=cost(21),
        name="owner",
    )(core, rows, w_depth, *operands)


def latent_kernel(
    clat, clon, wide, grid_ref, mix_ref, top_ref, bottom_ref, left_ref, right_ref, wp_ref, out_ref
):
    width = wp_ref.shape[0]
    w_point = wp_ref[...]
    line = lax.broadcasted_iota(i32, (clon, width), 0)
    column = lax.broadcasted_iota(i32, (clon, 1), 0)
    natural_order = one_hot(place_of(column, clon // GROUPS), clon)

    def body(i, carry):
        at = pl.ds(pl.multiple_of(i * clon, 16), clon)
        mixed = mix_ref[pl.ds(pl.multiple_of((i + 1) * wide, 16), clon), :].astype(f32)
        mixed = mixed + (i == 0).astype(f32) * top_ref[...].astype(f32)
        mixed = mixed + (i == clat - 1).astype(f32) * bottom_ref[...].astype(f32)
        mixed = mixed + jnp.where(
            line == 0, left_ref[pl.ds(i + 1, 1), :], jnp.where(line == clon - 1, right_ref[pl.ds(i + 1, 1), :], 0.0)
        )
        out = grid_ref[at, :].astype(f32) + dot(mixed.astype(bf16), w_point)
        out_ref[at, :] = dot(natural_order, out.astype(bf16)).astype(bf16)
        return carry

    lax.fori_loop(0, clat, body, 0, unroll=2)


def finish_latent(grid, mix_ext, sides, w_point, clat, clon, wide):
    return pl.pallas_call(
        functools.partial(latent_kernel, clat, clon, wide),
        out_shape=jax.ShapeDtypeStruct(grid.shape, bf16),
        in_specs=[vmem()] * 7,
        out_specs=vmem(),
        compiler_params=params(6),
        cost_estimate=cost(5),
        name="latent",
    )(grid, mix_ext, *sides, w_point)


SWAP = [(0, 1), (1, 0)]


def add_kernel(mine_ref, got_ref, out_ref):
    out_ref[...] = (mine_ref[...].astype(f32) + got_ref[...].astype(f32)).astype(bf16)


def core_sum(mine, other):
    return pl.pallas_call(
        add_kernel,
        out_shape=jax.ShapeDtypeStruct(mine.shape, bf16),
        in_specs=[vmem()] * 2,
        out_specs=vmem(),
        compiler_params=params(8),
        cost_estimate=cost(1),
        name="core_sum",
    )(mine, lax.ppermute(other, "core", SWAP))


def totals_kernel(parts_ref, *refs):
    out_ref = refs[-1]
    total = jnp.sum(parts_ref[...].astype(f32), axis=0).astype(bf16)
    out_ref[...] = jnp.broadcast_to(total[None], parts_ref.shape)


def totals(parts, *after):
    return pl.pallas_call(
        totals_kernel,
        out_shape=jax.ShapeDtypeStruct(parts.shape, bf16),
        in_specs=[vmem()] + [anywhere()] * len(after),
        out_specs=vmem(),
        compiler_params=params(8),
        cost_estimate=cost(1),
        name="totals",
    )(parts, *after)


def unpack_kernel(
    obs_scale, cell_scale, core_ref, own_ref, sibling_ref, gi_ref, go_ref, gp_ref, gd_ref
):
    width = gi_ref.shape[1]
    chips = own_ref.shape[0]
    count = width // (2 * LANES)
    per = chips // count
    core = core_ref[0]
    for ref, half in ((own_ref, core), (sibling_ref, 1 - core)):
        for n in range(count):
            cols = pl.ds(pl.multiple_of((half * count + n) * LANES, LANES), LANES)
            block = ref[n * per : (n + 1) * per].astype(f32)
            block = block.reshape(per * block.shape[1], LANES)
            start = 0
            for out_ref, scale in (
                (go_ref, obs_scale), (gi_ref, obs_scale), (gp_ref, cell_scale), (gd_ref, cell_scale)
            ):
                size = out_ref.shape[0]
                out_ref[:, cols] = block[start : start + size] * scale
                start += round_up(size, 16)


def unpack(core, own, sibling, spec, width, obs_scale, cell_scale):
    return pl.pallas_call(
        functools.partial(unpack_kernel, obs_scale, cell_scale),
        out_shape=tuple(
            jax.ShapeDtypeStruct((rows, width), f32) for rows in (spec, width, width, 9)
        ),
        in_specs=[smem()] + [vmem()] * 2,
        out_specs=(vmem(),) * 4,
        compiler_params=params(8),
        cost_estimate=cost(3),
        name="unpack",
    )(core, own, sibling)


def neighbours(axes, periodic):
    count = lax.axis_size(axes)
    up = [(i, i + 1) for i in range(count - 1)]
    if periodic:
        up.append((count - 1, 0))
    return up, [(t, s) for s, t in up]


LAT = ("x", "core")
CHIPS = ("lon", "x")


def spread(values):
    chips = lax.axis_size(CHIPS)
    values = values.reshape(chips, values.size // (chips * LANES), LANES)
    return lax.all_to_all(values, CHIPS, split_axis=0, concat_axis=0, tiled=True)


def on_device(spectra, owner, cell, w_in, w_out, w_point, w_depth, cotangent):
    tiles = lax.axis_size(LAT) * lax.axis_size("lon")
    rows_here, spec = spectra.shape
    cap = max(2, 2 * rows_here // tiles)
    clat, clon, width = cotangent.shape
    cells = clat * clon
    wide = clon + 16
    spec_wide = round_up(spec + 2, LANES)
    core = lax.axis_index("core").reshape(1)
    east_way, west_way = neighbours("lon", True)
    south_way, north_way = neighbours(LAT, False)

    from_west = lax.ppermute(cotangent[:, -1], "lon", east_way)
    from_east = lax.ppermute(cotangent[:, 0], "lon", west_way)

    outgoing = route(
        owner.reshape(1, rows_here), cell.reshape(1, rows_here), spectra.T,
        tiles, lax.axis_size("lon"), cap, clon, spec_wide,
    )
    outgoing, from_west, from_east, w_in, w_out = lax.optimization_barrier(
        (outgoing, from_west, from_east, w_in, w_out)
    )
    arrived = lax.all_to_all(
        outgoing.reshape(tiles, cap, spec_wide), ("lon", "x", "core"), 0, 0, tiled=True
    ).reshape(tiles * cap, spec_wide)

    fill = jnp.zeros((wide - clon - 2, width), bf16)

    def halo_row(i):
        return jnp.concatenate([cotangent[i], from_east[i, None], fill, from_west[i, None]], axis=0)

    from_north = lax.ppermute(halo_row(clat - 1), LAT, south_way)
    from_south = lax.ppermute(halo_row(0), LAT, north_way)
    cot_t, g_mixed, g_grid = grid_grad(
        cotangent.reshape(cells, width),
        (from_east, from_west, from_north, from_south),
        w_point, w_depth, clat, clon, wide,
    )
    w_in_t = jnp.pad(w_in.T, ((0, 0), (0, spec_wide - spec)))

    out_rows = round_up(2 * width + round_up(spec, 16) + 16, 16 * tiles * LANES // width)
    operands = w_in_t, w_out.T, g_grid, w_out, g_mixed, cot_t
    mine, other, east, west, grid, mix_ext = owner_part(
        core, arrived, w_depth, operands, spec, clat, clon, wide, out_rows
    )
    summed = core_sum(mine, other)
    summed, east, west, mix_ext = lax.optimization_barrier((summed, east, west, mix_ext))
    parts = spread(summed)

    left = lax.ppermute(east, "lon", east_way)
    right = lax.ppermute(west, "lon", west_way)
    sent = totals(parts, left, right)
    full = spread(sent)
    line = lax.broadcasted_iota(i32, (clon, width), 0)

    def edge_row(e):
        row = mix_ext[e * wide : e * wide + clon].astype(f32)
        sides = jnp.where(line == 0, left[e], jnp.where(line == clon - 1, right[e], 0.0))
        return (row + sides).astype(bf16)

    top = lax.ppermute(edge_row(clat + 1), LAT, south_way)
    bottom = lax.ppermute(edge_row(0), LAT, north_way)
    latent = finish_latent(grid, mix_ext, (top, bottom, left, right), w_point, clat, clon, wide)

    obs_scale = float((rows_here * tiles) ** -0.5)
    cell_scale = float((cells * tiles) ** -0.5)
    full, latent = lax.optimization_barrier((full, latent))
    sibling = lax.ppermute(full, "core", SWAP)
    grad_in, grad_out, grad_point, grad_depth = unpack(
        core, full, sibling, spec, width, obs_scale, cell_scale
    )
    return latent.reshape(clat, clon, width), grad_in, grad_out, grad_point, grad_depth


def solution(mesh):
    lat, lon = mesh.devices.shape
    fine = Mesh(mesh.devices.reshape(lat // 2, 2, lon), ("x", "core", "lon"))
    everyone = P(("x", "core", "lon"))
    field = P(LAT, "lon", None)
    in_specs = (everyone, everyone, everyone, P(), P(), P(), P(), field)
    out_specs = (field, P(), P(), P(), P())
    return jax.shard_map(
        on_device, mesh=fine, in_specs=in_specs, out_specs=out_specs, check_vma=False
    )
```

```python
import functools

import jax
import jax.numpy as jnp
from jax import lax
from jax.experimental import pallas as pl
from jax.experimental.pallas import tpu as pltpu
from jax.sharding import Mesh
from jax.sharding import PartitionSpec as P

LANES = 128
bf16 = jnp.bfloat16
f32 = jnp.float32
i32 = jnp.int32


def params(mib):
    return pltpu.CompilerParams(vmem_limit_bytes=mib * 1024 * 1024)


def round_up(n, m):
    return -(-n // m) * m


def dot(a, b, dims=(1, 0)):
    return lax.dot_general(
        a, b, (((dims[0],), (dims[1],)), ((), ())), preferred_element_type=f32
    )


def cost(us):
    return pl.CostEstimate(flops=us * 1153500000, bytes_accessed=0, transcendentals=0)


def smem():
    return pl.BlockSpec(memory_space=pltpu.SMEM)


def anywhere():
    return pl.BlockSpec(memory_space=pl.ANY)


def vmem():
    return pl.BlockSpec(memory_space=pltpu.VMEM)


def route_kernel(tiles, n_lon, cap, clon, owner_ref, cell_ref, rows_ref, out_ref):
    spec, n = rows_ref.shape
    head = out_ref.shape[1] - LANES
    owner = owner_ref[...]
    owner = (owner % n_lon) * (tiles // n_lon) + owner // n_lon
    hits = owner == lax.broadcasted_iota(i32, (tiles, n), 0)
    above = lax.broadcasted_iota(i32, (n, n), 0) < lax.broadcasted_iota(i32, (n, n), 1)
    count = dot(hits.astype(f32).astype(bf16), above.astype(f32).astype(bf16))
    rank = jnp.sum(jnp.where(hits, count, 0.0), axis=0, keepdims=True)
    slot = owner * cap + rank.astype(i32)
    cell = cell_ref[...]
    line = lax.broadcasted_iota(i32, (LANES - (spec - head), n), 0)
    high = cell // clon
    spots = jnp.where(line == 0, high, jnp.where(line == 1, cell - high * clon, 0)).astype(f32)
    last = jnp.concatenate([rows_ref[head:, :].astype(f32), spots], axis=0).astype(bf16)
    first = rows_ref[:head, :]
    step = min(256, tiles * cap)

    def body(t, carry):
        base = t * step
        place = lax.broadcasted_iota(i32, (step, n), 0) + base
        pick = (slot == place).astype(f32).astype(bf16)
        at = pl.ds(pl.multiple_of(base, step), step)
        out_ref[at, :head] = dot(pick, first, (1, 1)).astype(bf16)
        out_ref[at, head:] = dot(pick, last, (1, 1)).astype(bf16)
        return carry

    lax.fori_loop(0, tiles * cap // step, body, 0)


def route(owner, cell, rows, tiles, n_lon, cap, clon, spec_wide):
    return pl.pallas_call(
        functools.partial(route_kernel, tiles, n_lon, cap, clon),
        out_shape=jax.ShapeDtypeStruct((tiles * cap, spec_wide), bf16),
        in_specs=[vmem()] * 3,
        out_specs=vmem(),
        compiler_params=params(60),
        cost_estimate=cost(3),
        name="route",
    )(owner, cell, rows)


GROUPS = 8
CHUNK = 8 * GROUPS


def column_of(place, per):
    return per * (place % GROUPS) + place // GROUPS


def place_of(column, per):
    return GROUPS * (column % per) + column // per


def one_hot(wanted, count):
    hit = wanted == lax.broadcasted_iota(i32, (wanted.shape[0], count), 1)
    return hit.astype(f32).astype(bf16)


def grid_grad_kernel(
    clat, clon, wide, cot_ref, east_ref, west_ref, north_ref, south_ref, wp_ref, wd_ref,
    cott_hbm, gm_hbm, gg_hbm, cott_ref, gm_ref, gg_ref, cot_ext, cot_own, east, west, sems,
):
    width = wp_ref.shape[0]
    per = clon // GROUPS
    w_point = wp_ref[...]
    east[...] = east_ref[...].astype(f32)
    west[...] = west_ref[...].astype(f32)
    line = lax.broadcasted_iota(i32, (wide - clon, width), 0)
    place = lax.broadcasted_iota(i32, (wide, 1), 0)
    column = column_of(place, per) - 1
    spread_order = one_hot(jnp.where(column < 0, wide - 1, column), wide)
    ends = jnp.where(place == clon + GROUPS - 1, clon, jnp.where(place == clon + GROUPS, wide - 1, -1))
    point_order = one_hot(jnp.where(place < clon, column_of(place, per), ends), wide)
    puts = [
        pltpu.make_async_copy(source, target, sems.at[i])
        for i, (source, target) in enumerate(
            ((gg_ref, gg_hbm), (gm_ref, gm_hbm), (cott_ref, cott_hbm))
        )
    ]

    def reorder(e, rows):
        ordered = dot(spread_order, rows)
        g = dot(ordered.astype(bf16), w_point, (1, 1)).astype(bf16).astype(f32)
        for n in range(width // LANES):
            gm_ref[n, e] = g[:, n * LANES : (n + 1) * LANES]
        cot_ext[pl.ds(pl.multiple_of(e * wide, 16), wide), :] = dot(point_order, rows).astype(bf16)
        return ordered

    def matmul(i, carry):
        at = pl.ds(pl.multiple_of(i * clon, 16), clon)
        tail = jnp.where(
            line == 0, east[pl.ds(i, 1), :], jnp.where(line == wide - clon - 1, west[pl.ds(i, 1), :], 0.0)
        )
        ordered = reorder(i + 1, jnp.concatenate([cot_ref[at, :], tail.astype(bf16)], axis=0))
        cot_own[at, :] = ordered[GROUPS : GROUPS + clon].astype(bf16)
        return carry

    reorder(0, north_ref[...])
    reorder(clat + 1, south_ref[...])
    used = (clat + 2) * wide
    cot_ext[used:, :] = jnp.zeros((cot_ext.shape[0] - used, width), bf16)
    lax.fori_loop(0, clat, matmul, 0)
    puts[1].start()

    def conv(i, carry):
        for n in range(width // LANES):
            cols = slice(n * LANES, (n + 1) * LANES)
            for c in range(0, clon, CHUNK):
                at = pl.ds(pl.multiple_of(i * clon + c, 16), CHUNK)
                out = cot_own[at, cols].astype(f32)
                for a in range(3):
                    g = gm_ref[n, i + 2 - a, c : c + CHUNK + 2 * GROUPS, :]
                    for b in range(3):
                        k = 3 * a + b
                        first = GROUPS * (2 - b)
                        out = out + wd_ref[k : k + 1, cols] * g[first : first + CHUNK]
                gg_ref[at, cols] = out.astype(bf16)
        return carry

    lax.fori_loop(0, clat, conv, 0)
    puts[0].start()

    def transpose(k, carry):
        at = pl.ds(pl.multiple_of(k * LANES, LANES), LANES)
        cott_ref[:, at] = cot_ext[at, :].T
        return carry

    lax.fori_loop(0, cot_ext.shape[0] // LANES, transpose, 0)
    puts[2].start()
    for put in puts:
        put.wait()


def grid_grad(cot, sides, w_point, w_depth, clat, clon, wide):
    width = w_point.shape[0]
    ext_rows = round_up((clat + 2) * wide, LANES)
    outs = (
        jax.ShapeDtypeStruct((width, ext_rows), bf16),
        jax.ShapeDtypeStruct((width // LANES, clat + 2, wide, LANES), f32),
        jax.ShapeDtypeStruct((clat * clon, width), bf16),
    )
    return pl.pallas_call(
        functools.partial(grid_grad_kernel, clat, clon, wide),
        out_shape=outs,
        in_specs=[vmem()] * 7,
        out_specs=(anywhere(),) * 3,
        scratch_shapes=[pltpu.VMEM(x.shape, x.dtype) for x in outs]
        + [pltpu.VMEM((ext_rows, width), bf16), pltpu.VMEM((clat * clon, width), bf16)]
        + [pltpu.VMEM((clat, width), f32)] * 2
        + [pltpu.SemaphoreType.DMA((3,))],
        compiler_params=params(58),
        cost_estimate=cost(10),
        name="grid_grad",
    )(cot, *sides, w_point, w_depth)


def write_halves(core, total, start, mine_ref, other_ref, first=0, size=None):
    size = total.shape[0] if size is None else size
    half = total.shape[1] // 2
    for ref, base in ((mine_ref, core * half), (other_ref, (1 - core) * half)):
        for n in range(half // LANES):
            cols = pl.ds(pl.multiple_of(base + n * LANES, LANES), LANES)
            ref[n, start : start + size, :] = total[first : first + size, cols].astype(bf16)


def clear_tail(start, *refs):
    for ref in refs:
        unused = ref.shape[1] - start
        if unused:
            ref[:, start:, :] = jnp.zeros((ref.shape[0], unused, LANES), bf16)


def start_loads(sources, targets, sems):
    loads = [
        pltpu.make_async_copy(source, target, sems.at[i])
        for i, (source, target) in enumerate(zip(sources, targets))
    ]
    for load in loads:
        load.start()
    return loads


def owner_kernel(
    spec, clat, clon, wide, core_ref, rows_ref, wd_ref, wit_hbm, wot_hbm, gg_hbm, wo_hbm, gm_hbm, cott_hbm,
    mine_ref, other_ref, east_out, west_out, grid_hbm, mix_hbm,
    wit_ref, wot_ref, gg_ref, wo_ref, gm_ref, cott_ref,
    emb_ref, gi, gi_out, go, wide_ref, grid_ref, mix_ref, east_ref, west_ref, gp, gd, sems,
):
    loads = start_loads((wit_hbm, wot_hbm), (wit_ref, wot_ref), sems)
    put_grid = pltpu.make_async_copy(grid_ref, grid_hbm, sems.at[6])
    put_mix = pltpu.make_async_copy(mix_ref, mix_hbm, sems.at[7])
    core = core_ref[0]
    slots, spec_wide = rows_ref.shape
    cells, width = gg_ref.shape
    blocks = width // LANES
    step = min(512, slots)

    for t in range(slots // step):
        at = slice(t * step, (t + 1) * step)
        rows = rows_ref[at, :]
        line = rows[:, spec : spec + 1].astype(f32).astype(i32)
        column = rows[:, spec + 1 : spec + 2].astype(f32).astype(i32)
        hits = one_hot(line * clon + place_of(column, clon // GROUPS), cells)
        if t == 0:
            loads[0].wait()
            loads += start_loads((gg_hbm, wo_hbm), (gg_ref, wo_ref), sems.at[pl.ds(2, 2)])
        preact = dot(wit_ref[...], rows, (1, 1))
        sig = 1.0 / (1.0 + jnp.exp(-preact))
        hidden = (preact * sig).astype(bf16)
        if t == 0:
            loads[1].wait()
        emb_ref[:, at] = dot(wot_ref[...], hidden).astype(bf16)
        if t == 0:
            loads[2].wait()
        g_emb = dot(hits, gg_ref[...]).astype(bf16)
        g_out = dot(hidden, g_emb)
        if t == 0:
            loads[3].wait()
            late = start_loads((gm_hbm, cott_hbm), (gm_ref, cott_ref), sems.at[pl.ds(4, 2)])
        g_hid = dot(wo_ref[...], g_emb, (1, 1))
        g_pre = (g_hid * (sig * (1.0 + preact * (1.0 - sig)))).astype(bf16)
        g_in = dot(g_pre, rows)
        if t == 0:
            go[...] = g_out
            gi[...] = g_in
        else:
            go[...] += g_out
            gi[...] += g_in

    last = rows_ref[:, spec_wide - LANES :]
    col = spec - (spec_wide - LANES)
    lane = lax.broadcasted_iota(i32, (16, LANES), 1)
    pick = jnp.where(lane == col, float(clon), jnp.where(lane == col + 1, 1.0, 0.0)).astype(bf16)
    cell = dot(pick, last, (1, 1))[0:1, :].astype(i32)
    lines = 4
    place = lax.broadcasted_iota(i32, (wide, 1), 0)
    column = column_of(place, clon // GROUPS) - 1
    inside = (column >= 0) & (column < clon)
    wanted = [jnp.where(inside, column + k * clon, -clat * clon) for k in range(lines)]
    wanted = jnp.concatenate(wanted, axis=0)
    empty = jnp.zeros((blocks, 2, wide, LANES), f32)
    wide_ref[:, 0:2] = empty
    wide_ref[:, clat + 2 :] = empty
    gd[...] = jnp.zeros_like(gd)
    used = (clat + 2) * wide
    mix_ref[used:, :] = jnp.zeros((mix_ref.shape[0] - used, width), bf16)

    def bins(t, carry):
        hits = (cell == wanted + t * (lines * clon)).astype(f32).astype(bf16)
        grid = dot(hits, emb_ref[...], (1, 1)).astype(bf16).astype(f32)
        for k in range(lines):
            line = grid[k * wide : (k + 1) * wide]
            for n in range(blocks):
                wide_ref[n, t * lines + k + 2] = line[:, n * LANES : (n + 1) * LANES]
            at = pl.ds(pl.multiple_of((t * lines + k) * clon, 16), clon)
            grid_ref[at, :] = line[GROUPS : GROUPS + clon].astype(bf16)
        return carry

    lax.fori_loop(0, clat // lines, bins, 0)
    put_grid.start()
    late[0].wait()
    group = lax.broadcasted_iota(i32, (GROUPS, LANES), 0)

    def conv(e, carry):
        for n in range(blocks):
            cols = slice(n * LANES, (n + 1) * LANES)
            weights = [wd_ref[k : k + 1, cols] for k in range(9)]
            taps = [gd[8 * k : 8 * k + 8, cols] for k in range(9)]
            for c in range(0, clon, CHUNK):
                grads = gm_ref[n, e, c : c + CHUNK + 2 * GROUPS, :]
                mixed = None
                for a in range(3):
                    cells = wide_ref[n, e + a, c : c + CHUNK + 2 * GROUPS, :]
                    middle = cells[GROUPS : GROUPS + CHUNK]
                    for b in range(3):
                        k = 3 * a + b
                        term = weights[k] * cells[GROUPS * b : GROUPS * b + CHUNK]
                        mixed = term if mixed is None else mixed + term
                        first = GROUPS * (2 - b)
                        part = (grads[first : first + CHUNK] * middle).reshape(CHUNK // 8, 8, LANES)
                        taps[k] = taps[k] + jnp.sum(part, axis=0)
                out_at = pl.ds(pl.multiple_of(e * wide + c, 16), CHUNK)
                mix_ref[out_at, cols] = mixed.astype(bf16)
            for k in range(9):
                gd[8 * k : 8 * k + 8, cols] = taps[k]
            ends = []
            for b, at, valid in ((0, clon, GROUPS - 1), (2, GROUPS, 0)):
                end = None
                for a in range(3):
                    term = weights[3 * a + b] * wide_ref[n, e + a, at : at + GROUPS, :]
                    end = term if end is None else end + term
                ends.append(jnp.where(group == valid, end, 0.0))
            east_ref[e, :, cols] = ends[0]
            west_ref[e, :, cols] = ends[1]
            out_at = pl.ds(pl.multiple_of(e * wide + clon, 16), wide - clon)
            mix_ref[out_at, cols] = jnp.concatenate(ends, axis=0).astype(bf16)
        return carry

    lax.fori_loop(0, clat + 2, conv, 0, unroll=2)
    put_mix.start()
    late[1].wait()
    gp[...] = dot(cott_ref[...], mix_ref[...]).astype(bf16).T
    gi_out[...] = gi[...].astype(bf16).T
    east_out[...] = east_ref[:, GROUPS - 1, :]
    west_out[...] = west_ref[:, 0, :]
    taps = [jnp.sum(gd[8 * k : 8 * k + 8, :], axis=0, keepdims=True) for k in range(9)]
    gd[0:16, :] = jnp.concatenate(taps + [jnp.zeros((7, width), f32)], axis=0)
    start = 0
    for total, size in ((go, width), (gi_out, round_up(spec, 16)), (gp, width), (gd, 16)):
        write_halves(core, total, start, mine_ref, other_ref, 0, size)
        start += size
    clear_tail(start, mine_ref, other_ref)
    put_grid.wait()
    put_mix.wait()


def owner_part(core, rows, w_depth, operands, spec, clat, clon, wide, out_rows):
    slots, spec_wide = rows.shape
    width = w_depth.shape[1]
    half = jax.ShapeDtypeStruct((width // LANES // 2, out_rows, LANES), bf16)
    column = jax.ShapeDtypeStruct((clat + 2, width), f32)
    grid = jax.ShapeDtypeStruct((clat * clon, width), bf16)
    ext = jax.ShapeDtypeStruct(operands[-1].shape[::-1], bf16)
    return pl.pallas_call(
        functools.partial(owner_kernel, spec, clat, clon, wide),
        out_shape=(half, half, column, column, grid, ext),
        in_specs=[smem()] + [vmem()] * 2 + [anywhere()] * len(operands),
        out_specs=(vmem(),) * 4 + (anywhere(),) * 2,
        scratch_shapes=[pltpu.VMEM(x.shape, x.dtype) for x in operands]
        + [
            pltpu.VMEM((width, slots), bf16),
            pltpu.VMEM((width, spec_wide), f32),
            pltpu.VMEM((spec_wide, width), bf16),
            pltpu.VMEM((width, width), f32),
            pltpu.VMEM((width // LANES, clat + 4, wide, LANES), f32),
            pltpu.VMEM(grid.shape, bf16),
            pltpu.VMEM(ext.shape, bf16),
            pltpu.VMEM((clat + 2, GROUPS, width), f32),
            pltpu.VMEM((clat + 2, GROUPS, width), f32),
            pltpu.VMEM((width, width), bf16),
            pltpu.VMEM((72, width), f32),
            pltpu.SemaphoreType.DMA((8,)),
        ],
        compiler_params=params(48),
        cost_estimate=cost(21),
        name="owner",
    )(core, rows, w_depth, *operands)


def latent_kernel(
    clat, clon, wide, grid_ref, mix_ref, top_ref, bottom_ref, left_ref, right_ref, wp_ref, out_ref
):
    width = wp_ref.shape[0]
    w_point = wp_ref[...]
    line = lax.broadcasted_iota(i32, (clon, width), 0)
    column = lax.broadcasted_iota(i32, (clon, 1), 0)
    natural_order = one_hot(place_of(column, clon // GROUPS), clon)

    def body(i, carry):
        at = pl.ds(pl.multiple_of(i * clon, 16), clon)
        mixed = mix_ref[pl.ds(pl.multiple_of((i + 1) * wide, 16), clon), :].astype(f32)
        mixed = mixed + (i == 0).astype(f32) * top_ref[...].astype(f32)
        mixed = mixed + (i == clat - 1).astype(f32) * bottom_ref[...].astype(f32)
        mixed = mixed + jnp.where(
            line == 0, left_ref[pl.ds(i + 1, 1), :], jnp.where(line == clon - 1, right_ref[pl.ds(i + 1, 1), :], 0.0)
        )
        out = grid_ref[at, :].astype(f32) + dot(mixed.astype(bf16), w_point)
        out_ref[at, :] = dot(natural_order, out.astype(bf16)).astype(bf16)
        return carry

    lax.fori_loop(0, clat, body, 0, unroll=2)


def finish_latent(grid, mix_ext, sides, w_point, clat, clon, wide):
    return pl.pallas_call(
        functools.partial(latent_kernel, clat, clon, wide),
        out_shape=jax.ShapeDtypeStruct(grid.shape, bf16),
        in_specs=[vmem()] * 7,
        out_specs=vmem(),
        compiler_params=params(6),
        cost_estimate=cost(5),
        name="latent",
    )(grid, mix_ext, *sides, w_point)


SWAP = [(0, 1), (1, 0)]


def add_kernel(mine_ref, got_ref, out_ref):
    out_ref[...] = (mine_ref[...].astype(f32) + got_ref[...].astype(f32)).astype(bf16)


def core_sum(mine, other):
    return pl.pallas_call(
        add_kernel,
        out_shape=jax.ShapeDtypeStruct(mine.shape, bf16),
        in_specs=[vmem()] * 2,
        out_specs=vmem(),
        compiler_params=params(8),
        cost_estimate=cost(1),
        name="core_sum",
    )(mine, lax.ppermute(other, "core", SWAP))


def totals_kernel(parts_ref, *refs):
    out_ref = refs[-1]
    total = jnp.sum(parts_ref[...].astype(f32), axis=0).astype(bf16)
    out_ref[...] = jnp.broadcast_to(total[None], parts_ref.shape)


def totals(parts, *after):
    return pl.pallas_call(
        totals_kernel,
        out_shape=jax.ShapeDtypeStruct(parts.shape, bf16),
        in_specs=[vmem()] + [anywhere()] * len(after),
        out_specs=vmem(),
        compiler_params=params(8),
        cost_estimate=cost(1),
        name="totals",
    )(parts, *after)


def unpack_kernel(
    obs_scale, cell_scale, core_ref, own_ref, sibling_ref, gi_ref, go_ref, gp_ref, gd_ref
):
    width = gi_ref.shape[1]
    chips = own_ref.shape[0]
    count = width // (2 * LANES)
    per = chips // count
    core = core_ref[0]
    for ref, half in ((own_ref, core), (sibling_ref, 1 - core)):
        for n in range(count):
            cols = pl.ds(pl.multiple_of((half * count + n) * LANES, LANES), LANES)
            block = ref[n * per : (n + 1) * per].astype(f32)
            block = block.reshape(per * block.shape[1], LANES)
            start = 0
            for out_ref, scale in (
                (go_ref, obs_scale), (gi_ref, obs_scale), (gp_ref, cell_scale), (gd_ref, cell_scale)
            ):
                size = out_ref.shape[0]
                out_ref[:, cols] = block[start : start + size] * scale
                start += round_up(size, 16)


def unpack(core, own, sibling, spec, width, obs_scale, cell_scale):
    return pl.pallas_call(
        functools.partial(unpack_kernel, obs_scale, cell_scale),
        out_shape=tuple(
            jax.ShapeDtypeStruct((rows, width), f32) for rows in (spec, width, width, 9)
        ),
        in_specs=[smem()] + [vmem()] * 2,
        out_specs=(vmem(),) * 4,
        compiler_params=params(8),
        cost_estimate=cost(3),
        name="unpack",
    )(core, own, sibling)


def neighbours(axes, periodic):
    count = lax.axis_size(axes)
    up = [(i, i + 1) for i in range(count - 1)]
    if periodic:
        up.append((count - 1, 0))
    return up, [(t, s) for s, t in up]


LAT = ("x", "core")
CHIPS = ("x", "lon")


def spread(values):
    chips = lax.axis_size(CHIPS)
    values = values.reshape(chips, values.size // (chips * LANES), LANES)
    return lax.all_to_all(values, CHIPS, split_axis=0, concat_axis=0, tiled=True)


def on_device(spectra, owner, cell, w_in, w_out, w_point, w_depth, cotangent):
    tiles = lax.axis_size(LAT) * lax.axis_size("lon")
    rows_here, spec = spectra.shape
    cap = max(2, 2 * rows_here // tiles)
    clat, clon, width = cotangent.shape
    cells = clat * clon
    wide = clon + 16
    spec_wide = round_up(spec + 2, LANES)
    core = lax.axis_index("core").reshape(1)
    east_way, west_way = neighbours("lon", True)
    south_way, north_way = neighbours(LAT, False)

    from_west = lax.ppermute(cotangent[:, -1], "lon", east_way)
    from_east = lax.ppermute(cotangent[:, 0], "lon", west_way)

    outgoing = route(
        owner.reshape(1, rows_here), cell.reshape(1, rows_here), spectra.T,
        tiles, lax.axis_size("lon"), cap, clon, spec_wide,
    )
    outgoing, from_west, from_east, w_in, w_out = lax.optimization_barrier(
        (outgoing, from_west, from_east, w_in, w_out)
    )
    arrived = lax.all_to_all(
        outgoing.reshape(tiles, cap, spec_wide), ("lon", "x", "core"), 0, 0, tiled=True
    ).reshape(tiles * cap, spec_wide)

    fill = jnp.zeros((wide - clon - 2, width), bf16)

    def halo_row(i):
        return jnp.concatenate([cotangent[i], from_east[i, None], fill, from_west[i, None]], axis=0)

    from_north = lax.ppermute(halo_row(clat - 1), LAT, south_way)
    from_south = lax.ppermute(halo_row(0), LAT, north_way)
    cot_t, g_mixed, g_grid = grid_grad(
        cotangent.reshape(cells, width),
        (from_east, from_west, from_north, from_south),
        w_point, w_depth, clat, clon, wide,
    )
    w_in_t = jnp.pad(w_in.T, ((0, 0), (0, spec_wide - spec)))

    out_rows = round_up(2 * width + round_up(spec, 16) + 16, 16 * tiles * LANES // width)
    operands = w_in_t, w_out.T, g_grid, w_out, g_mixed, cot_t
    mine, other, east, west, grid, mix_ext = owner_part(
        core, arrived, w_depth, operands, spec, clat, clon, wide, out_rows
    )
    summed = core_sum(mine, other)
    summed, east, west, mix_ext = lax.optimization_barrier((summed, east, west, mix_ext))
    parts = spread(summed)

    left = lax.ppermute(east, "lon", east_way)
    right = lax.ppermute(west, "lon", west_way)
    sent = totals(parts, left, right)
    full = spread(sent)
    line = lax.broadcasted_iota(i32, (clon, width), 0)

    def edge_row(e):
        row = mix_ext[e * wide : e * wide + clon].astype(f32)
        sides = jnp.where(line == 0, left[e], jnp.where(line == clon - 1, right[e], 0.0))
        return (row + sides).astype(bf16)

    top = lax.ppermute(edge_row(clat + 1), LAT, south_way)
    bottom = lax.ppermute(edge_row(0), LAT, north_way)
    latent = finish_latent(grid, mix_ext, (top, bottom, left, right), w_point, clat, clon, wide)

    obs_scale = float((rows_here * tiles) ** -0.5)
    cell_scale = float((cells * tiles) ** -0.5)
    full, latent = lax.optimization_barrier((full, latent))
    sibling = lax.ppermute(full, "core", SWAP)
    grad_in, grad_out, grad_point, grad_depth = unpack(
        core, full, sibling, spec, width, obs_scale, cell_scale
    )
    return latent.reshape(clat, clon, width), grad_in, grad_out, grad_point, grad_depth


def solution(mesh):
    lat, lon = mesh.devices.shape
    fine = Mesh(mesh.devices.reshape(lat // 2, 2, lon), ("x", "core", "lon"))
    everyone = P(("x", "core", "lon"))
    field = P(LAT, "lon", None)
    in_specs = (everyone, everyone, everyone, P(), P(), P(), P(), field)
    out_specs = (field, P(), P(), P(), P())
    return jax.shard_map(
        on_device, mesh=fine, in_specs=in_specs, out_specs=out_specs, check_vma=False
    )
```
